32 devices in a mesh: ctx: 16 (over z, x, core), wt: 2 (over y).
Axes of the slice: x: 2, y: 2, z: 4, core: 2. Of those that a mesh axis runs over, the one named last changes fastest.
Arguments:
- tokens: bfloat16 [2, 4096, 1280], P('wt', 'ctx'), may hold values from -6 to 6
- cotangent: bfloat16 [2, 4096, 1280], P('wt', 'ctx'), may hold values from -6 to 6
- deal: int32 [2, 32], P('wt'), may hold values from 0 to 31, as said below
- lengths: int32 [2, 1], P('wt'), may hold values from 2048 to 4096, as said below
- gain_attn: bfloat16 [1280], P('wt'), may hold values from 0.5 to 1.5
- w_query: bfloat16 [1280, 1280], P('wt'), may hold values from -0.15625 to 0.15625
- w_key: bfloat16 [1280, 1280], P('wt'), may hold values from -0.15625 to 0.15625
- w_value: bfloat16 [1280, 1280], P('wt'), may hold values from -0.15625 to 0.15625
- w_output: bfloat16 [1280, 1280], P('wt'), may hold values from -4 to 4
- query_scale: float32 [80], replicated, may hold values from -1 to 1
- gain_mlp: bfloat16 [1280], P('wt'), may hold values from 0.5 to 1.5
- w_expand: bfloat16 [1280, 1280], P('wt'), may hold values from -0.15625 to 0.15625
- w_contract: bfloat16 [1280, 1280], P('wt'), may hold values from -0.15625 to 0.15625
Outputs:
- result: bfloat16 [2, 4096, 1280], P('wt', 'ctx')
- grad_inputs: bfloat16 [2, 4096, 1280], P('wt', 'ctx')
- grad_gain_attn: float32 [1280], P('wt')
- grad_query: float32 [1280, 1280], P('wt')
- grad_key: float32 [1280, 1280], P('wt')
- grad_value: float32 [1280, 1280], P('wt')
- grad_output: float32 [1280, 1280], P('wt')
- grad_scale: float32 [80], replicated
- grad_gain_mlp: float32 [1280], P('wt')
- grad_expand: float32 [1280, 1280], P('wt')
- grad_contract: float32 [1280, 1280], P('wt')
The draws below stay inside these ranges and needn't reach their ends.
Inputs may be any that keep to these rules, and one draw needn't show every extreme that they name: `deal`: each group's row is a permutation of the span numbers 0 to 31; in each group one sequence, of length 4096, has its first span dealt to row 0 and its last span to row 31. `lengths`: in each group one sequence has length 4096.
All inputs are finite; a program needn't handle non-finite values.
Results may differ from the reference program's by a relative error of at most 0.023.
Values may be sent and summed in bfloat16 or wider, within the bound.
No kernel may reach another device: no remote copies, remote signals or barrier semaphores. Data moves between devices by JAX's collectives and lax.ppermute only.
A program may use at most 512 MiB of HBM per device.

```python
import math
from functools import partial
import jax
import jax.numpy as jnp
from jax import lax

D = 1280
HEADS = 16
HEAD = 80
FF = 1280
SPAN = 128
GROUP_TOK = 4096
GROUPS = 2
SLOT = 4096
SEQS = 1
NCHUNK = 32


def pick_longest(key):
    return jax.random.randint(key, (GROUPS,), 0, SEQS)


def draw_lengths(key, part):
    longest = pick_longest(key)
    key = jax.random.fold_in(key, 11)
    drawn = jax.random.randint(key, (GROUPS, SEQS), SLOT // 2, SLOT + 1)
    chosen = jnp.arange(SEQS)[None, :] == longest[:, None]
    return jnp.where(chosen, SLOT, drawn).astype(jnp.int32)


def draw_deal(key, part):
    longest = pick_longest(key)
    key = jax.random.fold_in(key, 23)
    subkeys = jax.random.split(key, GROUPS)
    per_seq = SLOT // SPAN

    def one_group(subkey, sequence):
        order = jax.random.permutation(subkey, NCHUNK).astype(jnp.int32)
        first_span = (sequence * per_seq).astype(jnp.int32)
        last_span = first_span + per_seq - 1
        where_first = jnp.argmax(order == first_span)
        order = order.at[where_first].set(order[0])
        order = order.at[0].set(first_span)
        where_last = jnp.argmax(order == last_span)
        order = order.at[where_last].set(order[NCHUNK - 1])
        order = order.at[NCHUNK - 1].set(last_span)
        return order
    return jax.vmap(one_group)(subkeys, longest).astype(jnp.int32)


def block_levels(key, extent, shards, smallest, top_value):
    factor_of, own = 1.0, jax.random.fold_in(key, 6)
    for axis_at, blocks in shards:
        heights = jnp.exp(jax.random.uniform(jax.random.fold_in(own, axis_at), (blocks,), jnp.float32, smallest / len(shards), top_value / len(shards)))
        factor_of = factor_of * jnp.repeat(heights, extent[axis_at] // blocks).reshape([-1 if axis == axis_at else 1 for axis in range(len(extent))])
    return factor_of


def noise(rng, dims, deviation, most, pieces=(), kind=jnp.bfloat16):
    entries = jax.random.normal(rng, dims, jnp.float32) * deviation
    if len(pieces) > 0:
        entries = block_levels(rng, dims, pieces, -0.22, 0.18) * entries
    return jnp.clip(entries, min=-most, max=most).astype(kind)


def setup_inputs(seed: int = 0) -> dict:
    seeds = jax.random.split(jax.random.key(seed), 14)
    tokens = noise(seeds[0], (GROUPS, GROUP_TOK, D), 1.0, 6.0, ((0, 2), (1, 16)))
    cotangent = noise(seeds[1], (GROUPS, GROUP_TOK, D), 1.0, 6.0, ((0, 2), (1, 16)))
    deal = draw_deal(jax.random.fold_in(seeds[13], 71), 0)
    lengths = draw_lengths(jax.random.fold_in(seeds[13], 71), 0)
    gain_attn = jnp.clip(1.0 + 0.1 * jax.random.normal(seeds[4], (D,), jnp.float32), 0.5, 1.5).astype(jnp.bfloat16)
    w_query = noise(seeds[5], (D, D), D ** -0.5, 0.15625, ((0, 2),))
    w_key = noise(seeds[6], (D, D), D ** -0.5, 0.15625, ((0, 2),))
    w_value = noise(seeds[7], (D, D), D ** -0.5, 0.15625, ((0, 2),))
    w_output = noise(seeds[8], (D, D), (D * 8 // SLOT) ** -0.5, 4.0, ((0, 2),))
    query_scale = jnp.clip(jax.random.uniform(seeds[9], (HEAD,), jnp.float32, -1.0, 1.0), -1.0, 1.0)
    gain_mlp = jnp.clip(1.0 + 0.1 * jax.random.normal(seeds[10], (D,), jnp.float32), 0.5, 1.5).astype(jnp.bfloat16)
    w_expand = noise(seeds[11], (D, FF), D ** -0.5, 0.15625, ((0, 2),))
    w_contract = noise(seeds[12], (FF, D), FF ** -0.5, 0.15625, ((0, 2),))
    return dict(tokens=tokens, cotangent=cotangent, deal=deal, lengths=lengths, gain_attn=gain_attn, w_query=w_query, w_key=w_key, w_value=w_value, w_output=w_output, query_scale=query_scale, gain_mlp=gain_mlp, w_expand=w_expand, w_contract=w_contract)


EPS = 1e-06
LOG2E = 1.442695041
NEG = -1e+30
HIGH = lax.Precision.HIGHEST

@jax.custom_vjp
def low(v):
    return lax.optimization_barrier(v.astype(jnp.bfloat16)).astype(jnp.float32)

@jax.custom_vjp
def low_back(v):
    return v

def low_keep(v):
    return (low(v), None)

def low_pass(kept, grad):
    return (grad,)

def back_keep(v):
    return (v, None)

def back_low(kept, grad):
    return (low(grad),)
low.defvjp(low_keep, low_pass)
low_back.defvjp(back_keep, back_low)

def normed(values, gain):
    return values * lax.rsqrt(lax.optimization_barrier(jnp.mean(values * values, axis=-1, keepdims=True)) + EPS) * gain

def project(left, right):
    return jnp.dot(left, right, precision=HIGH)

def attend_sequence(queries, key_rows, value_rows, length):
    block_rows = min(512, SLOT)
    positions = jnp.arange(SLOT, dtype=jnp.int32)
    key_valid = positions < length

    def one_block(offset):
        query_block = lax.dynamic_slice_in_dim(queries, offset, block_rows, 0)
        query_pos = offset + jnp.arange(block_rows, dtype=jnp.int32)
        permit = (positions[None, :] <= query_pos[:, None]) & key_valid[None, :]
        scores = low_back(jnp.einsum('qhd,khd->hqk', query_block, key_rows, precision=HIGH))
        scores = jnp.where(permit[None], scores, NEG)
        row_peak = lax.optimization_barrier(jnp.max(scores, axis=-1, keepdims=True))
        weights = jnp.exp(scores - row_peak)
        probabilities = low(weights / lax.optimization_barrier(jnp.sum(weights, axis=-1, keepdims=True)))
        return jnp.einsum('hqk,khd->qhd', probabilities, value_rows, precision=HIGH)
    offsets = jnp.arange(SLOT // block_rows, dtype=jnp.int32) * block_rows
    return lax.map(jax.checkpoint(one_block), offsets).reshape(SLOT, HEADS, HEAD)

def attend_group(operands):
    queries, key_rows, value_rows, dealt_spans, seq_lengths = operands

    def natural(values):
        spanned = values.reshape(NCHUNK, SPAN, HEADS, HEAD)
        placed = jnp.zeros_like(spanned).at[dealt_spans].set(spanned)
        return placed.reshape(SEQS, SLOT, HEADS, HEAD)

    def one_sequence(parts):
        return attend_sequence(parts[0], parts[1], parts[2], parts[3])
    attended = lax.map(one_sequence, (natural(queries), natural(key_rows), natural(value_rows), seq_lengths))
    attended = attended.reshape(NCHUNK, SPAN, HEADS * HEAD)
    return jnp.take(attended, dealt_spans, axis=0).reshape(GROUP_TOK, HEADS * HEAD)

def forward(deal, lengths, inputs, gain_attn, w_query, w_key, w_value, w_output, query_scale, gain_mlp, w_expand, w_contract):
    attn_in = low(normed(inputs, gain_attn))
    scale_row = LOG2E / math.sqrt(HEAD) * jax.nn.softplus(query_scale)
    query_lin = low_back(project(attn_in, w_query))
    queries = low(query_lin.reshape(GROUPS, GROUP_TOK, HEADS, HEAD) * scale_row)
    key_rows = low(low_back(project(attn_in, w_key))).reshape(GROUPS, GROUP_TOK, HEADS, HEAD)
    value_rows = low(low_back(project(attn_in, w_value))).reshape(GROUPS, GROUP_TOK, HEADS, HEAD)
    attended = lax.map(attend_group, (queries, key_rows, value_rows, deal, lengths))
    attn_out = low(low_back(attended))
    mid = inputs + low_back(project(attn_out, w_output))
    mlp_in = low(normed(mid, gain_mlp))
    expanded = low_back(project(mlp_in, w_expand))
    activated = low(jax.nn.silu(expanded))
    return mid + low_back(project(activated, w_contract))

def reference(tokens, cotangent, deal, lengths, gain_attn, w_query, w_key, w_value, w_output, query_scale, gain_mlp, w_expand, w_contract):
    floats = tuple((value.astype(jnp.float32) for value in (tokens, gain_attn, w_query, w_key, w_value, w_output, query_scale, gain_mlp, w_expand, w_contract)))
    result, pullback = jax.vjp(partial(forward, deal, lengths), *floats)
    gradients = pullback(cotangent.astype(jnp.float32))
    return (result.astype(jnp.bfloat16), gradients[0].astype(jnp.bfloat16), gradients[1], gradients[2], gradients[3], gradients[4], gradients[5], gradients[6], gradients[7], gradients[8], gradients[9])
```

```python
import functools
import math

import jax
import jax.numpy as jnp
import numpy as np
from jax import lax
from jax.experimental import pallas as pl
from jax.experimental.pallas import tpu as pltpu
from jax.sharding import PartitionSpec as P

HEADS = 16
HEAD = 80
SPAN = 128
LONGEST = 4096


EPS = 1e-06
LOG2E = 1.442695041
NEG = -1e30


def normed(values, gain):
    return values * lax.rsqrt(jnp.mean(values * values, axis=-1, keepdims=True) + EPS) * gain


def locate(dealt_spans, seq_lengths, offset, count, slot_tokens):
    row_ids = offset + jnp.arange(count, dtype=jnp.int32)
    slot_ids = row_ids // SPAN
    matches = slot_ids[:, None] == jnp.arange(dealt_spans.shape[0], dtype=jnp.int32)[None, :]
    span_ids = jnp.sum(jnp.where(matches, dealt_spans[None, :], 0), axis=1)
    natural = span_ids * SPAN + row_ids % SPAN
    sequence = natural // slot_tokens
    position = natural % slot_tokens
    owners = sequence[:, None] == jnp.arange(seq_lengths.shape[0], dtype=jnp.int32)[None, :]
    limits = jnp.sum(jnp.where(owners, seq_lengths[None, :], 0), axis=1)
    return (sequence, position, position < limits)


def permitted(query_place, key_place):
    same_seq = query_place[0][:, None] == key_place[0][None, :]
    causal = key_place[1][None, :] <= query_place[1][:, None]
    return (same_seq & causal & key_place[2][None, :])[None]


def per_device(
    tokens,
    cotangent,
    deal,
    lengths,
    gain_attn,
    w_query,
    w_key,
    w_value,
    w_output,
    query_scale,
    gain_mlp,
    w_expand,
    w_contract,
):
    row_count = tokens.shape[1]
    feat_width = tokens.shape[2]
    group_rows = row_count * lax.axis_size("ctx")
    slot_tokens = min(LONGEST, group_rows)
    block_rows = min(512, group_rows)
    blocks = group_rows // block_rows
    dealt_spans = deal[0]
    seq_lengths = lengths[0]
    inputs = tokens[0].astype(jnp.float32)
    shards = (gain_attn, w_query, w_key, w_value, w_output, gain_mlp, w_expand, w_contract)
    gathered = (
        lax.all_gather(shards[0], "wt", axis=0, tiled=True),
        lax.all_gather(shards[1], "wt", axis=0, tiled=True),
        lax.all_gather(shards[2], "wt", axis=0, tiled=True),
        lax.all_gather(shards[3], "wt", axis=0, tiled=True),
        lax.all_gather(shards[4], "wt", axis=0, tiled=True),
        lax.all_gather(shards[5], "wt", axis=0, tiled=True),
        lax.all_gather(shards[6], "wt", axis=0, tiled=True),
        lax.all_gather(shards[7], "wt", axis=0, tiled=True),
    )
    gain_one = gathered[0].astype(jnp.float32)
    gain_two = gathered[5].astype(jnp.float32)
    query_place = locate(
        dealt_spans, seq_lengths, lax.axis_index("ctx") * row_count, row_count, slot_tokens
    )
    scale_row = LOG2E / math.sqrt(HEAD) * jax.nn.softplus(query_scale)
    attn_in = normed(inputs, gain_one).astype(jnp.bfloat16)
    query_lin = jnp.dot(attn_in, gathered[1], preferred_element_type=jnp.float32)
    queries = (query_lin.reshape(row_count, HEADS, HEAD) * scale_row).astype(jnp.bfloat16)
    key_own = jnp.dot(attn_in, gathered[2], preferred_element_type=jnp.float32).astype(jnp.bfloat16)
    value_own = jnp.dot(attn_in, gathered[3], preferred_element_type=jnp.float32).astype(
        jnp.bfloat16
    )
    portion = (
        lax.all_gather(key_own, "ctx", axis=0, tiled=True),
        lax.all_gather(value_own, "ctx", axis=0, tiled=True),
    )
    running = jnp.full((HEADS, row_count), NEG, jnp.float32)
    count = portion[0].shape[0]
    key_rows = portion[0].reshape(count, HEADS, HEAD)
    value_rows = portion[1].reshape(count, HEADS, HEAD)
    permit_mask = permitted(
        query_place, locate(dealt_spans, seq_lengths, jnp.int32(0), count, slot_tokens)
    )
    scores = jnp.einsum("qhd,khd->hqk", queries, key_rows, preferred_element_type=jnp.float32)
    scores = jnp.where(permit_mask, scores, NEG)
    newest = jnp.maximum(running, jnp.max(scores, axis=-1))
    weights = jnp.where(permit_mask, jnp.exp(scores - newest[..., None]), 0.0)
    running_total = jnp.sum(weights, axis=-1)
    update = jnp.einsum(
        "hqk,khd->qhd", weights.astype(jnp.bfloat16), value_rows, preferred_element_type=jnp.float32
    )
    summed = update
    running, running_total, summed = (newest, running_total, summed)
    log_norm = running + jnp.log(running_total)
    attended = summed / jnp.transpose(running_total)[:, :, None]
    attn_out = attended.reshape(row_count, feat_width).astype(jnp.bfloat16)
    mid = inputs + jnp.dot(attn_out, gathered[4], preferred_element_type=jnp.float32)
    mlp_in = normed(mid, gain_two).astype(jnp.bfloat16)
    expanded = jnp.dot(mlp_in, gathered[6], preferred_element_type=jnp.float32)
    activated = jax.nn.silu(expanded).astype(jnp.bfloat16)
    result = mid + jnp.dot(activated, gathered[7], preferred_element_type=jnp.float32)
    weights_back = (
        lax.all_gather(shards[0], "wt", axis=0, tiled=True),
        lax.all_gather(shards[1], "wt", axis=0, tiled=True),
        lax.all_gather(shards[2], "wt", axis=0, tiled=True),
        lax.all_gather(shards[3], "wt", axis=0, tiled=True),
        lax.all_gather(shards[4], "wt", axis=0, tiled=True),
        lax.all_gather(shards[5], "wt", axis=0, tiled=True),
        lax.all_gather(shards[6], "wt", axis=0, tiled=True),
        lax.all_gather(shards[7], "wt", axis=0, tiled=True),
    )
    whole_keys, whole_values = (
        lax.all_gather(key_own, "ctx", axis=0, tiled=True),
        lax.all_gather(value_own, "ctx", axis=0, tiled=True),
    )
    grad_result = cotangent[0].astype(jnp.float32)
    grad_branch = grad_result.astype(jnp.bfloat16)
    grad_contract = jnp.einsum(
        "tf,td->fd", activated, grad_branch, preferred_element_type=jnp.float32
    )
    grad_act = jnp.einsum(
        "td,fd->tf", grad_branch, weights_back[7], preferred_element_type=jnp.float32
    )
    sigmoid_gate = jax.nn.sigmoid(expanded)
    grad_expanded = (grad_act * sigmoid_gate * (1.0 + expanded * (1.0 - sigmoid_gate))).astype(
        jnp.bfloat16
    )
    grad_expand = jnp.einsum("td,tf->df", mlp_in, grad_expanded, preferred_element_type=jnp.float32)
    grad_mlp_in = jnp.einsum(
        "tf,df->td", grad_expanded, weights_back[6], preferred_element_type=jnp.float32
    )
    unused_two, pull_two = jax.vjp(normed, mid, gain_two)
    grad_mid_norm, grad_gain_two = pull_two(grad_mlp_in)
    grad_mid = grad_result + grad_mid_norm
    grad_mid_low = grad_mid.astype(jnp.bfloat16)
    grad_output_w = jnp.einsum(
        "td,te->de", attn_out, grad_mid_low, preferred_element_type=jnp.float32
    )
    grad_attended = jnp.einsum(
        "te,de->td", grad_mid_low, weights_back[4], preferred_element_type=jnp.float32
    ).astype(jnp.bfloat16)
    out_grad = grad_attended.reshape(row_count, HEADS, HEAD)
    delta = jnp.transpose(jnp.sum(out_grad.astype(jnp.float32) * attended, axis=-1))
    key_blocks = (
        jnp.arange(blocks, dtype=jnp.int32),
        whole_keys.reshape(blocks, block_rows, feat_width),
        whole_values.reshape(blocks, block_rows, feat_width),
    )
    query_zero = jnp.zeros((row_count, HEADS, HEAD), jnp.float32)

    def back_block(query_grad, block_in):
        offset = block_in[0] * block_rows
        key_rows = block_in[1].reshape(block_rows, HEADS, HEAD)
        value_rows = block_in[2].reshape(block_rows, HEADS, HEAD)
        permit_mask = permitted(
            query_place, locate(dealt_spans, seq_lengths, offset, block_rows, slot_tokens)
        )
        scores = jnp.einsum("qhd,khd->hqk", queries, key_rows, preferred_element_type=jnp.float32)
        probabilities = jnp.where(permit_mask, jnp.exp(scores - log_norm[..., None]), 0.0)
        value_grad = jnp.einsum(
            "hqk,qhd->khd",
            probabilities.astype(jnp.bfloat16),
            out_grad,
            preferred_element_type=jnp.float32,
        )
        prob_grad = jnp.einsum(
            "qhd,khd->hqk", out_grad, value_rows, preferred_element_type=jnp.float32
        )
        score_grad = (probabilities * (prob_grad - delta[..., None])).astype(jnp.bfloat16)
        query_grad = query_grad + jnp.einsum(
            "hqk,khd->qhd", score_grad, key_rows, preferred_element_type=jnp.float32
        )
        key_grad = jnp.einsum(
            "hqk,qhd->khd", score_grad, queries, preferred_element_type=jnp.float32
        )
        return (
            query_grad,
            (key_grad.reshape(block_rows, feat_width), value_grad.reshape(block_rows, feat_width)),
        )

    query_grad, key_terms = lax.scan(back_block, query_zero, key_blocks)
    key_sum, value_sum = (
        lax.psum_scatter(
            key_terms[0].reshape(group_rows, feat_width).astype(jnp.bfloat16),
            "ctx",
            scatter_dimension=0,
            tiled=True,
        ).astype(jnp.float32),
        lax.psum_scatter(
            key_terms[1].reshape(group_rows, feat_width).astype(jnp.bfloat16),
            "ctx",
            scatter_dimension=0,
            tiled=True,
        ).astype(jnp.float32),
    )
    grad_keys = key_sum.astype(jnp.bfloat16)
    grad_values = value_sum.astype(jnp.bfloat16)
    grad_query_lin = (query_grad * scale_row).reshape(row_count, feat_width).astype(jnp.bfloat16)
    grad_scale = (
        jnp.sum(query_grad * query_lin.reshape(row_count, HEADS, HEAD), axis=(0, 1))
        * (LOG2E / math.sqrt(HEAD))
        * jax.nn.sigmoid(query_scale)
    )
    grad_query_w = jnp.einsum(
        "td,te->de", attn_in, grad_query_lin, preferred_element_type=jnp.float32
    )
    grad_key_w = jnp.einsum("td,te->de", attn_in, grad_keys, preferred_element_type=jnp.float32)
    grad_value_w = jnp.einsum("td,te->de", attn_in, grad_values, preferred_element_type=jnp.float32)
    grad_attn_in = jnp.einsum(
        "te,de->td", grad_query_lin, weights_back[1], preferred_element_type=jnp.float32
    )
    grad_attn_in = grad_attn_in + jnp.einsum(
        "te,de->td", grad_keys, weights_back[2], preferred_element_type=jnp.float32
    )
    grad_attn_in = grad_attn_in + jnp.einsum(
        "te,de->td", grad_values, weights_back[3], preferred_element_type=jnp.float32
    )
    unused_one, pull_one = jax.vjp(normed, inputs, gain_one)
    grad_in_norm, grad_gain_one = pull_one(grad_attn_in)
    grad_inputs = (grad_mid + grad_in_norm).astype(jnp.bfloat16)
    terms = (
        grad_gain_one,
        grad_query_w,
        grad_key_w,
        grad_value_w,
        grad_output_w,
        jnp.tile(grad_scale, lax.axis_size("wt")),
        grad_gain_two,
        grad_expand,
        grad_contract,
    )
    shares = (
        lax.psum_scatter(
            terms[0].astype(jnp.bfloat16), "wt", scatter_dimension=0, tiled=True
        ).astype(jnp.float32),
        lax.psum_scatter(
            terms[1].astype(jnp.bfloat16), "wt", scatter_dimension=0, tiled=True
        ).astype(jnp.float32),
        lax.psum_scatter(
            terms[2].astype(jnp.bfloat16), "wt", scatter_dimension=0, tiled=True
        ).astype(jnp.float32),
        lax.psum_scatter(
            terms[3].astype(jnp.bfloat16), "wt", scatter_dimension=0, tiled=True
        ).astype(jnp.float32),
        lax.psum_scatter(
            terms[4].astype(jnp.bfloat16), "wt", scatter_dimension=0, tiled=True
        ).astype(jnp.float32),
        lax.psum_scatter(
            terms[5].astype(jnp.bfloat16), "wt", scatter_dimension=0, tiled=True
        ).astype(jnp.float32),
        lax.psum_scatter(
            terms[6].astype(jnp.bfloat16), "wt", scatter_dimension=0, tiled=True
        ).astype(jnp.float32),
        lax.psum_scatter(
            terms[7].astype(jnp.bfloat16), "wt", scatter_dimension=0, tiled=True
        ).astype(jnp.float32),
        lax.psum_scatter(
            terms[8].astype(jnp.bfloat16), "wt", scatter_dimension=0, tiled=True
        ).astype(jnp.float32),
    )
    totals = (
        lax.psum(shares[0].astype(jnp.bfloat16), "ctx").astype(jnp.float32),
        lax.psum(shares[1].astype(jnp.bfloat16), "ctx").astype(jnp.float32),
        lax.psum(shares[2].astype(jnp.bfloat16), "ctx").astype(jnp.float32),
        lax.psum(shares[3].astype(jnp.bfloat16), "ctx").astype(jnp.float32),
        lax.psum(shares[4].astype(jnp.bfloat16), "ctx").astype(jnp.float32),
        lax.psum(shares[5].astype(jnp.bfloat16), "ctx").astype(jnp.float32),
        lax.psum(shares[6].astype(jnp.bfloat16), "ctx").astype(jnp.float32),
        lax.psum(shares[7].astype(jnp.bfloat16), "ctx").astype(jnp.float32),
        lax.psum(shares[8].astype(jnp.bfloat16), "ctx").astype(jnp.float32),
    )
    return (
        result.astype(jnp.bfloat16)[None],
        grad_inputs[None],
        totals[0],
        totals[1],
        totals[2],
        totals[3],
        totals[4],
        totals[5],
        totals[6],
        totals[7],
        totals[8],
    )


BF = jnp.bfloat16
F32 = jnp.float32
NN = (((1,), (0,)), ((), ()))
NT = (((1,), (1,)), ((), ()))
AXES = ("ctx", "wt")
LIMIT = 56 * 1024 * 1024

RING = ((0, 0), (1, 0), (2, 0), (3, 0), (3, 1), (2, 1), (1, 1), (0, 1))
PLACE = {chip: at for at, chip in enumerate(RING)}
OFFSETS = (0, -1, 1, -2, 2, -3, 3, 4)


def flat(z, x, core, y):
    return ((z * 2 + x) * 2 + core) * 2 + y


def pairs(move):
    return [
        (flat(z, x, core, y), flat(*move(z, x, core, y)))
        for z in range(4)
        for x in range(2)
        for core in range(2)
        for y in range(2)
    ]


def turned(by):
    def move(z, x, core, y):
        return (*RING[(PLACE[(z, x)] + by) % 8], core, y)

    return move


CORE_SWAP = pairs(lambda z, x, core, y: (z, x, 1 - core, y))
Y_SWAP = pairs(lambda z, x, core, y: (z, x, core, 1 - y))
X_SWAP = pairs(lambda z, x, core, y: (z, 1 - x, core, y))
NEAR_SWAP = pairs(lambda z, x, core, y: (z ^ 1, x, core, y))
FAR_SWAP = pairs(lambda z, x, core, y: (z ^ 2, x, core, y))
FORTH = pairs(turned(1))
BACK = pairs(turned(-1))


def slot_table():
    rows = []
    for c in range(16):
        z, x, core = c // 4, (c // 2) % 2, c % 2
        chips = [RING[(PLACE[(z, x)] + by) % 8] for by in OFFSETS]
        own = [(a * 2 + b) * 2 + core for a, b in chips]
        rows.append(own + [dev ^ 1 for dev in own])
    return np.asarray(rows, np.int32)


def send(value, moves):
    return lax.ppermute(value, AXES, moves)


def mm(left, right, dims=NN):
    return lax.dot_general(left, right, dims, preferred_element_type=F32)


def call(body, outs, args, smem=0, anys=0, scratch=(), cost=None, out_any=False):
    whole = pl.BlockSpec(memory_space=pltpu.VMEM)
    specs = [pl.BlockSpec(memory_space=pltpu.SMEM)] * smem
    specs += [whole] * (len(args) - smem - anys)
    specs += [pl.BlockSpec(memory_space=pl.ANY)] * anys
    out_spec = pl.BlockSpec(memory_space=pl.ANY) if out_any else whole
    estimate = None
    if cost is not None:
        estimate = pl.CostEstimate(flops=int(cost[0]), bytes_accessed=int(cost[1]), transcendentals=int(cost[2]))
    return pl.pallas_call(
        body,
        out_shape=[jax.ShapeDtypeStruct(shape, kind) for shape, kind in outs],
        in_specs=specs,
        out_specs=[out_spec] * len(outs),
        scratch_shapes=list(scratch),
        cost_estimate=estimate,
        compiler_params=pltpu.CompilerParams(vmem_limit_bytes=LIMIT),
    )(*args)


def half(y, width=640):
    return pl.ds(pl.multiple_of(y * width, 128), width)


def pick_kernel(info, wq, wk, wv, gain_a, gain_m, out):
    chip = info[2]
    cols = lax.broadcasted_iota(jnp.int32, (2 * HEAD, wq.shape[1]), 1)
    rows = lax.broadcasted_iota(jnp.int32, (2 * HEAD, wq.shape[1]), 0)
    chosen = jnp.where(cols == rows + chip * (2 * HEAD), 1.0, 0.0).astype(BF)
    for at, ref in enumerate((wq, wk, wv)):
        both = mm(chosen, ref[...], NT).astype(BF)
        out[at * HEAD : (at + 1) * HEAD] = both[:HEAD]
        out[3 * HEAD + at * HEAD : 3 * HEAD + (at + 1) * HEAD] = both[HEAD:]
    line = lax.broadcasted_iota(jnp.int32, (16, gain_a.shape[1]), 0)
    tail = jnp.where(line == 0, gain_a[...].astype(F32), 0.0)
    tail = jnp.where(line == 1, gain_m[...].astype(F32), tail)
    out[6 * HEAD :] = tail.astype(BF)


def project_kernel(count, info, *refs):
    xs = refs[:count]
    own, other, scale, attn_in, mine, partner, weight, gain, lines = refs[count:]
    y, core = info[0], info[1]
    weight[:, half(y)] = own[: 6 * HEAD]
    weight[:, half(1 - y)] = other[: 6 * HEAD]
    gain[:, half(y)] = own[6 * HEAD :].astype(F32)
    gain[:, half(1 - y)] = other[6 * HEAD :].astype(F32)
    row = 0
    for ref in xs:
        values = ref[...].astype(F32)
        scaled = values * lax.rsqrt(jnp.mean(values * values, axis=-1, keepdims=True) + EPS)
        attn_in[row : row + ref.shape[0]] = (scaled * gain[0:1]).astype(BF)
        row += ref.shape[0]
    lin = mm(weight[...], attn_in[...], NT)
    for head in range(2):
        base = head * 3 * HEAD
        lines[base : base + HEAD] = (lin[base : base + HEAD] * scale[...]).astype(BF)
        lines[base + HEAD : base + 3 * HEAD] = lin[base + HEAD : base + 3 * HEAD].astype(BF)
    mine[...] = lines[pl.ds(pl.multiple_of(core * 3 * HEAD, 16), 3 * HEAD)]
    partner[...] = lines[pl.ds(pl.multiple_of((1 - core) * 3 * HEAD, 16), 3 * HEAD)]


def span_slots(pieces):
    return [(ref, col) for ref in pieces for col in range(0, ref.shape[1], SPAN)]


def natural_span(info, deal, slot):
    return deal[2 * info[4 + slot // 2] + slot % 2]


def at_span(span):
    return pl.ds(pl.multiple_of(span * SPAN, SPAN), SPAN)


BLOCK = 512


def forward_kernel(info, deal, *refs):
    pieces = refs[:10]
    out, lse, queries, keys, values, dealt = refs[10:]
    total = queries.shape[1]
    length = info[3]
    spans = total // SPAN

    @pl.loop(0, spans)
    def _(at):
        dealt[deal[at]] = at

    line = lax.broadcasted_iota(jnp.int32, (16, total), 0)
    values[HEAD:] = jnp.where(line == 0, 1.0, 0.0).astype(BF)
    for slot, (ref, col) in enumerate(span_slots(pieces)):
        where = at_span(natural_span(info, deal, slot))
        queries[:, where] = ref[:HEAD, col : col + SPAN]
        keys[where, :] = ref[HEAD : 2 * HEAD, col : col + SPAN].T
        values[:HEAD, where] = ref[2 * HEAD :, col : col + SPAN]

    key_at = lax.broadcasted_iota(jnp.int32, (BLOCK, BLOCK), 0)
    query_at = lax.broadcasted_iota(jnp.int32, (BLOCK, BLOCK), 1)

    @pl.loop(0, total // BLOCK)
    def _(i):
        here = pl.ds(pl.multiple_of(i * BLOCK, BLOCK), BLOCK)
        query = queries[:, here]

        def step(masked, j, carry):
            peak, acc = carry
            there = pl.ds(pl.multiple_of(j * BLOCK, BLOCK), BLOCK)
            scores = mm(keys[there, :], query)
            if masked:
                key_pos = j * BLOCK + key_at
                allowed = (key_pos <= i * BLOCK + query_at) & (key_pos < length)
                scores = jnp.where(allowed, scores, NEG)
            newest = jnp.maximum(peak, jnp.max(scores, axis=0, keepdims=True))
            weights = jnp.exp(scores - newest)
            acc = acc * jnp.exp(peak - newest) + mm(values[:, there], weights.astype(BF))
            return newest, acc

        carry = (jnp.full((1, BLOCK), NEG, F32), jnp.zeros((HEAD + 16, BLOCK), F32))
        split = jnp.minimum(i, length // BLOCK)
        carry = lax.fori_loop(0, split, functools.partial(step, False), carry)
        peak, acc = lax.fori_loop(split, i + 1, functools.partial(step, True), carry)
        norm = acc[HEAD : HEAD + 1]
        lse[:, here] = peak + jnp.log(norm)
        attended = (acc[:HEAD] / norm).astype(BF)
        for part in range(BLOCK // SPAN):
            row = dealt[i * (BLOCK // SPAN) + part]
            out[row // 2, :, at_span(row % 2)] = attended[:, part * SPAN : (part + 1) * SPAN]


def backward_kernel(info, deal, *refs):
    pieces = refs[:10]
    lse, attended, grad_out, scale, out = refs[10:15]
    q_n, k_n, v_n, g_n, q_t, k_t, g_t, delta, dq_t, dk, dv, dealt = refs[15:]
    total = q_t.shape[1]
    length = info[3]
    spans = total // SPAN
    blocks = total // BLOCK

    @pl.loop(0, spans)
    def _(at):
        dealt[deal[at]] = at

    for slot, (ref, col) in enumerate(span_slots(pieces)):
        where = at_span(natural_span(info, deal, slot))
        cols = slice(col, col + SPAN)
        q_t[:, where] = ref[:HEAD, cols]
        k_t[:, where] = ref[HEAD : 2 * HEAD, cols]
        q_n[where, :] = ref[:HEAD, cols].T
        k_n[where, :] = ref[HEAD : 2 * HEAD, cols].T
        v_n[where, :] = ref[2 * HEAD :, cols].T
    for row in range(spans):
        where = at_span(deal[row])
        cols = slice(row % 2 * SPAN, row % 2 * SPAN + SPAN)
        grad = grad_out[row // 2, :, cols]
        g_t[:, where] = grad
        g_n[where, :] = grad.T
        product = grad.astype(F32) * attended[row // 2, :, cols].astype(F32)
        delta[:, where] = jnp.sum(product, axis=0, keepdims=True)
    dq_t[...] = jnp.zeros_like(dq_t)

    key_at = lax.broadcasted_iota(jnp.int32, (BLOCK, BLOCK), 0)
    query_at = lax.broadcasted_iota(jnp.int32, (BLOCK, BLOCK), 1)

    @pl.loop(0, blocks)
    def _(j):
        there = pl.ds(pl.multiple_of(j * BLOCK, BLOCK), BLOCK)
        dk[...] = jnp.zeros_like(dk)
        dv[...] = jnp.zeros_like(dv)

        def step(masked, i, carry):
            here = pl.ds(pl.multiple_of(i * BLOCK, BLOCK), BLOCK)
            scores = mm(k_n[there, :], q_t[:, here])
            probs = jnp.exp(scores - lse[:, here])
            if masked:
                key_pos = j * BLOCK + key_at
                allowed = (key_pos <= i * BLOCK + query_at) & (key_pos < length)
                probs = jnp.where(allowed, probs, 0.0)
            grad_probs = mm(v_n[there, :], g_t[:, here])
            grad_scores = (probs * (grad_probs - delta[:, here])).astype(BF)
            dv[...] += mm(probs.astype(BF), g_n[here, :])
            dk[...] += mm(grad_scores, q_n[here, :])
            dq_t[:, here] += mm(k_t[:, there], grad_scores)
            return carry

        split = jnp.where((j + 1) * BLOCK <= length, j + 1, blocks)
        lax.fori_loop(j, split, functools.partial(step, True), 0)
        lax.fori_loop(split, blocks, functools.partial(step, False), 0)
        for part in range(BLOCK // SPAN):
            row = dealt[j * (BLOCK // SPAN) + part]
            rows = slice(part * SPAN, (part + 1) * SPAN)
            out[row // 2, HEAD : 2 * HEAD, at_span(row % 2)] = dk[rows].T.astype(BF)
            out[row // 2, 2 * HEAD :, at_span(row % 2)] = dv[rows].T.astype(BF)

    for row in range(spans):
        cols = slice(row % 2 * SPAN, row % 2 * SPAN + SPAN)
        out[row // 2, :HEAD, cols] = (dq_t[:, at_span(deal[row])] * scale[...]).astype(BF)


def load_weights(info, parts, wholes, sems):
    y, core = info[0], info[1]
    started = []
    for at, whole in enumerate(wholes):
        own, direct, passed = parts[3 * at : 3 * at + 3]
        rows, part = own.shape[0], direct.shape[0]
        far = (1 - y) * rows
        places = ((own, y * rows), (direct, far + core * part), (passed, far + (1 - core) * part))
        copies = []
        for piece, (ref, start) in enumerate(places):
            target = whole.at[pl.ds(pl.multiple_of(start, 64), ref.shape[0])]
            copies.append(pltpu.make_async_copy(ref, target, sems.at[3 * at + piece]))
            copies[-1].start()
        started.append(copies)
    return started


def arrive(copies):
    for copy in copies:
        copy.wait()


def mlp_kernel(info, tokens, cotangent, attn_t, own, other, *refs):
    parts, outs = refs[:9], refs[9:16]
    w_output, w_expand, w_contract, gain, sems = refs[16:]
    result, grad_mid_out, grad_attended_t, act_out, mlp_in_out, grad_expanded_out, grad_mid_low_out = outs
    y = info[0]
    loads = load_weights(info, parts, (w_output, w_expand, w_contract), sems)
    gain[:, half(y)] = own[6 * HEAD :].astype(F32)
    gain[:, half(1 - y)] = other[6 * HEAD :].astype(F32)
    gains = gain[1:2]
    attn = attn_t[...].T
    arrive(loads[0])
    mid = tokens[...].astype(F32) + mm(attn, w_output[...])
    rate = lax.rsqrt(jnp.mean(mid * mid, axis=-1, keepdims=True) + EPS)
    mlp_in = (mid * rate * gains).astype(BF)
    mlp_in_out[...] = mlp_in
    arrive(loads[1])
    expanded = mm(mlp_in, w_expand[...])
    gate = jax.nn.sigmoid(expanded)
    act = (expanded * gate).astype(BF)
    act_out[...] = act
    arrive(loads[2])
    result[...] = (mid + mm(act, w_contract[...])).astype(BF)
    grad_act = mm(cotangent[...], w_contract[...], NT)
    grad_expanded = (grad_act * gate * (1.0 + expanded * (1.0 - gate))).astype(BF)
    grad_expanded_out[...] = grad_expanded
    grad_mlp_in = mm(grad_expanded, w_expand[...], NT) * gains
    inner = jnp.mean(grad_mlp_in * mid, axis=-1, keepdims=True)
    grad_mid = cotangent[...].astype(F32) + rate * grad_mlp_in - mid * (rate * rate * rate * inner)
    grad_mid_out[...] = grad_mid
    low = grad_mid.astype(BF)
    grad_mid_low_out[...] = low
    grad_attended_t[...] = mm(w_output[...], low, NT).astype(BF)


def outer_kernel(info, act, cotangent, mlp_in, grad_expanded, attn_t, grad_mid_low, *outs):
    core = info[1]
    lefts = (act[...].T, mlp_in[...].T, attn_t[...])
    for at, right in enumerate((cotangent, grad_expanded, grad_mid_low)):
        outs[2 * at][...] = mm(lefts[at], right[:, half(core)]).astype(BF)
        outs[2 * at + 1][...] = mm(lefts[at], right[:, half(1 - core)]).astype(BF)


def row_sums(products):
    ones = jnp.ones((16, products.shape[1]), BF)
    high = products.astype(BF)
    low = (products - high.astype(F32)).astype(BF)
    return mm(ones, high, NT) + mm(ones, low, NT)


def piece_rows(refs):
    slots = []
    for colour in range(2):
        group = refs[9 * colour : 9 * colour + 9]
        slots += [[(ref, 0)] for ref in group[:7]]
        slots.append([(group[7], 0), (group[8], group[7].shape[0])])
    return slots


def spread_kernel(info, *refs):
    pieces, (w_expand, gain) = refs[:18], refs[18:20]
    outs, grad_gain, stage = refs[20:23], refs[23], refs[24]
    for slot, parts in enumerate(piece_rows(pieces)):
        dev = info[4 + slot]
        block = ((dev // 2) % 2) * 4 + dev // 4
        for ref, row in parts:
            stage[slot, row : row + ref.shape[0]] = ref[...]
        rows = pl.ds(pl.multiple_of(block * 80, 16), 80)
        for at in range(3):
            outs[at][rows, half(dev % 2)] = stage[slot, at * 80 : at * 80 + 80].astype(F32)
    grad_gain[...] = row_sums(w_expand[...].astype(F32) * outs[1][...])[0:1] / gain[...].astype(F32)


def weight_kernel(info, grads, own, other, *refs):
    inputs = refs[:10]
    keep, away, lines, weight, total = refs[10:]
    y, core = info[0], info[1]
    slot = 0
    for ref in inputs:
        for _ in range(0, ref.shape[0], 256):
            lines[:, slot * 256 : slot * 256 + 256] = grads[info[4 + slot]]
            slot += 1
    weight[:, half(y)] = own[pl.ds(pl.multiple_of(core * 3 * HEAD, 16), HEAD)].astype(F32)
    weight[:, half(1 - y)] = other[pl.ds(pl.multiple_of(core * 3 * HEAD, 16), HEAD)].astype(F32)
    total[...] = jnp.zeros_like(total)
    col = 0
    for ref in inputs:
        total[...] += mm(lines[:, col : col + ref.shape[0]], ref[...])
        col += ref.shape[0]
    keep[: 3 * HEAD] = total[:, half(y)]
    away[: 3 * HEAD] = total[:, half(1 - y)].astype(BF)
    sums = row_sums(weight[...] * total[:HEAD])
    keep[3 * HEAD :] = jnp.zeros((16, keep.shape[1]), F32)
    away[3 * HEAD :] = jnp.zeros((16, keep.shape[1]), BF)
    keep[3 * HEAD :, :HEAD] = sums
    away[3 * HEAD :, :HEAD] = sums.astype(BF)


def finish_kernel(info, *refs):
    pieces, (wq, wk, wv, gain, factor) = refs[:18], refs[18:23]
    outs, grad_gain, grad_scale = refs[23:26], refs[26], refs[27]
    stage, stacks = refs[28], refs[29:32]
    scale_sum = jnp.zeros((1, HEAD), F32)
    for slot, parts in enumerate(piece_rows(pieces)):
        dev = info[4 + slot]
        for ref, row in parts:
            stage[slot, row : row + ref.shape[0]] = ref[...]
        rows = pl.ds(pl.multiple_of(dev * HEAD, 16), HEAD)
        for at in range(3):
            stacks[at][rows] = stage[slot, at * HEAD : (at + 1) * HEAD]
        scale_sum += stage[slot, 3 * HEAD :, :HEAD].astype(F32)[0:1]
    grad_scale[...] = scale_sum * factor[...]
    size = stage.shape[2]
    same = lax.broadcasted_iota(jnp.int32, (size, size), 0) == lax.broadcasted_iota(jnp.int32, (size, size), 1)
    unit = jnp.where(same, 1.0, 0.0).astype(BF)
    sums = jnp.zeros((16, size), F32)
    for at, own in enumerate((wq, wk, wv)):
        turned_grad = mm(unit, stacks[at][...], NT)
        outs[at][...] = turned_grad
        sums += row_sums(own[...].astype(F32) * turned_grad)
    grad_gain[...] = sums[0:1] / gain[...].astype(F32)


def input_kernel(info, tokens, grads, grad_mid, own, other, *refs):
    parts, out = refs[:9], refs[9]
    weights, gain, sems = refs[10:13], refs[13], refs[14]
    y = info[0]
    loads = load_weights(info, parts, weights, sems)
    gain[:, half(y)] = own[6 * HEAD :].astype(F32)
    gain[:, half(1 - y)] = other[6 * HEAD :].astype(F32)
    heads, width = grads.shape[0], grads.shape[2]
    turned_grad = jnp.zeros((heads * HEAD, width), F32)
    for at, ref in enumerate(weights):
        part = grads[:, at * HEAD : (at + 1) * HEAD, :].reshape(heads * HEAD, width)
        arrive(loads[at])
        turned_grad += mm(ref[...], part)
    grad = turned_grad.T * gain[0:1]
    values = tokens[...].astype(F32)
    rate = lax.rsqrt(jnp.mean(values * values, axis=-1, keepdims=True) + EPS)
    inner = jnp.mean(grad * values, axis=-1, keepdims=True)
    out[...] = (grad_mid[...] + rate * grad - values * (rate * rate * rate * inner)).astype(BF)


def ring_gather(value, pieces_wanted=True):
    forth, back = [value], [value]
    for _ in range(3):
        forth.append(send(forth[-1], FORTH))
        back.append(send(back[-1], BACK))
    cut = value.shape[0] // 32 * 16
    last = (send(forth[-1][:cut], FORTH), send(back[-1][cut:], BACK))
    return [value, forth[1], back[1], forth[2], back[2], forth[3], back[3], *last]


def chip_gather(value):
    mine = ring_gather(value)
    return mine + [send(piece, CORE_SWAP) for piece in mine]


def weight_parts(shards, core):
    parts = []
    for shard in shards:
        size = shard.shape[0] // 2
        direct = send(lax.dynamic_slice_in_dim(shard, core * size, size, 0), Y_SWAP)
        parts += [shard, direct, send(direct, CORE_SWAP)]
    return parts


def halve(keep, away, where, moves, axis):
    mine = lax.dynamic_index_in_dim(keep, where, axis, keepdims=False)
    theirs = lax.dynamic_index_in_dim(keep, 1 - where, axis, keepdims=False)
    return (mine.astype(F32) + send(theirs, moves).astype(F32)).astype(BF)


def ring_device(
    tokens, cotangent, deal, lengths, gain_attn, w_query, w_key, w_value, w_output, query_scale,
    gain_mlp, w_expand, w_contract
):
    rows, width = tokens.shape[1:]
    c, y = lax.axis_index("ctx"), lax.axis_index("wt")
    core, x, z = c % 2, (c // 2) % 2, c // 4
    table = lax.dynamic_index_in_dim(jnp.asarray(slot_table()), c, 0, keepdims=False)
    info = jnp.concatenate([jnp.stack([y, core, c // 2, lengths[0, 0]]).astype(jnp.int32), table])
    dealt = deal[0]
    total = rows * 16
    softplus = jax.nn.softplus(query_scale)
    scale_col = (LOG2E / math.sqrt(HEAD) * softplus)[:, None]
    factor = (jax.nn.sigmoid(query_scale) / softplus)[None, :]
    inputs = tokens[0]
    cot = cotangent[0]

    arrived = ring_gather(inputs)
    own = call(
        pick_kernel,
        [((6 * HEAD + 16, width // 2), BF)],
        [info, w_query, w_key, w_value, gain_attn[None], gain_mlp[None]],
        smem=1,
        cost=(2 * 480 * 640 * 1280, 3 * 640 * 1280 * 2, 0),
    )[0]
    other = send(own, Y_SWAP)
    mlp_weights = weight_parts((w_output, w_expand, w_contract), core)

    attn_in, mine, partner = [], [], []
    for group in (arrived[:1], arrived[1:3], arrived[3:5], arrived[5:7], arrived[7:]):
        count = sum(part.shape[0] for part in group)
        got = call(
            functools.partial(project_kernel, len(group)),
            [((count, width), BF), ((3 * HEAD, count), BF), ((3 * HEAD, count), BF)],
            [info, *group, own, other, scale_col],
            smem=1,
            scratch=[
                pltpu.VMEM((6 * HEAD, width), BF),
                pltpu.VMEM((16, width), F32),
                pltpu.VMEM((6 * HEAD, count), BF),
            ],
            cost=(2 * 480 * 1280 * count, 4 * 1280 * count, 0),
        )
        attn_in.append(got[0])
        mine.append(got[1])
        partner.append(send(got[2], CORE_SWAP))
    spans = mine + partner

    attended, lse = call(
        forward_kernel,
        [((16, HEAD, rows), BF), ((1, total), F32)],
        [info, dealt, *spans],
        smem=2,
        scratch=[
            pltpu.VMEM((HEAD, total), BF),
            pltpu.VMEM((total, HEAD), BF),
            pltpu.VMEM((HEAD + 16, total), BF),
            pltpu.SMEM((total // SPAN,), jnp.int32),
        ],
        cost=(2 * total * total * 256, 3 * total * 160, total * total // 2),
    )
    attn_in += [send(piece, CORE_SWAP) for piece in attn_in]
    back_weights = weight_parts((w_query, w_key, w_value), core)

    attn_t = lax.all_to_all(attended, "ctx", 0, 0).reshape(width, rows)
    whole_scratch = [pltpu.VMEM((width, width), BF)] * 3
    whole_scratch += [pltpu.VMEM((16, width), F32), pltpu.SemaphoreType.DMA((9,))]
    wide, low = ((rows, width), F32), ((rows, width), BF)
    result, grad_mid, grad_attended_t, act, mlp_in, grad_expanded, grad_mid_low = call(
        mlp_kernel,
        [low, wide, ((width, rows), BF), low, low, low, low],
        [info, inputs, cot, attn_t, own, other, *mlp_weights],
        smem=1,
        anys=9,
        scratch=whole_scratch,
        cost=(12 * rows * width * width, 6 * width * width, 0),
    )
    grad_out = lax.all_to_all(grad_attended_t.reshape(16, HEAD, rows), "ctx", 0, 0)

    terms = call(
        outer_kernel,
        [((width, width // 2), BF)] * 6,
        [info, act, cot, mlp_in, grad_expanded, attn_t, grad_mid_low],
        smem=1,
        cost=(6 * rows * width * width, 6 * width * width, 0),
    )
    bits = {"y": (y, Y_SWAP), "x": (x, X_SWAP), "far": (z // 2, FAR_SWAP), "near": (z % 2, NEAR_SWAP)}
    orders = (("y", "x", "near", "far"), ("x", "y", "near", "far"), ("near", "y", "x", "far"))
    pieces = []
    for at, order in enumerate(orders):
        held = (terms[2 * at].astype(F32) + send(terms[2 * at + 1], CORE_SWAP).astype(F32)).astype(BF)
        held = held.reshape(2, 2, 2, 2, 80, width // 2)
        left = ["y", "x", "far", "near"]
        for name in order:
            held = halve(held, None, bits[name][0], bits[name][1], left.index(name))
            left.remove(name)
        pieces.append(held)
    spread = chip_gather(jnp.concatenate(pieces, axis=0))
    shard = ((width // 2, width), F32)
    line = ((1, width // 2), F32)
    grad_contract, grad_expand, grad_output, grad_gain_mlp = call(
        spread_kernel,
        [shard, shard, shard, line],
        [info, *spread, w_expand, gain_mlp[None]],
        smem=1,
        scratch=[pltpu.VMEM((16, 240, width // 2), BF)],
        cost=(0, 3 * 640 * 1280 * 4, 0),
    )

    grads = call(
        backward_kernel,
        [((16, 3 * HEAD, rows), BF)],
        [info, dealt, *spans, lse, attended, grad_out, scale_col],
        smem=2,
        scratch=[pltpu.VMEM((total, HEAD), BF)] * 4
        + [pltpu.VMEM((HEAD, total), BF)] * 3
        + [
            pltpu.VMEM((1, total), F32),
            pltpu.VMEM((HEAD, total), F32),
            pltpu.VMEM((BLOCK, HEAD), F32),
            pltpu.VMEM((BLOCK, HEAD), F32),
            pltpu.SMEM((total // SPAN,), jnp.int32),
        ],
        cost=(5 * total * total * 256, 6 * total * 160, total * total // 2),
    )[0]

    keep, away = call(
        weight_kernel,
        [((256, width // 2), F32), ((256, width // 2), BF)],
        [info, grads, own, other, *attn_in],
        smem=1,
        scratch=[
            pltpu.VMEM((3 * HEAD, total), BF),
            pltpu.VMEM((HEAD, width), F32),
            pltpu.VMEM((3 * HEAD, width), F32),
        ],
        cost=(2 * 240 * total * width, 2 * total * width, 0),
    )
    summed = (keep + send(away, Y_SWAP).astype(F32)).astype(BF)
    returned = lax.all_to_all(grads, "ctx", 0, 0)
    grad_inputs = call(
        input_kernel,
        [low],
        [info, inputs, returned, grad_mid, own, other, *back_weights],
        smem=1,
        anys=9,
        scratch=whole_scratch,
        cost=(6 * rows * width * width, 6 * width * width, 0),
    )[0]
    spread = chip_gather(summed)
    grad_query, grad_key, grad_value, grad_gain_attn, grad_scale = call(
        finish_kernel,
        [shard, shard, shard, line, ((1, HEAD), F32)],
        [info, *spread, w_query, w_key, w_value, gain_attn[None], factor],
        smem=1,
        scratch=[pltpu.VMEM((16, 256, width // 2), BF)] + [pltpu.VMEM((width, width // 2), BF)] * 3,
        cost=(6 * 640 * 640 * 1280, 3 * 640 * 1280 * 4, 0),
    )
    return (
        result[None], grad_inputs[None], grad_gain_attn[0], grad_query, grad_key, grad_value, grad_output,
        grad_scale[0], grad_gain_mlp[0], grad_expand, grad_contract,
    )


def solution(mesh):
    in_specs = (
        P("wt", "ctx", None),
        P("wt", "ctx", None),
        P("wt", None),
        P("wt", None),
        P("wt"),
        P("wt", None),
        P("wt", None),
        P("wt", None),
        P("wt", None),
        P(),
        P("wt"),
        P("wt", None),
        P("wt", None),
    )
    out_specs = (
        P("wt", "ctx", None),
        P("wt", "ctx", None),
        P("wt"),
        P("wt", None),
        P("wt", None),
        P("wt", None),
        P("wt", None),
        P(),
        P("wt"),
        P("wt", None),
        P("wt", None),
    )
    body = ring_device if mesh.shape["ctx"] == HEADS and mesh.shape["wt"] == 2 else per_device
    return jax.shard_map(
        body, mesh=mesh, in_specs=in_specs, out_specs=out_specs, check_vma=False
    )
```

```python
import functools
import math

import jax
import jax.numpy as jnp
import numpy as np
from jax import lax
from jax.experimental import pallas as pl
from jax.experimental.pallas import tpu as pltpu
from jax.sharding import PartitionSpec as P

HEADS = 16
HEAD = 80
SPAN = 128
LONGEST = 4096


EPS = 1e-06
LOG2E = 1.442695041
NEG = -1e30


def normed(values, gain):
    return values * lax.rsqrt(jnp.mean(values * values, axis=-1, keepdims=True) + EPS) * gain


def locate(dealt_spans, seq_lengths, offset, count, slot_tokens):
    row_ids = offset + jnp.arange(count, dtype=jnp.int32)
    slot_ids = row_ids // SPAN
    matches = slot_ids[:, None] == jnp.arange(dealt_spans.shape[0], dtype=jnp.int32)[None, :]
    span_ids = jnp.sum(jnp.where(matches, dealt_spans[None, :], 0), axis=1)
    natural = span_ids * SPAN + row_ids % SPAN
    sequence = natural // slot_tokens
    position = natural % slot_tokens
    owners = sequence[:, None] == jnp.arange(seq_lengths.shape[0], dtype=jnp.int32)[None, :]
    limits = jnp.sum(jnp.where(owners, seq_lengths[None, :], 0), axis=1)
    return (sequence, position, position < limits)


def permitted(query_place, key_place):
    same_seq = query_place[0][:, None] == key_place[0][None, :]
    causal = key_place[1][None, :] <= query_place[1][:, None]
    return (same_seq & causal & key_place[2][None, :])[None]


def per_device(
    tokens,
    cotangent,
    deal,
    lengths,
    gain_attn,
    w_query,
    w_key,
    w_value,
    w_output,
    query_scale,
    gain_mlp,
    w_expand,
    w_contract,
):
    row_count = tokens.shape[1]
    feat_width = tokens.shape[2]
    group_rows = row_count * lax.axis_size("ctx")
    slot_tokens = min(LONGEST, group_rows)
    block_rows = min(512, group_rows)
    blocks = group_rows // block_rows
    dealt_spans = deal[0]
    seq_lengths = lengths[0]
    inputs = tokens[0].astype(jnp.float32)
    shards = (gain_attn, w_query, w_key, w_value, w_output, gain_mlp, w_expand, w_contract)
    gathered = (
        lax.all_gather(shards[0], "wt", axis=0, tiled=True),
        lax.all_gather(shards[1], "wt", axis=0, tiled=True),
        lax.all_gather(shards[2], "wt", axis=0, tiled=True),
        lax.all_gather(shards[3], "wt", axis=0, tiled=True),
        lax.all_gather(shards[4], "wt", axis=0, tiled=True),
        lax.all_gather(shards[5], "wt", axis=0, tiled=True),
        lax.all_gather(shards[6], "wt", axis=0, tiled=True),
        lax.all_gather(shards[7], "wt", axis=0, tiled=True),
    )
    gain_one = gathered[0].astype(jnp.float32)
    gain_two = gathered[5].astype(jnp.float32)
    query_place = locate(
        dealt_spans, seq_lengths, lax.axis_index("ctx") * row_count, row_count, slot_tokens
    )
    scale_row = LOG2E / math.sqrt(HEAD) * jax.nn.softplus(query_scale)
    attn_in = normed(inputs, gain_one).astype(jnp.bfloat16)
    query_lin = jnp.dot(attn_in, gathered[1], preferred_element_type=jnp.float32)
    queries = (query_lin.reshape(row_count, HEADS, HEAD) * scale_row).astype(jnp.bfloat16)
    key_own = jnp.dot(attn_in, gathered[2], preferred_element_type=jnp.float32).astype(jnp.bfloat16)
    value_own = jnp.dot(attn_in, gathered[3], preferred_element_type=jnp.float32).astype(
        jnp.bfloat16
    )
    portion = (
        lax.all_gather(key_own, "ctx", axis=0, tiled=True),
        lax.all_gather(value_own, "ctx", axis=0, tiled=True),
    )
    running = jnp.full((HEADS, row_count), NEG, jnp.float32)
    count = portion[0].shape[0]
    key_rows = portion[0].reshape(count, HEADS, HEAD)
    value_rows = portion[1].reshape(count, HEADS, HEAD)
    permit_mask = permitted(
        query_place, locate(dealt_spans, seq_lengths, jnp.int32(0), count, slot_tokens)
    )
    scores = jnp.einsum("qhd,khd->hqk", queries, key_rows, preferred_element_type=jnp.float32)
    scores = jnp.where(permit_mask, scores, NEG)
    newest = jnp.maximum(running, jnp.max(scores, axis=-1))
    weights = jnp.where(permit_mask, jnp.exp(scores - newest[..., None]), 0.0)
    running_total = jnp.sum(weights, axis=-1)
    update = jnp.einsum(
        "hqk,khd->qhd", weights.astype(jnp.bfloat16), value_rows, preferred_element_type=jnp.float32
    )
    summed = update
    running, running_total, summed = (newest, running_total, summed)
    log_norm = running + jnp.log(running_total)
    attended = summed / jnp.transpose(running_total)[:, :, None]
    attn_out = attended.reshape(row_count, feat_width).astype(jnp.bfloat16)
    mid = inputs + jnp.dot(attn_out, gathered[4], preferred_element_type=jnp.float32)
    mlp_in = normed(mid, gain_two).astype(jnp.bfloat16)
    expanded = jnp.dot(mlp_in, gathered[6], preferred_element_type=jnp.float32)
    activated = jax.nn.silu(expanded).astype(jnp.bfloat16)
    result = mid + jnp.dot(activated, gathered[7], preferred_element_type=jnp.float32)
    weights_back = (
        lax.all_gather(shards[0], "wt", axis=0, tiled=True),
        lax.all_gather(shards[1], "wt", axis=0, tiled=True),
        lax.all_gather(shards[2], "wt", axis=0, tiled=True),
        lax.all_gather(shards[3], "wt", axis=0, tiled=True),
        lax.all_gather(shards[4], "wt", axis=0, tiled=True),
        lax.all_gather(shards[5], "wt", axis=0, tiled=True),
        lax.all_gather(shards[6], "wt", axis=0, tiled=True),
        lax.all_gather(shards[7], "wt", axis=0, tiled=True),
    )
    whole_keys, whole_values = (
        lax.all_gather(key_own, "ctx", axis=0, tiled=True),
        lax.all_gather(value_own, "ctx", axis=0, tiled=True),
    )
    grad_result = cotangent[0].astype(jnp.float32)
    grad_branch = grad_result.astype(jnp.bfloat16)
    grad_contract = jnp.einsum(
        "tf,td->fd", activated, grad_branch, preferred_element_type=jnp.float32
    )
    grad_act = jnp.einsum(
        "td,fd->tf", grad_branch, weights_back[7], preferred_element_type=jnp.float32
    )
    sigmoid_gate = jax.nn.sigmoid(expanded)
    grad_expanded = (grad_act * sigmoid_gate * (1.0 + expanded * (1.0 - sigmoid_gate))).astype(
        jnp.bfloat16
    )
    grad_expand = jnp.einsum("td,tf->df", mlp_in, grad_expanded, preferred_element_type=jnp.float32)
    grad_mlp_in = jnp.einsum(
        "tf,df->td", grad_expanded, weights_back[6], preferred_element_type=jnp.float32
    )
    unused_two, pull_two = jax.vjp(normed, mid, gain_two)
    grad_mid_norm, grad_gain_two = pull_two(grad_mlp_in)
    grad_mid = grad_result + grad_mid_norm
    grad_mid_low = grad_mid.astype(jnp.bfloat16)
    grad_output_w = jnp.einsum(
        "td,te->de", attn_out, grad_mid_low, preferred_element_type=jnp.float32
    )
    grad_attended = jnp.einsum(
        "te,de->td", grad_mid_low, weights_back[4], preferred_element_type=jnp.float32
    ).astype(jnp.bfloat16)
    out_grad = grad_attended.reshape(row_count, HEADS, HEAD)
    delta = jnp.transpose(jnp.sum(out_grad.astype(jnp.float32) * attended, axis=-1))
    key_blocks = (
        jnp.arange(blocks, dtype=jnp.int32),
        whole_keys.reshape(blocks, block_rows, feat_width),
        whole_values.reshape(blocks, block_rows, feat_width),
    )
    query_zero = jnp.zeros((row_count, HEADS, HEAD), jnp.float32)

    def back_block(query_grad, block_in):
        offset = block_in[0] * block_rows
        key_rows = block_in[1].reshape(block_rows, HEADS, HEAD)
        value_rows = block_in[2].reshape(block_rows, HEADS, HEAD)
        permit_mask = permitted(
            query_place, locate(dealt_spans, seq_lengths, offset, block_rows, slot_tokens)
        )
        scores = jnp.einsum("qhd,khd->hqk", queries, key_rows, preferred_element_type=jnp.float32)
        probabilities = jnp.where(permit_mask, jnp.exp(scores - log_norm[..., None]), 0.0)
        value_grad = jnp.einsum(
            "hqk,qhd->khd",
            probabilities.astype(jnp.bfloat16),
            out_grad,
            preferred_element_type=jnp.float32,
        )
        prob_grad = jnp.einsum(
            "qhd,khd->hqk", out_grad, value_rows, preferred_element_type=jnp.float32
        )
        score_grad = (probabilities * (prob_grad - delta[..., None])).astype(jnp.bfloat16)
        query_grad = query_grad + jnp.einsum(
            "hqk,khd->qhd", score_grad, key_rows, preferred_element_type=jnp.float32
        )
        key_grad = jnp.einsum(
            "hqk,qhd->khd", score_grad, queries, preferred_element_type=jnp.float32
        )
        return (
            query_grad,
            (key_grad.reshape(block_rows, feat_width), value_grad.reshape(block_rows, feat_width)),
        )

    query_grad, key_terms = lax.scan(back_block, query_zero, key_blocks)
    key_sum, value_sum = (
        lax.psum_scatter(
            key_terms[0].reshape(group_rows, feat_width).astype(jnp.bfloat16),
            "ctx",
            scatter_dimension=0,
            tiled=True,
        ).astype(jnp.float32),
        lax.psum_scatter(
            key_terms[1].reshape(group_rows, feat_width).astype(jnp.bfloat16),
            "ctx",
            scatter_dimension=0,
            tiled=True,
        ).astype(jnp.float32),
    )
    grad_keys = key_sum.astype(jnp.bfloat16)
    grad_values = value_sum.astype(jnp.bfloat16)
    grad_query_lin = (query_grad * scale_row).reshape(row_count, feat_width).astype(jnp.bfloat16)
    grad_scale = (
        jnp.sum(query_grad * query_lin.reshape(row_count, HEADS, HEAD), axis=(0, 1))
        * (LOG2E / math.sqrt(HEAD))
        * jax.nn.sigmoid(query_scale)
    )
    grad_query_w = jnp.einsum(
        "td,te->de", attn_in, grad_query_lin, preferred_element_type=jnp.float32
    )
    grad_key_w = jnp.einsum("td,te->de", attn_in, grad_keys, preferred_element_type=jnp.float32)
    grad_value_w = jnp.einsum("td,te->de", attn_in, grad_values, preferred_element_type=jnp.float32)
    grad_attn_in = jnp.einsum(
        "te,de->td", grad_query_lin, weights_back[1], preferred_element_type=jnp.float32
    )
    grad_attn_in = grad_attn_in + jnp.einsum(
        "te,de->td", grad_keys, weights_back[2], preferred_element_type=jnp.float32
    )
    grad_attn_in = grad_attn_in + jnp.einsum(
        "te,de->td", grad_values, weights_back[3], preferred_element_type=jnp.float32
    )
    unused_one, pull_one = jax.vjp(normed, inputs, gain_one)
    grad_in_norm, grad_gain_one = pull_one(grad_attn_in)
    grad_inputs = (grad_mid + grad_in_norm).astype(jnp.bfloat16)
    terms = (
        grad_gain_one,
        grad_query_w,
        grad_key_w,
        grad_value_w,
        grad_output_w,
        jnp.tile(grad_scale, lax.axis_size("wt")),
        grad_gain_two,
        grad_expand,
        grad_contract,
    )
    shares = (
        lax.psum_scatter(
            terms[0].astype(jnp.bfloat16), "wt", scatter_dimension=0, tiled=True
        ).astype(jnp.float32),
        lax.psum_scatter(
            terms[1].astype(jnp.bfloat16), "wt", scatter_dimension=0, tiled=True
        ).astype(jnp.float32),
        lax.psum_scatter(
            terms[2].astype(jnp.bfloat16), "wt", scatter_dimension=0, tiled=True
        ).astype(jnp.float32),
        lax.psum_scatter(
            terms[3].astype(jnp.bfloat16), "wt", scatter_dimension=0, tiled=True
        ).astype(jnp.float32),
        lax.psum_scatter(
            terms[4].astype(jnp.bfloat16), "wt", scatter_dimension=0, tiled=True
        ).astype(jnp.float32),
        lax.psum_scatter(
            terms[5].astype(jnp.bfloat16), "wt", scatter_dimension=0, tiled=True
        ).astype(jnp.float32),
        lax.psum_scatter(
            terms[6].astype(jnp.bfloat16), "wt", scatter_dimension=0, tiled=True
        ).astype(jnp.float32),
        lax.psum_scatter(
            terms[7].astype(jnp.bfloat16), "wt", scatter_dimension=0, tiled=True
        ).astype(jnp.float32),
        lax.psum_scatter(
            terms[8].astype(jnp.bfloat16), "wt", scatter_dimension=0, tiled=True
        ).astype(jnp.float32),
    )
    totals = (
        lax.psum(shares[0].astype(jnp.bfloat16), "ctx").astype(jnp.float32),
        lax.psum(shares[1].astype(jnp.bfloat16), "ctx").astype(jnp.float32),
        lax.psum(shares[2].astype(jnp.bfloat16), "ctx").astype(jnp.float32),
        lax.psum(shares[3].astype(jnp.bfloat16), "ctx").astype(jnp.float32),
        lax.psum(shares[4].astype(jnp.bfloat16), "ctx").astype(jnp.float32),
        lax.psum(shares[5].astype(jnp.bfloat16), "ctx").astype(jnp.float32),
        lax.psum(shares[6].astype(jnp.bfloat16), "ctx").astype(jnp.float32),
        lax.psum(shares[7].astype(jnp.bfloat16), "ctx").astype(jnp.float32),
        lax.psum(shares[8].astype(jnp.bfloat16), "ctx").astype(jnp.float32),
    )
    return (
        result.astype(jnp.bfloat16)[None],
        grad_inputs[None],
        totals[0],
        totals[1],
        totals[2],
        totals[3],
        totals[4],
        totals[5],
        totals[6],
        totals[7],
        totals[8],
    )


BF = jnp.bfloat16
F32 = jnp.float32
NN = (((1,), (0,)), ((), ()))
NT = (((1,), (1,)), ((), ()))
AXES = ("ctx", "wt")
LIMIT = 56 * 1024 * 1024

RING = ((0, 0), (1, 0), (2, 0), (3, 0), (3, 1), (2, 1), (1, 1), (0, 1))
PLACE = {chip: at for at, chip in enumerate(RING)}
OFFSETS = (0, -1, 1, -2, 2, -3, 3, 4)


def flat(z, x, core, y):
    return ((z * 2 + x) * 2 + core) * 2 + y


def pairs(move):
    return [
        (flat(z, x, core, y), flat(*move(z, x, core, y)))
        for z in range(4)
        for x in range(2)
        for core in range(2)
        for y in range(2)
    ]


def turned(by):
    def move(z, x, core, y):
        return (*RING[(PLACE[(z, x)] + by) % 8], core, y)

    return move


CORE_SWAP = pairs(lambda z, x, core, y: (z, x, 1 - core, y))
Y_SWAP = pairs(lambda z, x, core, y: (z, x, core, 1 - y))
X_SWAP = pairs(lambda z, x, core, y: (z, 1 - x, core, y))
NEAR_SWAP = pairs(lambda z, x, core, y: (z ^ 1, x, core, y))
FAR_SWAP = pairs(lambda z, x, core, y: (z ^ 2, x, core, y))
FORTH = pairs(turned(1))
BACK = pairs(turned(-1))


def slot_table():
    rows = []
    for c in range(16):
        z, x, core = c // 4, (c // 2) % 2, c % 2
        chips = [RING[(PLACE[(z, x)] + by) % 8] for by in OFFSETS]
        own = [(a * 2 + b) * 2 + core for a, b in chips]
        rows.append(own + [dev ^ 1 for dev in own])
    return np.asarray(rows, np.int32)


def send(value, moves):
    return lax.ppermute(value, AXES, moves)


def mm(left, right, dims=NN):
    return lax.dot_general(left, right, dims, preferred_element_type=F32)


def call(body, outs, args, smem=0, anys=(), scratch=(), cost=None, out_anys=(), aliases=None):
    whole, anywhere = pl.BlockSpec(memory_space=pltpu.VMEM), pl.BlockSpec(memory_space=pl.ANY)
    specs = [pl.BlockSpec(memory_space=pltpu.SMEM)] * smem
    specs += [anywhere if at in anys else whole for at in range(smem, len(args))]
    estimate = None
    if cost is not None:
        estimate = pl.CostEstimate(flops=int(cost[0]), bytes_accessed=int(cost[1]), transcendentals=int(cost[2]))
    return pl.pallas_call(
        body,
        out_shape=[jax.ShapeDtypeStruct(shape, kind) for shape, kind in outs],
        in_specs=specs,
        out_specs=[anywhere if at in out_anys else whole for at in range(len(outs))],
        scratch_shapes=list(scratch),
        input_output_aliases=aliases or {},
        cost_estimate=estimate,
        compiler_params=pltpu.CompilerParams(vmem_limit_bytes=LIMIT),
    )(*args)


def half(y, width=640):
    return pl.ds(pl.multiple_of(y * width, 128), width)


def pick_kernel(info, wq, wk, wv, gain_a, gain_m, out):
    chip = info[2]
    cols = lax.broadcasted_iota(jnp.int32, (2 * HEAD, wq.shape[1]), 1)
    rows = lax.broadcasted_iota(jnp.int32, (2 * HEAD, wq.shape[1]), 0)
    chosen = jnp.where(cols == rows + chip * (2 * HEAD), 1.0, 0.0).astype(BF)
    for at, ref in enumerate((wq, wk, wv)):
        both = mm(chosen, ref[...], NT).astype(BF)
        out[at * HEAD : (at + 1) * HEAD] = both[:HEAD]
        out[3 * HEAD + at * HEAD : 3 * HEAD + (at + 1) * HEAD] = both[HEAD:]
    line = lax.broadcasted_iota(jnp.int32, (16, gain_a.shape[1]), 0)
    tail = jnp.where(line == 0, gain_a[...].astype(F32), 0.0)
    tail = jnp.where(line == 1, gain_m[...].astype(F32), tail)
    out[6 * HEAD :] = tail.astype(BF)


def project_kernel(count, start, info, *refs):
    xs = refs[:count]
    own, other, scale = refs[count : count + 3]
    whole, mine, partner, attn_in, weight, gain, lines, sem = refs[-8:]
    y, core = info[0], info[1]
    weight[:, half(y)] = own[: 6 * HEAD]
    weight[:, half(1 - y)] = other[: 6 * HEAD]
    gain[:, half(y)] = own[6 * HEAD :].astype(F32)
    gain[:, half(1 - y)] = other[6 * HEAD :].astype(F32)
    row = 0
    for ref in xs:
        values = ref[...].astype(F32)
        scaled = values * lax.rsqrt(jnp.mean(values * values, axis=-1, keepdims=True) + EPS)
        attn_in[row : row + ref.shape[0]] = (scaled * gain[0:1]).astype(BF)
        row += ref.shape[0]
    copy = pltpu.make_async_copy(attn_in, whole.at[pl.ds(start, row)], sem)
    copy.start()
    lin = mm(weight[...], attn_in[...], NT)
    for head in range(2):
        base = head * 3 * HEAD
        lines[base : base + HEAD] = (lin[base : base + HEAD] * scale[...]).astype(BF)
        lines[base + HEAD : base + 3 * HEAD] = lin[base + HEAD : base + 3 * HEAD].astype(BF)
    mine[...] = lines[pl.ds(pl.multiple_of(core * 3 * HEAD, 16), 3 * HEAD)]
    partner[...] = lines[pl.ds(pl.multiple_of((1 - core) * 3 * HEAD, 16), 3 * HEAD)]
    copy.wait()


def span_slots(pieces):
    return [(ref, col) for ref in pieces for col in range(0, ref.shape[1], SPAN)]


def natural_span(info, deal, slot):
    return deal[2 * info[4 + slot // 2] + slot % 2]


def at_span(span):
    return pl.ds(pl.multiple_of(span * SPAN, SPAN), SPAN)


BLOCK = 1024
WIDE = 128


def block_at(at):
    return pl.ds(pl.multiple_of(at * BLOCK, BLOCK), BLOCK)


def in_parts(line):
    high = line.astype(BF)
    rest = line - high.astype(F32)
    middle = rest.astype(BF)
    low = (rest - middle.astype(F32)).astype(BF)
    at = lax.broadcasted_iota(jnp.int32, (16, line.shape[1]), 0)
    rows = jnp.where(at == 0, high.astype(F32), 0.0)
    rows = jnp.where(at == 1, middle.astype(F32), rows)
    return jnp.where(at == 2, low.astype(F32), rows).astype(BF)


def ones_behind(ref):
    at = lax.broadcasted_iota(jnp.int32, ref.shape, 1)
    ref[...] = jnp.where((at >= HEAD) & (at < HEAD + 3), 1.0, 0.0).astype(BF)


def forward_kernel(info, deal, *refs):
    pieces = refs[:10]
    out, q_out, k_out, queries, keys, values, lse, dealt = refs[10:]
    total = queries.shape[1]
    length = info[3]
    spans = total // SPAN
    blocks = total // BLOCK

    @pl.loop(0, spans)
    def _(at):
        dealt[deal[at]] = at

    line = lax.broadcasted_iota(jnp.int32, (16, total), 0)
    values[HEAD:] = jnp.where(line == 0, 1.0, 0.0).astype(BF)
    queries[HEAD:] = jnp.zeros((WIDE - HEAD, total), BF)
    ones_behind(keys)
    longest = jnp.zeros((1, SPAN), F32)
    for slot, (ref, col) in enumerate(span_slots(pieces)):
        where = at_span(natural_span(info, deal, slot))
        key = ref[HEAD : 2 * HEAD, col : col + SPAN]
        queries[:HEAD, where] = ref[:HEAD, col : col + SPAN]
        keys[where, :HEAD] = key.T
        values[:HEAD, where] = ref[2 * HEAD :, col : col + SPAN]
        sizes = key.astype(F32)
        longest = jnp.maximum(longest, jnp.sum(sizes * sizes, axis=0, keepdims=True))
    longest = jnp.max(longest, axis=1, keepdims=True)

    key_at = lax.broadcasted_iota(jnp.int32, (BLOCK, BLOCK), 0)
    query_at = lax.broadcasted_iota(jnp.int32, (BLOCK, BLOCK), 1)

    def scores_of(masked, i, j):
        scores = mm(keys[block_at(j), :], queries[:, block_at(i)])
        if masked:
            key_pos = j * BLOCK + key_at
            allowed = (key_pos <= i * BLOCK + query_at) & (key_pos < length)
            scores = jnp.where(allowed, scores, NEG)
        return scores

    def finish(i, peak, acc):
        here = block_at(i)
        norm = acc[HEAD : HEAD + 1]
        lse[:, here] = peak + jnp.log(norm)
        attended = (acc[:HEAD] / norm).astype(BF)
        for part in range(BLOCK // SPAN):
            row = dealt[i * (BLOCK // SPAN) + part]
            out[row // 2, :, at_span(row % 2)] = attended[:, part * SPAN : (part + 1) * SPAN]
        return jnp.min(norm)

    def bounded(i, least):
        here = block_at(i)
        query = queries[:HEAD, here].astype(F32)
        bound = jnp.sqrt(jnp.sum(query * query, axis=0, keepdims=True) * longest) - 40.0
        shift = in_parts(-bound)
        queries[HEAD : HEAD + 16, here] = shift

        def step(masked, j, acc):
            weights = jnp.exp(scores_of(masked, i, j)).astype(BF)
            return acc + mm(values[:, block_at(j)], weights)

        split = jnp.minimum(i, length // BLOCK)
        acc = lax.fori_loop(0, split, functools.partial(step, False), jnp.zeros((HEAD + 16, BLOCK), F32))
        acc = lax.fori_loop(split, i + 1, functools.partial(step, True), acc)
        exact = jnp.sum(shift.astype(F32), axis=0, keepdims=True)
        return jnp.minimum(least, finish(i, -exact, acc))

    least = lax.fori_loop(0, blocks, bounded, jnp.float32(1.0))

    @pl.when(jnp.logical_not(least > 1e-26))
    def _():
        queries[HEAD:] = jnp.zeros((WIDE - HEAD, total), BF)

        @pl.loop(0, blocks)
        def _(i):
            def step(j, carry):
                peak, acc = carry
                scores = scores_of(True, i, j)
                newest = jnp.maximum(peak, jnp.max(scores, axis=0, keepdims=True))
                weights = jnp.exp(scores - newest).astype(BF)
                return newest, acc * jnp.exp(peak - newest) + mm(values[:, block_at(j)], weights)

            start = (jnp.full((1, BLOCK), NEG, F32), jnp.zeros((HEAD + 16, BLOCK), F32))
            finish(i, *lax.fori_loop(0, i + 1, step, start))

    q_out[:HEAD] = queries[:HEAD]
    q_out[HEAD : HEAD + 16] = in_parts(-lse[...])
    q_out[HEAD + 16 :] = jnp.zeros((WIDE - HEAD - 16, total), BF)
    k_out[...] = keys[...]


def turn_kernel(info, deal, *refs):
    pieces, (k_t, q_n, v_n) = refs[:10], refs[10:]
    q_n[...] = jnp.zeros_like(q_n)
    ones_behind(v_n)
    for slot, (ref, col) in enumerate(span_slots(pieces)):
        where = at_span(natural_span(info, deal, slot))
        cols = slice(col, col + SPAN)
        k_t[:, where] = ref[HEAD : 2 * HEAD, cols]
        q_n[where, :HEAD] = ref[:HEAD, cols].T
        v_n[where, :HEAD] = ref[2 * HEAD :, cols].T


def backward_kernel(info, deal, *refs):
    q_t, k_n, k_t, q_n, v_n, attended, grad_out, scale, out, g_t, g_n, delta, dq_t, dk, dv, dealt = refs
    total = q_t.shape[1]
    length = info[3]
    spans = total // SPAN
    blocks = total // BLOCK

    @pl.loop(0, spans)
    def _(at):
        dealt[deal[at]] = at

    g_n[...] = jnp.zeros_like(g_n)
    g_t[HEAD:] = jnp.zeros((WIDE - HEAD, total), BF)
    for row in range(spans):
        where = at_span(deal[row])
        cols = slice(row % 2 * SPAN, row % 2 * SPAN + SPAN)
        grad = grad_out[row // 2, :, cols]
        g_t[:HEAD, where] = grad
        g_n[where, :HEAD] = grad.T
        product = grad.astype(F32) * attended[row // 2, :, cols].astype(F32)
        delta[:, where] = jnp.sum(product, axis=0, keepdims=True)
    g_t[HEAD : HEAD + 16] = in_parts(-delta[...])
    dq_t[...] = jnp.zeros_like(dq_t)

    key_at = lax.broadcasted_iota(jnp.int32, (BLOCK, BLOCK), 0)
    query_at = lax.broadcasted_iota(jnp.int32, (BLOCK, BLOCK), 1)

    @pl.loop(0, blocks)
    def _(j):
        there = block_at(j)
        dk[...] = jnp.zeros_like(dk)
        dv[...] = jnp.zeros_like(dv)

        def step(masked, i, carry):
            here = block_at(i)
            probs = jnp.exp(mm(k_n[there, :], q_t[:, here]))
            if masked:
                key_pos = j * BLOCK + key_at
                allowed = (key_pos <= i * BLOCK + query_at) & (key_pos < length)
                probs = jnp.where(allowed, probs, 0.0)
            grad_scores = (probs * mm(v_n[there, :], g_t[:, here])).astype(BF)
            dv[...] += mm(probs.astype(BF), g_n[here, :])
            dk[...] += mm(grad_scores, q_n[here, :])
            dq_t[:, here] += mm(k_t[:, there], grad_scores)
            return carry

        split = jnp.where((j + 1) * BLOCK <= length, j + 1, blocks)
        lax.fori_loop(j, split, functools.partial(step, True), 0)
        lax.fori_loop(split, blocks, functools.partial(step, False), 0)
        for part in range(BLOCK // SPAN):
            row = dealt[j * (BLOCK // SPAN) + part]
            rows = slice(part * SPAN, (part + 1) * SPAN)
            out[row // 2, HEAD : 2 * HEAD, at_span(row % 2)] = dk[rows].T[:HEAD].astype(BF)
            out[row // 2, 2 * HEAD :, at_span(row % 2)] = dv[rows].T[:HEAD].astype(BF)

    for row in range(spans):
        cols = slice(row % 2 * SPAN, row % 2 * SPAN + SPAN)
        out[row // 2, :HEAD, cols] = (dq_t[:, at_span(deal[row])] * scale[...]).astype(BF)


def load_weights(info, own, direct, passed, wholes, sems):
    y, core = info[0], info[1]
    started = []
    count = 0
    for at, whole in enumerate(wholes):
        rows, part = own[at].shape[0], own[at].shape[0] // 2
        far = (1 - y) * rows
        places = [(own[at], y * rows)]
        for chunks, base in ((direct, far + core * part), (passed, far + (1 - core) * part)):
            start = 0
            for chunk in chunks:
                low, high = max(start, at * part), min(start + chunk.shape[0], at * part + part)
                if low < high:
                    places.append((chunk.at[pl.ds(low - start, high - low)], base + low - at * part))
                start += chunk.shape[0]
        copies = []
        for ref, start in places:
            target = whole.at[pl.ds(pl.multiple_of(start, 16), ref.shape[0])]
            copies.append(pltpu.make_async_copy(ref, target, sems.at[count]))
            copies[-1].start()
            count += 1
        started.append(copies)
    return started


def arrive(copies):
    for copy in copies:
        copy.wait()


def mlp_kernel(chunks, info, tokens, cotangent, attn_t, own, other, *refs):
    shards, direct, passed = refs[:3], refs[3 : 3 + chunks], refs[3 + chunks : 3 + 2 * chunks]
    refs = refs[3 + 2 * chunks :]
    outs = refs[:5]
    w_output, w_expand, w_contract, gain, right, sems = refs[5:]
    result, grad_mid_out, grad_attended_t, away, rights = outs
    y, core = info[0], info[1]
    loads = load_weights(info, shards, direct, passed, (w_output, w_expand, w_contract), sems)
    gain[:, half(y)] = own[6 * HEAD :].astype(F32)
    gain[:, half(1 - y)] = other[6 * HEAD :].astype(F32)
    gains = gain[1:2]
    attn = attn_t[...].T
    arrive(loads[0])
    mid = tokens[...].astype(F32) + mm(attn, w_output[...])
    rate = lax.rsqrt(jnp.mean(mid * mid, axis=-1, keepdims=True) + EPS)
    mlp_in = (mid * rate * gains).astype(BF)
    away[1] = mlp_in
    arrive(loads[1])
    expanded = mm(mlp_in, w_expand[...])
    gate = jax.nn.sigmoid(expanded)
    act = (expanded * gate).astype(BF)
    away[0] = act
    arrive(loads[2])
    result[...] = (mid + mm(act, w_contract[...])).astype(BF)
    grad_act = mm(cotangent[...], w_contract[...], NT)
    grad_expanded = (grad_act * gate * (1.0 + expanded * (1.0 - gate))).astype(BF)
    right[0] = grad_expanded
    grad_mlp_in = mm(grad_expanded, w_expand[...], NT) * gains
    inner = jnp.mean(grad_mlp_in * mid, axis=-1, keepdims=True)
    grad_mid = cotangent[...].astype(F32) + rate * grad_mlp_in - mid * (rate * rate * rate * inner)
    grad_mid_out[...] = grad_mid
    low = grad_mid.astype(BF)
    right[1] = low
    grad_attended_t[...] = mm(w_output[...], low, NT).astype(BF)
    for at in range(2):
        rights[:, at * 640 : at * 640 + 640] = right[at, :, half(core)]
        away[2, :, at * 640 : at * 640 + 640] = right[at, :, half(1 - core)]


BITS = ("y", "x", "far", "near")
ORDERS = (("y", "x", "near", "far"), ("x", "near", "y", "far"), ("near", "y", "x", "far"))
BIT_AT = {"y": 0, "x": 20, "near": 21, "far": 22}
PART = 80


def left_bits(order, done):
    return [name for name in BITS if name not in order[:done]]


def halves(info, order, done):
    left = left_bits(order, done)
    name = order[done]
    bit = info[BIT_AT[name]]
    stride = 1 << (len(left) - 1 - left.index(name))
    count = 1 << len(left)
    bases = [block for block in range(count) if block & stride == 0]
    return [(base + bit * stride, base + (1 - bit) * stride) for base in bases]


def rows_of(block):
    start = block * PART
    return pl.ds(start if isinstance(block, int) else pl.multiple_of(start, 16), PART)


def outer_kernel(info, own, rights, partner, attn_t, attn_t_partner, cot, cot_partner, *refs):
    outs, (left, right, full) = refs[:6], refs[6:]
    core = info[1]
    rows = cot.shape[0]
    for at in range(3):
        if at < 2:
            left[:, :rows] = own[at].T
            left[:, rows:] = partner[at].T
        else:
            left[:, :rows] = attn_t[...]
            left[:, rows:] = attn_t_partner[...]
        if at == 0:
            right[:rows] = cot[:, half(core)]
            right[rows:] = cot_partner[:, half(core)]
        else:
            cols = slice((at - 1) * 640, at * 640)
            right[:rows] = rights[:, cols]
            right[rows:] = partner[2, :, cols]
        full[...] = mm(left[...], right[...]).astype(BF)
        for to, (kept, sent) in enumerate(halves(info, ORDERS[at], 0)):
            outs[at][rows_of(to)] = full[rows_of(kept)]
            outs[3 + at][rows_of(to)] = full[rows_of(sent)]


def round_kernel(done, info, *refs):
    kept, came, outs = refs[:3], refs[3:6], refs[6:]
    for at in range(3):
        for to, (mine, theirs) in enumerate(halves(info, ORDERS[at], done)):
            if len(outs) == 6:
                stay, away, target = outs[at], outs[3 + at], rows_of(to)
            else:
                stay, away, target = outs[0], outs[1], rows_of(at)
            for out, block in ((stay, mine), (away, theirs)):
                total = kept[at][rows_of(block)].astype(F32) + came[at][rows_of(block)].astype(F32)
                out[target] = total.astype(BF)


def folded(products):
    return sum(products[:, at : at + 128] for at in range(0, products.shape[1], 128))


def row_sums(products):
    ones = jnp.ones((16, products.shape[1]), BF)
    high = products.astype(BF)
    low = (products - high.astype(F32)).astype(BF)
    return mm(ones, high, NT) + mm(ones, low, NT)


def stack_kernel(*refs):
    for at, ref in enumerate(refs[:-1]):
        refs[-1][at] = ref[...]


def joined(pieces, last):
    count = len(pieces) // 2
    ready = []
    for colour in range(2):
        group = pieces[colour * count : colour * count + count]
        cut = group[-2].shape[0]
        last[colour, :cut] = group[-2][...]
        last[colour, cut:] = group[-1][...]
        ready += [*group[:-2], last.at[colour]]
    return ready


def slot_of(at, count, first):
    return first + at if at < count else 8 + first + at - count


def scatter(info, refs, first, blocks, sems, outs, expand, sums):
    copies = []
    for at, ref in enumerate(refs):
        dev = info[4 + slot_of(at, len(refs) // 2, first)]
        block = ((dev // 2) % 2) * 4 + dev // 4
        rows = pl.ds(pl.multiple_of(block * PART, 16), PART)
        for way in range(3):
            blocks[3 * at + way] = ref[way * PART : (way + 1) * PART].astype(F32)
            target = outs[way].at[rows, half(dev % 2)]
            copies.append(pltpu.make_async_copy(blocks.at[3 * at + way], target, sems.at[3 * at + way]))
            copies[-1].start()
        sums[rows] += folded(blocks[3 * at + 1] * expand[rows, half(dev % 2)].astype(F32))
    return copies


def spread_kernel(info, near, near_partner, expand, sums, *refs):
    outs, (blocks, sems) = refs[:3], refs[3:]
    pieces = [stack.at[at] for stack in (near, near_partner) for at in range(5)]
    sums[...] = jnp.zeros_like(sums)
    arrive(scatter(info, pieces, 0, blocks, sems, outs, expand, sums))


def spread_last_kernel(info, *refs):
    pieces, (before, gain, expand), (*outs, grad_gain), refs = refs[:8], refs[8:11], refs[14:18], refs[18:]
    blocks, last, sums, sems = refs
    sums[...] = before[...]
    copies = scatter(info, joined(pieces, last), 5, blocks, sems, outs, expand, sums)
    size = sums.shape[0]
    grad_gain[...] = (row_sums(sums[...])[0:1] / gain[...].astype(F32)).reshape(size)
    arrive(copies)


def weight_kernel(info, grads, own, other, *refs):
    inputs = refs[:2]
    keep, away, lines, weight, total, attn_in, sems = refs[2:]
    y, core = info[0], info[1]
    rows = attn_in.shape[0] // 8
    loads = []
    for at in range(8):
        source = inputs[at // 4].at[pl.ds(at % 4 * rows, rows)]
        loads.append(pltpu.make_async_copy(source, attn_in.at[pl.ds(at * rows, rows)], sems.at[at]))
        loads[-1].start()
    for slot in range(16):
        lines[:, slot * 256 : slot * 256 + 256] = grads[info[4 + slot]]
    weight[:, half(y)] = own[pl.ds(pl.multiple_of(core * 3 * HEAD, 16), HEAD)].astype(F32)
    weight[:, half(1 - y)] = other[pl.ds(pl.multiple_of(core * 3 * HEAD, 16), HEAD)].astype(F32)
    total[...] = jnp.zeros_like(total)
    for at in range(4):
        loads[2 * at].wait()
        loads[2 * at + 1].wait()
        part = slice(2 * at * rows, 2 * (at + 1) * rows)
        total[...] += mm(lines[:, part], attn_in[part])
    keep[: 3 * HEAD] = total[:, half(y)]
    away[: 3 * HEAD] = total[:, half(1 - y)].astype(BF)
    sums = row_sums(weight[...] * total[:HEAD])
    keep[3 * HEAD :] = jnp.zeros((16, keep.shape[1]), F32)
    away[3 * HEAD :] = jnp.zeros((16, keep.shape[1]), BF)
    keep[3 * HEAD :, :HEAD] = sums
    away[3 * HEAD :, :HEAD] = sums.astype(BF)


def finish_kernel(info, near, near_partner, *refs):
    pieces, shards, (gain, factor), refs = refs[:8], refs[8:11], refs[11:13], refs[13:]
    outs, (grad_gain, grad_scale), (stacks, weights, last, turned, sems) = refs[:3], refs[3:5], refs[5:]
    loads = [pltpu.make_async_copy(ref, weights.at[at], sems.at[at]) for at, ref in enumerate(shards)]
    for load in loads:
        load.start()
    scale_sum = jnp.zeros((1, HEAD), F32)
    early = [stack.at[at] for stack in (near, near_partner) for at in range(5)]
    for first, group in ((0, early), (5, joined(pieces, last))):
        for at, ref in enumerate(group):
            rows = pl.ds(pl.multiple_of(info[4 + slot_of(at, len(group) // 2, first)] * HEAD, 16), HEAD)
            for way in range(3):
                stacks[way, rows] = ref[way * HEAD : (way + 1) * HEAD]
            scale_sum += ref[3 * HEAD :, :HEAD].astype(F32)[0:1]
    grad_scale[...] = scale_sum * factor[...]
    size = turned.shape[1]
    same = lax.broadcasted_iota(jnp.int32, (size, size), 0) == lax.broadcasted_iota(jnp.int32, (size, size), 1)
    unit = jnp.where(same, 1.0, 0.0).astype(BF)
    copies = []
    sums = jnp.zeros((size, 128), F32)
    for at, out in enumerate(outs):
        turned[at] = mm(unit, stacks[at], NT)
        copies.append(pltpu.make_async_copy(turned.at[at], out, sems.at[3 + at]))
        copies[-1].start()
        loads[at].wait()
        sums += folded(weights[at].astype(F32) * turned[at])
    grad_gain[...] = (row_sums(sums)[0:1] / gain[...].astype(F32)).reshape(size)
    arrive(copies)


def input_kernel(chunks, info, tokens, grads, grad_mid, own, other, *refs):
    shards, direct, passed = refs[:3], refs[3 : 3 + chunks], refs[3 + chunks : 3 + 2 * chunks]
    out, *weights, gain, sems = refs[3 + 2 * chunks :]
    y = info[0]
    loads = load_weights(info, shards, direct, passed, weights, sems)
    gain[:, half(y)] = own[6 * HEAD :].astype(F32)
    gain[:, half(1 - y)] = other[6 * HEAD :].astype(F32)
    heads, width = grads.shape[0], grads.shape[2]
    turned_grad = jnp.zeros((heads * HEAD, width), F32)
    for at, ref in enumerate(weights):
        part = grads[:, at * HEAD : (at + 1) * HEAD, :].reshape(heads * HEAD, width)
        arrive(loads[at])
        turned_grad += mm(ref[...], part)
    grad = turned_grad.T * gain[0:1]
    values = tokens[...].astype(F32)
    rate = lax.rsqrt(jnp.mean(values * values, axis=-1, keepdims=True) + EPS)
    inner = jnp.mean(grad * values, axis=-1, keepdims=True)
    out[...] = (grad_mid[...] + rate * grad - values * (rate * rate * rate * inner)).astype(BF)


def after(values, *others):
    return lax.optimization_barrier((tuple(values), others))[0]


def weight_rows(shards, core):
    size = shards[0].shape[0] // 2
    return jnp.concatenate([lax.dynamic_slice_in_dim(shard, core * size, size, 0) for shard in shards], axis=0)


def ring_device(
    tokens, cotangent, deal, lengths, gain_attn, w_query, w_key, w_value, w_output, query_scale,
    gain_mlp, w_expand, w_contract
):
    rows, width = tokens.shape[1:]
    c, y = lax.axis_index("ctx"), lax.axis_index("wt")
    core, x, z = c % 2, (c // 2) % 2, c // 4
    table = lax.dynamic_index_in_dim(jnp.asarray(slot_table()), c, 0, keepdims=False)
    head = jnp.stack([y, core, c // 2, lengths[0, 0]]).astype(jnp.int32)
    info = jnp.concatenate([head, table, jnp.stack([x, z % 2, z // 2]).astype(jnp.int32)])
    dealt = deal[0]
    total = rows * 16
    softplus = jax.nn.softplus(query_scale)
    scale_col = (LOG2E / math.sqrt(HEAD) * softplus)[:, None]
    factor = (jax.nn.sigmoid(query_scale) / softplus)[None, :]
    inputs = tokens[0]
    cot = cotangent[0]
    cut = rows // 2
    mine, partner, gathered = [], [], []

    def project(*group):
        count = sum(part.shape[0] for part in group)
        start = sum(piece.shape[1] for piece in mine)
        args = [info, *group, own, other, scale_col]
        got = call(
            functools.partial(project_kernel, len(group), start),
            [((8 * rows, width), BF), ((3 * HEAD, count), BF), ((3 * HEAD, count), BF)],
            args + gathered[-1:],
            smem=1,
            anys=range(len(args), len(args) + 1),
            out_anys=(0,),
            aliases={len(args): 0} if gathered else None,
            scratch=[
                pltpu.VMEM((count, width), BF),
                pltpu.VMEM((6 * HEAD, width), BF),
                pltpu.VMEM((16, width), F32),
                pltpu.VMEM((6 * HEAD, count), BF),
                pltpu.SemaphoreType.DMA,
            ],
            cost=(2 * 480 * 1280 * count, 4 * 1280 * count, 0),
        )
        gathered.append(got[0])
        mine.append(got[1])
        partner.append(send(got[2], CORE_SWAP))
        return got[1]

    forth1, back1 = send(inputs, FORTH), send(inputs, BACK)
    size = width // 4
    first_rows = lax.dynamic_slice_in_dim(w_output, core * size, 128, 0)
    direct, passed = [send(first_rows, Y_SWAP)], []
    own = call(
        pick_kernel,
        [((6 * HEAD + 16, width // 2), BF)],
        [info, w_query, w_key, w_value, gain_attn[None], gain_mlp[None]],
        smem=1,
        cost=(2 * 480 * 640 * 1280, 3 * 640 * 1280 * 2, 0),
    )[0]
    other = send(own, Y_SWAP)
    rows_out = weight_rows(after((w_output, w_expand, w_contract), own), core)
    rows_back = weight_rows(after((w_query, w_key, w_value), own), core)
    chunks = [rows_out[128:256], rows_out[256:512], rows_out[512:640], rows_out[640:], rows_back[:288]]
    chunks += [rows_back[288:448], rows_back[448:704], rows_back[704:]]
    forth1, back1, direct[0], *chunks = after((forth1, back1, direct[0], *chunks))

    forth2, back2 = send(forth1, FORTH), send(back1, BACK)
    passed.append(send(direct[0], CORE_SWAP))
    direct.append(send(after(chunks[:1], direct[0])[0], Y_SWAP))
    done = project(inputs)
    forth2, back2, direct[1], passed[0] = after((forth2, back2, direct[1], passed[0]), done)

    forth3, back3 = send(forth2, FORTH), send(back2, BACK)
    passed.append(send(direct[1], CORE_SWAP))
    direct.append(send(after(chunks[1:2], direct[1])[0], Y_SWAP))
    done = project(forth1, back1)
    forth3, back3, direct[2], passed[1] = after((forth3, back3, direct[2], passed[1]), done)

    forth4, back4 = send(forth3[:cut], FORTH), send(back3[cut:], BACK)
    passed.append(send(direct[2], CORE_SWAP))
    direct.append(send(after(chunks[2:3], direct[2])[0], Y_SWAP))
    done2 = project(forth2, back2)
    done3 = project(forth3, back3)
    forth4, back4, direct[3], passed[2] = after((forth4, back4, direct[3], passed[2]), done2, done3)
    passed.append(send(direct[3], CORE_SWAP))
    project(forth4, back4)
    *spans, passed[3] = after((*mine, *partner, passed[3]))
    direct.append(send(after(chunks[3:4], spans[0])[0], Y_SWAP))

    tall, flat_t = ((total, WIDE), BF), ((WIDE, total), BF)
    attended, q_t, k_n = call(
        forward_kernel,
        [((16, HEAD, rows), BF), flat_t, tall],
        [info, dealt, *spans],
        smem=2,
        scratch=[
            pltpu.VMEM((WIDE, total), BF),
            pltpu.VMEM((total, WIDE), BF),
            pltpu.VMEM((HEAD + 16, total), BF),
            pltpu.VMEM((1, total), F32),
            pltpu.SMEM((total // SPAN,), jnp.int32),
        ],
        cost=(2 * total * total * 256, 3 * total * 160, total * total // 2),
    )
    attended, direct[4] = after((attended, direct[4]))
    passed.append(send(direct[4], CORE_SWAP))
    direct_back = [send(after(chunks[4:5], direct[4])[0], Y_SWAP)]
    attn_in = gathered[-1]
    attn_in_partner, cot_partner = (send(value, CORE_SWAP) for value in after((attn_in, cot), attended))
    attn_t = lax.all_to_all(attended, "ctx", 0, 0).reshape(width, rows)
    k_t, q_n, v_n = call(
        turn_kernel,
        [((HEAD, total), BF), tall, tall],
        [info, dealt, *after(spans, attended)],
        smem=2,
        cost=(0, 6 * total * 256, 0),
    )
    attn_t, passed[4], attn_in_partner, cot_partner, direct_back[0] = after(
        (attn_t, passed[4], attn_in_partner, cot_partner, direct_back[0]), k_t
    )
    direct_back.append(send(after(chunks[5:6], attn_t)[0], Y_SWAP))
    whole_scratch = [pltpu.VMEM((width, width), BF)] * 3 + [pltpu.VMEM((16, width), F32)]
    wide, low = ((rows, width), F32), ((rows, width), BF)
    result, grad_mid, grad_attended_t, packed, rights = call(
        functools.partial(mlp_kernel, 5),
        [low, wide, ((width, rows), BF), ((3, rows, width), BF), low],
        [info, inputs, cot, attn_t, own, other, w_output, w_expand, w_contract, *direct, *passed],
        smem=1,
        anys=range(6, 19),
        scratch=whole_scratch + [pltpu.VMEM((2, rows, width), BF), pltpu.SemaphoreType.DMA((24,))],
        cost=(12 * rows * width * width, 6 * width * width, 0),
    )
    grad_attended_t, packed, direct_back[1] = after((grad_attended_t, packed, direct_back[1]))
    grad_out = lax.all_to_all(grad_attended_t.reshape(16, HEAD, rows), "ctx", 0, 0)
    packed_partner = send(packed, CORE_SWAP)
    direct_back.append(send(after(chunks[6:7], packed)[0], Y_SWAP))
    attn_t_partner = send(attn_t, CORE_SWAP)

    half_width = width // 2
    terms = call(
        outer_kernel,
        [((half_width, half_width), BF)] * 6,
        [info, packed, rights, packed_partner, attn_t, attn_t_partner, cot, cot_partner],
        smem=1,
        scratch=[
            pltpu.VMEM((width, 2 * rows), BF),
            pltpu.VMEM((2 * rows, half_width), BF),
            pltpu.VMEM((width, half_width), BF),
        ],
        cost=(6 * rows * width * width, 6 * width * width, 0),
    )
    moves = {"y": Y_SWAP, "x": X_SWAP, "near": NEAR_SWAP, "far": FAR_SWAP}

    def travel(values, done):
        return [send(value, moves[order[done]]) for value, order in zip(values, ORDERS)]

    def halving(kept, came, done):
        size = half_width >> done
        shapes = [((size, half_width), BF)] * 6 if done < 3 else [((3 * PART, half_width), BF)] * 2
        return call(
            functools.partial(round_kernel, done),
            shapes,
            [info, *kept, *came],
            smem=1,
            cost=(0, 12 * size * half_width, 0),
        )

    came = travel(terms[3:], 0)
    kept = terms[:3]
    grad_out, direct_back[2] = after((grad_out, direct_back[2]), kept[0])
    direct_back.append(send(after(chunks[7:], kept[0])[0], Y_SWAP))
    grads = call(
        backward_kernel,
        [((16, 3 * HEAD, rows), BF)],
        [info, dealt, q_t, k_n, k_t, q_n, v_n, attended, grad_out, scale_col],
        smem=2,
        scratch=[
            pltpu.VMEM((WIDE, total), BF),
            pltpu.VMEM((total, WIDE), BF),
            pltpu.VMEM((1, total), F32),
            pltpu.VMEM((HEAD, total), F32),
            pltpu.VMEM((BLOCK, WIDE), F32),
            pltpu.VMEM((BLOCK, WIDE), F32),
            pltpu.SMEM((total // SPAN,), jnp.int32),
        ],
        cost=(5 * total * total * 256, 6 * total * 160, total * total // 2),
    )[0]
    grads, direct_back[3], *came = after((grads, direct_back[3], *came))
    returned = lax.all_to_all(grads, "ctx", 0, 0)
    keep, away = call(
        weight_kernel,
        [((256, half_width), F32), ((256, half_width), BF)],
        [info, grads, own, other, attn_in, attn_in_partner],
        smem=1,
        anys=(4, 5),
        scratch=[
            pltpu.VMEM((3 * HEAD, total), BF),
            pltpu.VMEM((HEAD, width), F32),
            pltpu.VMEM((3 * HEAD, width), F32),
            pltpu.VMEM((total, width), BF),
            pltpu.SemaphoreType.DMA((8,)),
        ],
        cost=(2 * 240 * total * width, 2 * total * width, 0),
    )
    from_pair = send(away, Y_SWAP)
    terms = halving(kept, after(came, keep), 1)
    kept, came = terms[:3], travel(terms[3:], 1)
    keep = after((keep,), kept[0])[0]
    summed = (keep + from_pair.astype(F32)).astype(BF)
    passed_back = [send(value, CORE_SWAP) for value in after(direct_back, summed)]

    shard = ((half_width, width), F32)
    line = ((half_width,), F32)

    def stacked(values):
        stack = call(stack_kernel, [((len(values), *values[0].shape), BF)], values)[0]
        return stack, send(stack, CORE_SWAP)

    forth1, back1 = send(summed, FORTH), send(summed, BACK)
    forth2, back2 = send(forth1, FORTH), send(back1, BACK)
    terms = halving(kept, after(came, forth1), 2)
    kept, came = terms[:3], travel(terms[3:], 2)
    forth2, back2 = after((forth2, back2), kept[0], returned, *passed_back)
    forth3, back3 = send(forth2, FORTH), send(back2, BACK)
    near, near_partner = stacked([summed, forth1, back1, forth2, back2])
    terms = halving(kept, came, 3)
    far = send(terms[1], FAR_SWAP)
    forth3, back3, near_partner = after((forth3, back3, near_partner), terms[0])
    last = [send(forth3[:128], FORTH), send(back3[128:], BACK)]
    beyond = [send(value, CORE_SWAP) for value in (forth3, back3)]
    piece = (terms[0].astype(F32) + far.astype(F32)).astype(BF)
    *last, piece = after((*last, piece), *beyond)
    query_pieces = [near, near_partner, forth3, back3, *last, *beyond, *(send(value, CORE_SWAP) for value in last)]

    forth1, back1 = send(piece, FORTH), send(piece, BACK)
    grad_query, grad_key, grad_value, grad_gain_attn, grad_scale = call(
        finish_kernel,
        [shard] * 3 + [line, ((1, HEAD), F32)],
        [info, *query_pieces, w_query, w_key, w_value, gain_attn[None], factor],
        smem=1,
        anys=range(11, 14),
        out_anys=range(3),
        scratch=[
            pltpu.VMEM((3, width, half_width), BF),
            pltpu.VMEM((3, half_width, width), BF),
            pltpu.VMEM((2, 256, half_width), BF),
            pltpu.VMEM((3, half_width, width), F32),
            pltpu.SemaphoreType.DMA((6,)),
        ],
        cost=(6 * 640 * 640 * 1280, 3 * 640 * 1280 * 4, 0),
    )
    forth1, back1 = after((forth1, back1), grad_query)
    forth2, back2 = send(forth1, FORTH), send(back1, BACK)
    grad_inputs = call(
        functools.partial(input_kernel, 4),
        [low],
        [info, inputs, returned, grad_mid, own, other, w_query, w_key, w_value, *direct_back, *passed_back],
        smem=1,
        anys=range(6, 17),
        scratch=whole_scratch + [pltpu.SemaphoreType.DMA((24,))],
        cost=(6 * rows * width * width, 6 * width * width, 0),
    )[0]
    forth2, back2 = after((forth2, back2), grad_inputs)
    forth3, back3 = send(forth2, FORTH), send(back2, BACK)
    near, near_partner = stacked([piece, forth1, back1, forth2, back2])
    forth3, back3, near_partner = after((forth3, back3, near_partner))
    last = [send(forth3[:112], FORTH), send(back3[112:], BACK)]
    beyond = [send(value, CORE_SWAP) for value in (forth3, back3)]
    partial_out = call(
        spread_kernel,
        [((half_width, 128), F32), shard, shard, shard],
        [info, near, near_partner, w_expand],
        smem=1,
        out_anys=(1, 2, 3),
        scratch=[pltpu.VMEM((30, PART, half_width), F32), pltpu.SemaphoreType.DMA((30,))],
        cost=(0, 3 * 640 * 1280 * 4, 0),
    )
    last = after(last, partial_out[0], *beyond)
    args = [info, forth3, back3, *last, *beyond, *(send(value, CORE_SWAP) for value in last)]
    args += [partial_out[0], gain_mlp[None], w_expand, *partial_out[1:]]
    grad_contract, grad_expand, grad_output, grad_gain_mlp = call(
        spread_last_kernel,
        [shard] * 3 + [line],
        args,
        smem=1,
        anys=range(len(args) - 3, len(args)),
        out_anys=range(3),
        aliases={len(args) - 3 + at: at for at in range(3)},
        scratch=[
            pltpu.VMEM((18, PART, half_width), F32),
            pltpu.VMEM((2, *piece.shape), BF),
            pltpu.VMEM((half_width, 128), F32),
            pltpu.SemaphoreType.DMA((18,)),
        ],
        cost=(0, 3 * 640 * 1280 * 4, 0),
    )
    return (
        result[None], grad_inputs[None], grad_gain_attn, grad_query, grad_key, grad_value, grad_output,
        grad_scale[0], grad_gain_mlp, grad_expand, grad_contract,
    )


def solution(mesh):
    in_specs = (
        P("wt", "ctx", None),
        P("wt", "ctx", None),
        P("wt", None),
        P("wt", None),
        P("wt"),
        P("wt", None),
        P("wt", None),
        P("wt", None),
        P("wt", None),
        P(),
        P("wt"),
        P("wt", None),
        P("wt", None),
    )
    out_specs = (
        P("wt", "ctx", None),
        P("wt", "ctx", None),
        P("wt"),
        P("wt", None),
        P("wt", None),
        P("wt", None),
        P("wt", None),
        P(),
        P("wt"),
        P("wt", None),
        P("wt", None),
    )
    body = ring_device if mesh.shape["ctx"] == HEADS and mesh.shape["wt"] == 2 else per_device
    return jax.shard_map(
        body, mesh=mesh, in_specs=in_specs, out_specs=out_specs, check_vma=False
    )
```

```python
import functools
import math

import jax
import jax.numpy as jnp
import numpy as np
from jax import lax
from jax.experimental import pallas as pl
from jax.experimental.pallas import tpu as pltpu
from jax.sharding import PartitionSpec as P

HEADS = 16
HEAD = 80
SPAN = 128
LONGEST = 4096


EPS = 1e-06
LOG2E = 1.442695041
NEG = -1e30


def normed(values, gain):
    return values * lax.rsqrt(jnp.mean(values * values, axis=-1, keepdims=True) + EPS) * gain


def locate(dealt_spans, seq_lengths, offset, count, slot_tokens):
    row_ids = offset + jnp.arange(count, dtype=jnp.int32)
    slot_ids = row_ids // SPAN
    matches = slot_ids[:, None] == jnp.arange(dealt_spans.shape[0], dtype=jnp.int32)[None, :]
    span_ids = jnp.sum(jnp.where(matches, dealt_spans[None, :], 0), axis=1)
    natural = span_ids * SPAN + row_ids % SPAN
    sequence = natural // slot_tokens
    position = natural % slot_tokens
    owners = sequence[:, None] == jnp.arange(seq_lengths.shape[0], dtype=jnp.int32)[None, :]
    limits = jnp.sum(jnp.where(owners, seq_lengths[None, :], 0), axis=1)
    return (sequence, position, position < limits)


def permitted(query_place, key_place):
    same_seq = query_place[0][:, None] == key_place[0][None, :]
    causal = key_place[1][None, :] <= query_place[1][:, None]
    return (same_seq & causal & key_place[2][None, :])[None]


def per_device(
    tokens,
    cotangent,
    deal,
    lengths,
    gain_attn,
    w_query,
    w_key,
    w_value,
    w_output,
    query_scale,
    gain_mlp,
    w_expand,
    w_contract,
):
    row_count = tokens.shape[1]
    feat_width = tokens.shape[2]
    group_rows = row_count * lax.axis_size("ctx")
    slot_tokens = min(LONGEST, group_rows)
    block_rows = min(512, group_rows)
    blocks = group_rows // block_rows
    dealt_spans = deal[0]
    seq_lengths = lengths[0]
    inputs = tokens[0].astype(jnp.float32)
    shards = (gain_attn, w_query, w_key, w_value, w_output, gain_mlp, w_expand, w_contract)
    gathered = (
        lax.all_gather(shards[0], "wt", axis=0, tiled=True),
        lax.all_gather(shards[1], "wt", axis=0, tiled=True),
        lax.all_gather(shards[2], "wt", axis=0, tiled=True),
        lax.all_gather(shards[3], "wt", axis=0, tiled=True),
        lax.all_gather(shards[4], "wt", axis=0, tiled=True),
        lax.all_gather(shards[5], "wt", axis=0, tiled=True),
        lax.all_gather(shards[6], "wt", axis=0, tiled=True),
        lax.all_gather(shards[7], "wt", axis=0, tiled=True),
    )
    gain_one = gathered[0].astype(jnp.float32)
    gain_two = gathered[5].astype(jnp.float32)
    query_place = locate(
        dealt_spans, seq_lengths, lax.axis_index("ctx") * row_count, row_count, slot_tokens
    )
    scale_row = LOG2E / math.sqrt(HEAD) * jax.nn.softplus(query_scale)
    attn_in = normed(inputs, gain_one).astype(jnp.bfloat16)
    query_lin = jnp.dot(attn_in, gathered[1], preferred_element_type=jnp.float32)
    queries = (query_lin.reshape(row_count, HEADS, HEAD) * scale_row).astype(jnp.bfloat16)
    key_own = jnp.dot(attn_in, gathered[2], preferred_element_type=jnp.float32).astype(jnp.bfloat16)
    value_own = jnp.dot(attn_in, gathered[3], preferred_element_type=jnp.float32).astype(
        jnp.bfloat16
    )
    portion = (
        lax.all_gather(key_own, "ctx", axis=0, tiled=True),
        lax.all_gather(value_own, "ctx", axis=0, tiled=True),
    )
    running = jnp.full((HEADS, row_count), NEG, jnp.float32)
    count = portion[0].shape[0]
    key_rows = portion[0].reshape(count, HEADS, HEAD)
    value_rows = portion[1].reshape(count, HEADS, HEAD)
    permit_mask = permitted(
        query_place, locate(dealt_spans, seq_lengths, jnp.int32(0), count, slot_tokens)
    )
    scores = jnp.einsum("qhd,khd->hqk", queries, key_rows, preferred_element_type=jnp.float32)
    scores = jnp.where(permit_mask, scores, NEG)
    newest = jnp.maximum(running, jnp.max(scores, axis=-1))
    weights = jnp.where(permit_mask, jnp.exp(scores - newest[..., None]), 0.0)
    running_total = jnp.sum(weights, axis=-1)
    update = jnp.einsum(
        "hqk,khd->qhd", weights.astype(jnp.bfloat16), value_rows, preferred_element_type=jnp.float32
    )
    summed = update
    running, running_total, summed = (newest, running_total, summed)
    log_norm = running + jnp.log(running_total)
    attended = summed / jnp.transpose(running_total)[:, :, None]
    attn_out = attended.reshape(row_count, feat_width).astype(jnp.bfloat16)
    mid = inputs + jnp.dot(attn_out, gathered[4], preferred_element_type=jnp.float32)
    mlp_in = normed(mid, gain_two).astype(jnp.bfloat16)
    expanded = jnp.dot(mlp_in, gathered[6], preferred_element_type=jnp.float32)
    activated = jax.nn.silu(expanded).astype(jnp.bfloat16)
    result = mid + jnp.dot(activated, gathered[7], preferred_element_type=jnp.float32)
    weights_back = (
        lax.all_gather(shards[0], "wt", axis=0, tiled=True),
        lax.all_gather(shards[1], "wt", axis=0, tiled=True),
        lax.all_gather(shards[2], "wt", axis=0, tiled=True),
        lax.all_gather(shards[3], "wt", axis=0, tiled=True),
        lax.all_gather(shards[4], "wt", axis=0, tiled=True),
        lax.all_gather(shards[5], "wt", axis=0, tiled=True),
        lax.all_gather(shards[6], "wt", axis=0, tiled=True),
        lax.all_gather(shards[7], "wt", axis=0, tiled=True),
    )
    whole_keys, whole_values = (
        lax.all_gather(key_own, "ctx", axis=0, tiled=True),
        lax.all_gather(value_own, "ctx", axis=0, tiled=True),
    )
    grad_result = cotangent[0].astype(jnp.float32)
    grad_branch = grad_result.astype(jnp.bfloat16)
    grad_contract = jnp.einsum(
        "tf,td->fd", activated, grad_branch, preferred_element_type=jnp.float32
    )
    grad_act = jnp.einsum(
        "td,fd->tf", grad_branch, weights_back[7], preferred_element_type=jnp.float32
    )
    sigmoid_gate = jax.nn.sigmoid(expanded)
    grad_expanded = (grad_act * sigmoid_gate * (1.0 + expanded * (1.0 - sigmoid_gate))).astype(
        jnp.bfloat16
    )
    grad_expand = jnp.einsum("td,tf->df", mlp_in, grad_expanded, preferred_element_type=jnp.float32)
    grad_mlp_in = jnp.einsum(
        "tf,df->td", grad_expanded, weights_back[6], preferred_element_type=jnp.float32
    )
    unused_two, pull_two = jax.vjp(normed, mid, gain_two)
    grad_mid_norm, grad_gain_two = pull_two(grad_mlp_in)
    grad_mid = grad_result + grad_mid_norm
    grad_mid_low = grad_mid.astype(jnp.bfloat16)
    grad_output_w = jnp.einsum(
        "td,te->de", attn_out, grad_mid_low, preferred_element_type=jnp.float32
    )
    grad_attended = jnp.einsum(
        "te,de->td", grad_mid_low, weights_back[4], preferred_element_type=jnp.float32
    ).astype(jnp.bfloat16)
    out_grad = grad_attended.reshape(row_count, HEADS, HEAD)
    delta = jnp.transpose(jnp.sum(out_grad.astype(jnp.float32) * attended, axis=-1))
    key_blocks = (
        jnp.arange(blocks, dtype=jnp.int32),
        whole_keys.reshape(blocks, block_rows, feat_width),
        whole_values.reshape(blocks, block_rows, feat_width),
    )
    query_zero = jnp.zeros((row_count, HEADS, HEAD), jnp.float32)

    def back_block(query_grad, block_in):
        offset = block_in[0] * block_rows
        key_rows = block_in[1].reshape(block_rows, HEADS, HEAD)
        value_rows = block_in[2].reshape(block_rows, HEADS, HEAD)
        permit_mask = permitted(
            query_place, locate(dealt_spans, seq_lengths, offset, block_rows, slot_tokens)
        )
        scores = jnp.einsum("qhd,khd->hqk", queries, key_rows, preferred_element_type=jnp.float32)
        probabilities = jnp.where(permit_mask, jnp.exp(scores - log_norm[..., None]), 0.0)
        value_grad = jnp.einsum(
            "hqk,qhd->khd",
            probabilities.astype(jnp.bfloat16),
            out_grad,
            preferred_element_type=jnp.float32,
        )
        prob_grad = jnp.einsum(
            "qhd,khd->hqk", out_grad, value_rows, preferred_element_type=jnp.float32
        )
        score_grad = (probabilities * (prob_grad - delta[..., None])).astype(jnp.bfloat16)
        query_grad = query_grad + jnp.einsum(
            "hqk,khd->qhd", score_grad, key_rows, preferred_element_type=jnp.float32
        )
        key_grad = jnp.einsum(
            "hqk,qhd->khd", score_grad, queries, preferred_element_type=jnp.float32
        )
        return (
            query_grad,
            (key_grad.reshape(block_rows, feat_width), value_grad.reshape(block_rows, feat_width)),
        )

    query_grad, key_terms = lax.scan(back_block, query_zero, key_blocks)
    key_sum, value_sum = (
        lax.psum_scatter(
            key_terms[0].reshape(group_rows, feat_width).astype(jnp.bfloat16),
            "ctx",
            scatter_dimension=0,
            tiled=True,
        ).astype(jnp.float32),
        lax.psum_scatter(
            key_terms[1].reshape(group_rows, feat_width).astype(jnp.bfloat16),
            "ctx",
            scatter_dimension=0,
            tiled=True,
        ).astype(jnp.float32),
    )
    grad_keys = key_sum.astype(jnp.bfloat16)
    grad_values = value_sum.astype(jnp.bfloat16)
    grad_query_lin = (query_grad * scale_row).reshape(row_count, feat_width).astype(jnp.bfloat16)
    grad_scale = (
        jnp.sum(query_grad * query_lin.reshape(row_count, HEADS, HEAD), axis=(0, 1))
        * (LOG2E / math.sqrt(HEAD))
        * jax.nn.sigmoid(query_scale)
    )
    grad_query_w = jnp.einsum(
        "td,te->de", attn_in, grad_query_lin, preferred_element_type=jnp.float32
    )
    grad_key_w = jnp.einsum("td,te->de", attn_in, grad_keys, preferred_element_type=jnp.float32)
    grad_value_w = jnp.einsum("td,te->de", attn_in, grad_values, preferred_element_type=jnp.float32)
    grad_attn_in = jnp.einsum(
        "te,de->td", grad_query_lin, weights_back[1], preferred_element_type=jnp.float32
    )
    grad_attn_in = grad_attn_in + jnp.einsum(
        "te,de->td", grad_keys, weights_back[2], preferred_element_type=jnp.float32
    )
    grad_attn_in = grad_attn_in + jnp.einsum(
        "te,de->td", grad_values, weights_back[3], preferred_element_type=jnp.float32
    )
    unused_one, pull_one = jax.vjp(normed, inputs, gain_one)
    grad_in_norm, grad_gain_one = pull_one(grad_attn_in)
    grad_inputs = (grad_mid + grad_in_norm).astype(jnp.bfloat16)
    terms = (
        grad_gain_one,
        grad_query_w,
        grad_key_w,
        grad_value_w,
        grad_output_w,
        jnp.tile(grad_scale, lax.axis_size("wt")),
        grad_gain_two,
        grad_expand,
        grad_contract,
    )
    shares = (
        lax.psum_scatter(
            terms[0].astype(jnp.bfloat16), "wt", scatter_dimension=0, tiled=True
        ).astype(jnp.float32),
        lax.psum_scatter(
            terms[1].astype(jnp.bfloat16), "wt", scatter_dimension=0, tiled=True
        ).astype(jnp.float32),
        lax.psum_scatter(
            terms[2].astype(jnp.bfloat16), "wt", scatter_dimension=0, tiled=True
        ).astype(jnp.float32),
        lax.psum_scatter(
            terms[3].astype(jnp.bfloat16), "wt", scatter_dimension=0, tiled=True
        ).astype(jnp.float32),
        lax.psum_scatter(
            terms[4].astype(jnp.bfloat16), "wt", scatter_dimension=0, tiled=True
        ).astype(jnp.float32),
        lax.psum_scatter(
            terms[5].astype(jnp.bfloat16), "wt", scatter_dimension=0, tiled=True
        ).astype(jnp.float32),
        lax.psum_scatter(
            terms[6].astype(jnp.bfloat16), "wt", scatter_dimension=0, tiled=True
        ).astype(jnp.float32),
        lax.psum_scatter(
            terms[7].astype(jnp.bfloat16), "wt", scatter_dimension=0, tiled=True
        ).astype(jnp.float32),
        lax.psum_scatter(
            terms[8].astype(jnp.bfloat16), "wt", scatter_dimension=0, tiled=True
        ).astype(jnp.float32),
    )
    totals = (
        lax.psum(shares[0].astype(jnp.bfloat16), "ctx").astype(jnp.float32),
        lax.psum(shares[1].astype(jnp.bfloat16), "ctx").astype(jnp.float32),
        lax.psum(shares[2].astype(jnp.bfloat16), "ctx").astype(jnp.float32),
        lax.psum(shares[3].astype(jnp.bfloat16), "ctx").astype(jnp.float32),
        lax.psum(shares[4].astype(jnp.bfloat16), "ctx").astype(jnp.float32),
        lax.psum(shares[5].astype(jnp.bfloat16), "ctx").astype(jnp.float32),
        lax.psum(shares[6].astype(jnp.bfloat16), "ctx").astype(jnp.float32),
        lax.psum(shares[7].astype(jnp.bfloat16), "ctx").astype(jnp.float32),
        lax.psum(shares[8].astype(jnp.bfloat16), "ctx").astype(jnp.float32),
    )
    return (
        result.astype(jnp.bfloat16)[None],
        grad_inputs[None],
        totals[0],
        totals[1],
        totals[2],
        totals[3],
        totals[4],
        totals[5],
        totals[6],
        totals[7],
        totals[8],
    )


BF = jnp.bfloat16
F32 = jnp.float32
NN = (((1,), (0,)), ((), ()))
NT = (((1,), (1,)), ((), ()))
AXES = ("ctx", "wt")
LIMIT = 56 * 1024 * 1024

RING = ((0, 0), (1, 0), (2, 0), (3, 0), (3, 1), (2, 1), (1, 1), (0, 1))
PLACE = {chip: at for at, chip in enumerate(RING)}
OFFSETS = (0, -1, 1, -2, 2, -3, 3, 4)


def flat(z, x, core, y):
    return ((z * 2 + x) * 2 + core) * 2 + y


def pairs(move):
    return [
        (flat(z, x, core, y), flat(*move(z, x, core, y)))
        for z in range(4)
        for x in range(2)
        for core in range(2)
        for y in range(2)
    ]


def turned(by):
    def move(z, x, core, y):
        return (*RING[(PLACE[(z, x)] + by) % 8], core, y)

    return move


CORE_SWAP = pairs(lambda z, x, core, y: (z, x, 1 - core, y))
Y_SWAP = pairs(lambda z, x, core, y: (z, x, core, 1 - y))
X_SWAP = pairs(lambda z, x, core, y: (z, 1 - x, core, y))
NEAR_SWAP = pairs(lambda z, x, core, y: (z ^ 1, x, core, y))
FAR_SWAP = pairs(lambda z, x, core, y: (z ^ 2, x, core, y))
FORTH = pairs(turned(1))
BACK = pairs(turned(-1))


def slot_table():
    rows = []
    for c in range(16):
        z, x, core = c // 4, (c // 2) % 2, c % 2
        chips = [RING[(PLACE[(z, x)] + by) % 8] for by in OFFSETS]
        own = [(a * 2 + b) * 2 + core for a, b in chips]
        rows.append(own + [dev ^ 1 for dev in own])
    return np.asarray(rows, np.int32)


def send(value, moves):
    return lax.ppermute(value, AXES, moves)


def mm(left, right, dims=NN):
    return lax.dot_general(left, right, dims, preferred_element_type=F32)


def call(body, outs, args, smem=0, anys=(), scratch=(), cost=None, out_anys=(), aliases=None):
    whole, anywhere = pl.BlockSpec(memory_space=pltpu.VMEM), pl.BlockSpec(memory_space=pl.ANY)
    specs = [pl.BlockSpec(memory_space=pltpu.SMEM)] * smem
    specs += [anywhere if at in anys else whole for at in range(smem, len(args))]
    estimate = None
    if cost is not None:
        estimate = pl.CostEstimate(flops=int(cost[0]), bytes_accessed=int(cost[1]), transcendentals=int(cost[2]))
    return pl.pallas_call(
        body,
        out_shape=[jax.ShapeDtypeStruct(shape, kind) for shape, kind in outs],
        in_specs=specs,
        out_specs=[anywhere if at in out_anys else whole for at in range(len(outs))],
        scratch_shapes=list(scratch),
        input_output_aliases=aliases or {},
        cost_estimate=estimate,
        compiler_params=pltpu.CompilerParams(vmem_limit_bytes=LIMIT),
    )(*args)


def half(y, width=640):
    return pl.ds(pl.multiple_of(y * width, 128), width)


def pick_kernel(info, wq, wk, wv, gain_a, gain_m, out):
    chip = info[2]
    cols = lax.broadcasted_iota(jnp.int32, (2 * HEAD, wq.shape[1]), 1)
    rows = lax.broadcasted_iota(jnp.int32, (2 * HEAD, wq.shape[1]), 0)
    chosen = jnp.where(cols == rows + chip * (2 * HEAD), 1.0, 0.0).astype(BF)
    for at, ref in enumerate((wq, wk, wv)):
        both = mm(chosen, ref[...], NT).astype(BF)
        out[at * HEAD : (at + 1) * HEAD] = both[:HEAD]
        out[3 * HEAD + at * HEAD : 3 * HEAD + (at + 1) * HEAD] = both[HEAD:]
    line = lax.broadcasted_iota(jnp.int32, (16, gain_a.shape[1]), 0)
    tail = jnp.where(line == 0, gain_a[...].astype(F32), 0.0)
    tail = jnp.where(line == 1, gain_m[...].astype(F32), tail)
    out[6 * HEAD :] = tail.astype(BF)


def project_kernel(count, start, info, *refs):
    xs = refs[:count]
    own, other, scale = refs[count : count + 3]
    whole, mine, partner, attn_in, weight, gain, lines, sem = refs[-8:]
    y, core = info[0], info[1]
    weight[:, half(y)] = own[: 6 * HEAD]
    weight[:, half(1 - y)] = other[: 6 * HEAD]
    gain[:, half(y)] = own[6 * HEAD :].astype(F32)
    gain[:, half(1 - y)] = other[6 * HEAD :].astype(F32)
    row = 0
    for ref in xs:
        values = ref[...].astype(F32)
        scaled = values * lax.rsqrt(jnp.mean(values * values, axis=-1, keepdims=True) + EPS)
        attn_in[row : row + ref.shape[0]] = (scaled * gain[0:1]).astype(BF)
        row += ref.shape[0]
    copy = pltpu.make_async_copy(attn_in, whole.at[pl.ds(start, row)], sem)
    copy.start()
    lin = mm(weight[...], attn_in[...], NT)
    for head in range(2):
        base = head * 3 * HEAD
        lines[base : base + HEAD] = (lin[base : base + HEAD] * scale[...]).astype(BF)
        lines[base + HEAD : base + 3 * HEAD] = lin[base + HEAD : base + 3 * HEAD].astype(BF)
    mine[...] = lines[pl.ds(pl.multiple_of(core * 3 * HEAD, 16), 3 * HEAD)]
    partner[...] = lines[pl.ds(pl.multiple_of((1 - core) * 3 * HEAD, 16), 3 * HEAD)]
    copy.wait()


def span_slots(pieces):
    return [(ref, col) for ref in pieces for col in range(0, ref.shape[1], SPAN)]


def natural_span(info, deal, slot):
    return deal[2 * info[4 + slot // 2] + slot % 2]


def at_span(span):
    return pl.ds(pl.multiple_of(span * SPAN, SPAN), SPAN)


BLOCK = 1024
WIDE = 128


def block_at(at):
    return pl.ds(pl.multiple_of(at * BLOCK, BLOCK), BLOCK)


def in_parts(line):
    high = line.astype(BF)
    rest = line - high.astype(F32)
    middle = rest.astype(BF)
    low = (rest - middle.astype(F32)).astype(BF)
    at = lax.broadcasted_iota(jnp.int32, (16, line.shape[1]), 0)
    rows = jnp.where(at == 0, high.astype(F32), 0.0)
    rows = jnp.where(at == 1, middle.astype(F32), rows)
    return jnp.where(at == 2, low.astype(F32), rows).astype(BF)


def ones_behind(ref):
    at = lax.broadcasted_iota(jnp.int32, ref.shape, 1)
    ref[...] = jnp.where((at >= HEAD) & (at < HEAD + 3), 1.0, 0.0).astype(BF)


def forward_kernel(info, deal, *refs):
    pieces = refs[:10]
    out, queries, keys, values, lse, dealt = refs[10:]
    total = queries.shape[1]
    length = info[3]
    spans = total // SPAN
    blocks = total // BLOCK

    @pl.loop(0, spans)
    def _(at):
        dealt[deal[at]] = at

    line = lax.broadcasted_iota(jnp.int32, (16, total), 0)
    values[HEAD:] = jnp.where(line == 0, 1.0, 0.0).astype(BF)
    queries[HEAD:] = jnp.zeros((WIDE - HEAD, total), BF)
    ones_behind(keys)
    longest = jnp.zeros((1, SPAN), F32)
    for slot, (ref, col) in enumerate(span_slots(pieces)):
        where = at_span(natural_span(info, deal, slot))
        key = ref[HEAD : 2 * HEAD, col : col + SPAN]
        queries[:HEAD, where] = ref[:HEAD, col : col + SPAN]
        keys[where, :HEAD] = key.T
        values[:HEAD, where] = ref[2 * HEAD :, col : col + SPAN]
        sizes = key.astype(F32)
        longest = jnp.maximum(longest, jnp.sum(sizes * sizes, axis=0, keepdims=True))
    longest = jnp.max(longest, axis=1, keepdims=True)

    key_at = lax.broadcasted_iota(jnp.int32, (BLOCK, BLOCK), 0)
    query_at = lax.broadcasted_iota(jnp.int32, (BLOCK, BLOCK), 1)

    def scores_of(masked, i, j):
        scores = mm(keys[block_at(j), :], queries[:, block_at(i)])
        if masked:
            key_pos = j * BLOCK + key_at
            allowed = (key_pos <= i * BLOCK + query_at) & (key_pos < length)
            scores = jnp.where(allowed, scores, NEG)
        return scores

    def finish(i, peak, acc):
        here = block_at(i)
        norm = acc[HEAD : HEAD + 1]
        lse[:, here] = peak + jnp.log(norm)
        attended = (acc[:HEAD] / norm).astype(BF)
        for part in range(BLOCK // SPAN):
            row = dealt[i * (BLOCK // SPAN) + part]
            out[row // 2, :, at_span(row % 2)] = attended[:, part * SPAN : (part + 1) * SPAN]
        return jnp.min(norm)

    def bounded(i, least):
        here = block_at(i)
        query = queries[:HEAD, here].astype(F32)
        bound = jnp.sqrt(jnp.sum(query * query, axis=0, keepdims=True) * longest) - 40.0
        shift = in_parts(-bound)
        queries[HEAD : HEAD + 16, here] = shift

        def step(masked, j, acc):
            weights = jnp.exp(scores_of(masked, i, j)).astype(BF)
            return acc + mm(values[:, block_at(j)], weights)

        split = jnp.minimum(i, length // BLOCK)
        acc = lax.fori_loop(0, split, functools.partial(step, False), jnp.zeros((HEAD + 16, BLOCK), F32))
        acc = lax.fori_loop(split, i + 1, functools.partial(step, True), acc)
        exact = jnp.sum(shift.astype(F32), axis=0, keepdims=True)
        return jnp.minimum(least, finish(i, -exact, acc))

    least = lax.fori_loop(0, blocks, bounded, jnp.float32(1.0))

    @pl.when(jnp.logical_not(least > 1e-26))
    def _():
        queries[HEAD:] = jnp.zeros((WIDE - HEAD, total), BF)

        @pl.loop(0, blocks)
        def _(i):
            def step(j, carry):
                peak, acc = carry
                scores = scores_of(True, i, j)
                newest = jnp.maximum(peak, jnp.max(scores, axis=0, keepdims=True))
                weights = jnp.exp(scores - newest).astype(BF)
                return newest, acc * jnp.exp(peak - newest) + mm(values[:, block_at(j)], weights)

            start = (jnp.full((1, BLOCK), NEG, F32), jnp.zeros((HEAD + 16, BLOCK), F32))
            finish(i, *lax.fori_loop(0, i + 1, step, start))

    queries[HEAD : HEAD + 16] = in_parts(-lse[...])


def turn_kernel(info, deal, *refs):
    pieces, (k_t, q_n, v_n) = refs[:10], refs[10:]
    q_n[...] = jnp.zeros_like(q_n)
    ones_behind(v_n)
    for slot, (ref, col) in enumerate(span_slots(pieces)):
        where = at_span(natural_span(info, deal, slot))
        cols = slice(col, col + SPAN)
        k_t[:, where] = ref[HEAD : 2 * HEAD, cols]
        q_n[where, :HEAD] = ref[:HEAD, cols].T
        v_n[where, :HEAD] = ref[2 * HEAD :, cols].T


def backward_kernel(info, deal, *refs):
    q_t, k_n, k_t, q_n, v_n, attended, grad_out, scale, out, g_t, g_n, delta, dq_t, dk, dv, dealt = refs
    total = q_t.shape[1]
    length = info[3]
    spans = total // SPAN
    blocks = total // BLOCK

    @pl.loop(0, spans)
    def _(at):
        dealt[deal[at]] = at

    g_n[...] = jnp.zeros_like(g_n)
    g_t[HEAD:] = jnp.zeros((WIDE - HEAD, total), BF)
    for row in range(spans):
        where = at_span(deal[row])
        cols = slice(row % 2 * SPAN, row % 2 * SPAN + SPAN)
        grad = grad_out[row // 2, :, cols]
        g_t[:HEAD, where] = grad
        g_n[where, :HEAD] = grad.T
        product = grad.astype(F32) * attended[row // 2, :, cols].astype(F32)
        delta[:, where] = jnp.sum(product, axis=0, keepdims=True)
    g_t[HEAD : HEAD + 16] = in_parts(-delta[...])
    dq_t[...] = jnp.zeros_like(dq_t)

    key_at = lax.broadcasted_iota(jnp.int32, (BLOCK, BLOCK), 0)
    query_at = lax.broadcasted_iota(jnp.int32, (BLOCK, BLOCK), 1)

    @pl.loop(0, blocks)
    def _(j):
        there = block_at(j)
        dk[...] = jnp.zeros_like(dk)
        dv[...] = jnp.zeros_like(dv)

        def step(masked, i, carry):
            here = block_at(i)
            probs = jnp.exp(mm(k_n[there, :], q_t[:, here]))
            if masked:
                key_pos = j * BLOCK + key_at
                allowed = (key_pos <= i * BLOCK + query_at) & (key_pos < length)
                probs = jnp.where(allowed, probs, 0.0)
            probs = probs.astype(BF)
            grad_scores = probs * mm(v_n[there, :], g_t[:, here]).astype(BF)
            dv[...] += mm(probs, g_n[here, :])
            dk[...] += mm(grad_scores, q_n[here, :])
            dq_t[:, here] += mm(k_t[:, there], grad_scores)
            return carry

        split = jnp.where((j + 1) * BLOCK <= length, j + 1, blocks)
        lax.fori_loop(j, split, functools.partial(step, True), 0)
        lax.fori_loop(split, blocks, functools.partial(step, False), 0)
        for part in range(BLOCK // SPAN):
            row = dealt[j * (BLOCK // SPAN) + part]
            rows = slice(part * SPAN, (part + 1) * SPAN)
            out[row // 2, HEAD : 2 * HEAD, at_span(row % 2)] = dk[rows].T[:HEAD].astype(BF)
            out[row // 2, 2 * HEAD :, at_span(row % 2)] = dv[rows].T[:HEAD].astype(BF)

    for row in range(spans):
        cols = slice(row % 2 * SPAN, row % 2 * SPAN + SPAN)
        out[row // 2, :HEAD, cols] = (dq_t[:, at_span(deal[row])] * scale[...]).astype(BF)


def load_weights(info, own, direct, passed, wholes, sems):
    y, core = info[0], info[1]
    started = []
    count = 0
    for at, whole in enumerate(wholes):
        rows, part = own[at].shape[0], own[at].shape[0] // 2
        far = (1 - y) * rows
        places = [(own[at], y * rows)]
        for chunks, base in ((direct, far + core * part), (passed, far + (1 - core) * part)):
            start = 0
            for chunk in chunks:
                low, high = max(start, at * part), min(start + chunk.shape[0], at * part + part)
                if low < high:
                    places.append((chunk.at[pl.ds(low - start, high - low)], base + low - at * part))
                start += chunk.shape[0]
        copies = []
        for ref, start in places:
            target = whole.at[pl.ds(pl.multiple_of(start, 16), ref.shape[0])]
            copies.append(pltpu.make_async_copy(ref, target, sems.at[count]))
            copies[-1].start()
            count += 1
        started.append(copies)
    return started


def arrive(copies):
    for copy in copies:
        copy.wait()


def mlp_kernel(chunks, info, tokens, cotangent, attn_t, own, other, *refs):
    shards, direct, passed = refs[:3], refs[3 : 3 + chunks], refs[3 + chunks : 3 + 2 * chunks]
    refs = refs[3 + 2 * chunks :]
    outs = refs[:5]
    w_output, w_expand, w_contract, gain, right, sems = refs[5:]
    result, grad_mid_out, grad_attended_t, away, rights = outs
    y, core = info[0], info[1]
    loads = load_weights(info, shards, direct, passed, (w_output, w_expand, w_contract), sems)
    gain[:, half(y)] = own[6 * HEAD :].astype(F32)
    gain[:, half(1 - y)] = other[6 * HEAD :].astype(F32)
    gains = gain[1:2]
    attn = attn_t[...].T
    arrive(loads[0])
    mid = tokens[...].astype(F32) + mm(attn, w_output[...])
    rate = lax.rsqrt(jnp.mean(mid * mid, axis=-1, keepdims=True) + EPS)
    mlp_in = (mid * rate * gains).astype(BF)
    away[1] = mlp_in
    arrive(loads[1])
    expanded = mm(mlp_in, w_expand[...])
    gate = jax.nn.sigmoid(expanded)
    act = (expanded * gate).astype(BF)
    away[0] = act
    arrive(loads[2])
    result[...] = (mid + mm(act, w_contract[...])).astype(BF)
    grad_act = mm(cotangent[...], w_contract[...], NT)
    grad_expanded = (grad_act * gate * (1.0 + expanded * (1.0 - gate))).astype(BF)
    right[0] = grad_expanded
    grad_mlp_in = mm(grad_expanded, w_expand[...], NT) * gains
    inner = jnp.mean(grad_mlp_in * mid, axis=-1, keepdims=True)
    grad_mid = cotangent[...].astype(F32) + rate * grad_mlp_in - mid * (rate * rate * rate * inner)
    grad_mid_out[...] = grad_mid
    low = grad_mid.astype(BF)
    right[1] = low
    grad_attended_t[...] = mm(w_output[...], low, NT).astype(BF)
    for at in range(2):
        rights[:, at * 640 : at * 640 + 640] = right[at, :, half(core)]
        away[2, :, at * 640 : at * 640 + 640] = right[at, :, half(1 - core)]


BITS = ("y", "x", "far", "near")
ORDERS = (("y", "x", "near", "far"), ("x", "near", "y", "far"), ("near", "y", "x", "far"))
BIT_AT = {"y": 0, "x": 20, "near": 21, "far": 22}
PART = 80


def left_bits(order, done):
    return [name for name in BITS if name not in order[:done]]


def halves(info, order, done):
    left = left_bits(order, done)
    name = order[done]
    bit = info[BIT_AT[name]]
    stride = 1 << (len(left) - 1 - left.index(name))
    count = 1 << len(left)
    bases = [block for block in range(count) if block & stride == 0]
    return [(base + bit * stride, base + (1 - bit) * stride) for base in bases]


def rows_of(block):
    start = block * PART
    return pl.ds(start if isinstance(block, int) else pl.multiple_of(start, 16), PART)


def outer_kernel(info, own, rights, partner, attn_t, attn_t_partner, cot, cot_partner, *refs):
    outs, (left, right, full) = refs[:6], refs[6:]
    core = info[1]
    rows = cot.shape[0]
    for at in range(3):
        if at < 2:
            left[:, :rows] = own[at].T
            left[:, rows:] = partner[at].T
        else:
            left[:, :rows] = attn_t[...]
            left[:, rows:] = attn_t_partner[...]
        if at == 0:
            right[:rows] = cot[:, half(core)]
            right[rows:] = cot_partner[:, half(core)]
        else:
            cols = slice((at - 1) * 640, at * 640)
            right[:rows] = rights[:, cols]
            right[rows:] = partner[2, :, cols]
        full[...] = mm(left[...], right[...]).astype(BF)
        for to, (kept, sent) in enumerate(halves(info, ORDERS[at], 0)):
            outs[at][rows_of(to)] = full[rows_of(kept)]
            outs[3 + at][rows_of(to)] = full[rows_of(sent)]


def round_kernel(done, info, *refs):
    kept, came, outs = refs[:3], refs[3:6], refs[6:]
    for at in range(3):
        for to, (mine, theirs) in enumerate(halves(info, ORDERS[at], done)):
            if len(outs) == 6:
                stay, away, target = outs[at], outs[3 + at], rows_of(to)
            else:
                stay, away, target = outs[0], outs[1], rows_of(at)
            for out, block in ((stay, mine), (away, theirs)):
                total = kept[at][rows_of(block)].astype(F32) + came[at][rows_of(block)].astype(F32)
                out[target] = total.astype(BF)


def folded(products):
    return sum(products[:, at : at + 128] for at in range(0, products.shape[1], 128))


def row_sums(products):
    ones = jnp.ones((16, products.shape[1]), BF)
    high = products.astype(BF)
    low = (products - high.astype(F32)).astype(BF)
    return mm(ones, high, NT) + mm(ones, low, NT)


def stack_kernel(*refs):
    for at, ref in enumerate(refs[:-1]):
        refs[-1][at] = ref[...]


def joined(pieces, last):
    count = len(pieces) // 2
    ready = []
    for colour in range(2):
        group = pieces[colour * count : colour * count + count]
        cut = group[-2].shape[0]
        last[colour, :cut] = group[-2][...]
        last[colour, cut:] = group[-1][...]
        ready += [*group[:-2], last.at[colour]]
    return ready


def slot_of(at, count, first):
    return first + at if at < count else 8 + first + at - count


def scatter(info, refs, first, blocks, sems, outs, expand, sums):
    copies = []
    for at, ref in enumerate(refs):
        dev = info[4 + slot_of(at, len(refs) // 2, first)]
        block = ((dev // 2) % 2) * 4 + dev // 4
        rows = pl.ds(pl.multiple_of(block * PART, 16), PART)
        for way in range(3):
            blocks[3 * at + way] = ref[way * PART : (way + 1) * PART].astype(F32)
            target = outs[way].at[rows, half(dev % 2)]
            copies.append(pltpu.make_async_copy(blocks.at[3 * at + way], target, sems.at[3 * at + way]))
            copies[-1].start()
        sums[rows] += folded(blocks[3 * at + 1] * expand[rows, half(dev % 2)].astype(F32))
    return copies


def spread_kernel(info, near, near_partner, expand, sums, *refs):
    outs, (blocks, sems) = refs[:3], refs[3:]
    pieces = [stack.at[at] for stack in (near, near_partner) for at in range(5)]
    sums[...] = jnp.zeros_like(sums)
    arrive(scatter(info, pieces, 0, blocks, sems, outs, expand, sums))


def spread_last_kernel(info, *refs):
    pieces, (before, gain, expand), (*outs, grad_gain), refs = refs[:8], refs[8:11], refs[14:18], refs[18:]
    blocks, last, sums, sems = refs
    sums[...] = before[...]
    copies = scatter(info, joined(pieces, last), 5, blocks, sems, outs, expand, sums)
    size = sums.shape[0]
    grad_gain[...] = (row_sums(sums[...])[0:1] / gain[...].astype(F32)).reshape(size)
    arrive(copies)


def weight_kernel(info, grads, own, other, *refs):
    inputs = refs[:2]
    keep, away, lines, weight, total, gain_sums, attn_in, sems = refs[2:]
    y, core = info[0], info[1]
    rows = attn_in.shape[0] // 8
    loads = []
    for at in range(8):
        source = inputs[at // 4].at[pl.ds(at % 4 * rows, rows)]
        loads.append(pltpu.make_async_copy(source, attn_in.at[pl.ds(at * rows, rows)], sems.at[at]))
        loads[-1].start()
    for slot in range(16):
        lines[:, slot * 256 : slot * 256 + 256] = grads[info[4 + slot]]
    mine = pl.ds(pl.multiple_of(core * 3 * HEAD, 16), 3 * HEAD)
    weight[:, half(y)] = own[mine].astype(F32)
    weight[:, half(1 - y)] = other[mine].astype(F32)
    total[...] = jnp.zeros_like(total)
    for at in range(4):
        loads[2 * at].wait()
        loads[2 * at + 1].wait()
        part = slice(2 * at * rows, 2 * (at + 1) * rows)
        total[...] += mm(lines[:, part], attn_in[part])
    keep[: 3 * HEAD] = total[:, half(y)]
    away[: 3 * HEAD] = total[:, half(1 - y)].astype(BF)
    weight[...] *= total[...]
    scale_sums = row_sums(weight[:HEAD])[0:1]
    gain_sums[...] = jnp.sum(weight[...], axis=0, keepdims=True)
    line = lax.broadcasted_iota(jnp.int32, (16, keep.shape[1]), 0)
    keep[3 * HEAD :] = jnp.where(line == 1, gain_sums[:, half(y)], 0.0)
    away[3 * HEAD :] = jnp.where(line == 1, gain_sums[:, half(1 - y)], 0.0).astype(BF)
    keep[3 * HEAD : 3 * HEAD + 1, :HEAD] = scale_sums
    first = lax.broadcasted_iota(jnp.int32, (16, HEAD), 0) == 0
    behind = jnp.where(line == 1, gain_sums[:, half(1 - y)], 0.0)[:, :HEAD]
    away[3 * HEAD :, :HEAD] = jnp.where(first, scale_sums, behind).astype(BF)


def finish_kernel(info, near, near_partner, *refs):
    pieces, (gain, factor), outs, refs = refs[:8], refs[8:10], refs[10:13], refs[13:]
    grad_gain, grad_scale, stacks, last, turned, sems = refs
    extra = jnp.zeros((16, last.shape[2]), F32)
    early = [stack.at[at] for stack in (near, near_partner) for at in range(5)]
    for first, group in ((0, early), (5, joined(pieces, last))):
        for at, ref in enumerate(group):
            rows = pl.ds(pl.multiple_of(info[4 + slot_of(at, len(group) // 2, first)] * HEAD, 16), HEAD)
            for way in range(3):
                stacks[way, rows] = ref[way * HEAD : (way + 1) * HEAD]
            extra += ref[3 * HEAD :].astype(F32)
    grad_scale[...] = extra[0:1, :HEAD] * factor[...]
    size = turned.shape[1]
    grad_gain[...] = (extra[1:2] / gain[...].astype(F32)).reshape(size)
    same = lax.broadcasted_iota(jnp.int32, (size, size), 0) == lax.broadcasted_iota(jnp.int32, (size, size), 1)
    unit = jnp.where(same, 1.0, 0.0).astype(BF)
    copies = []
    for at, out in enumerate(outs):
        turned[at] = mm(unit, stacks[at], NT)
        copies.append(pltpu.make_async_copy(turned.at[at], out, sems.at[at]))
        copies[-1].start()
    arrive(copies)


def input_kernel(chunks, info, tokens, grads, grad_mid, own, other, *refs):
    shards, direct, passed = refs[:3], refs[3 : 3 + chunks], refs[3 + chunks : 3 + 2 * chunks]
    out, *weights, gain, sems = refs[3 + 2 * chunks :]
    y = info[0]
    loads = load_weights(info, shards, direct, passed, weights, sems)
    gain[:, half(y)] = own[6 * HEAD :].astype(F32)
    gain[:, half(1 - y)] = other[6 * HEAD :].astype(F32)
    heads, width = grads.shape[0], grads.shape[2]
    values = tokens[...].astype(F32)
    rate = lax.rsqrt(jnp.mean(values * values, axis=-1, keepdims=True) + EPS)
    turned_grad = None
    for at, ref in enumerate(weights):
        part = grads[:, at * HEAD : (at + 1) * HEAD, :].reshape(heads * HEAD, width)
        arrive(loads[at])
        product = mm(ref[...], part)
        turned_grad = product if turned_grad is None else turned_grad + product
    grad = turned_grad.T * gain[0:1]
    inner = jnp.mean(grad * values, axis=-1, keepdims=True)
    out[...] = (grad_mid[...] + rate * grad - values * (rate * rate * rate * inner)).astype(BF)


def after(values, *others):
    return lax.optimization_barrier((tuple(values), others))[0]


def weight_rows(shards, core):
    size = shards[0].shape[0] // 2
    return jnp.concatenate([lax.dynamic_slice_in_dim(shard, core * size, size, 0) for shard in shards], axis=0)


def ring_device(
    tokens, cotangent, deal, lengths, gain_attn, w_query, w_key, w_value, w_output, query_scale,
    gain_mlp, w_expand, w_contract
):
    rows, width = tokens.shape[1:]
    c, y = lax.axis_index("ctx"), lax.axis_index("wt")
    core, x, z = c % 2, (c // 2) % 2, c // 4
    table = lax.dynamic_index_in_dim(jnp.asarray(slot_table()), c, 0, keepdims=False)
    head = jnp.stack([y, core, c // 2, lengths[0, 0]]).astype(jnp.int32)
    info = jnp.concatenate([head, table, jnp.stack([x, z % 2, z // 2]).astype(jnp.int32)])
    dealt = deal[0]
    total = rows * 16
    softplus = jax.nn.softplus(query_scale)
    scale_col = (LOG2E / math.sqrt(HEAD) * softplus)[:, None]
    factor = (jax.nn.sigmoid(query_scale) / softplus)[None, :]
    inputs = tokens[0]
    cot = cotangent[0]
    cut = rows // 2
    mine, partner, gathered = [], [], []

    def project(other, *group):
        count = sum(part.shape[0] for part in group)
        start = sum(piece.shape[1] for piece in mine)
        args = [info, *group, own, other, scale_col]
        got = call(
            functools.partial(project_kernel, len(group), start),
            [((8 * rows, width), BF), ((3 * HEAD, count), BF), ((3 * HEAD, count), BF)],
            args + gathered[-1:],
            smem=1,
            anys=range(len(args), len(args) + 1),
            out_anys=(0,),
            aliases={len(args): 0} if gathered else None,
            scratch=[
                pltpu.VMEM((count, width), BF),
                pltpu.VMEM((6 * HEAD, width), BF),
                pltpu.VMEM((16, width), F32),
                pltpu.VMEM((6 * HEAD, count), BF),
                pltpu.SemaphoreType.DMA,
            ],
            cost=(2 * 480 * 1280 * count, 4 * 1280 * count, 0),
        )
        gathered.append(got[0])
        mine.append(got[1])
        partner.append(send(got[2], CORE_SWAP))
        return got[1]

    forth1, back1 = send(inputs, FORTH), send(inputs, BACK)
    size = width // 4
    first_rows = lax.dynamic_slice_in_dim(w_output, core * size, 128, 0)
    direct, passed = [send(first_rows, Y_SWAP)], []
    own = call(
        pick_kernel,
        [((6 * HEAD + 16, width // 2), BF)],
        [info, w_query, w_key, w_value, gain_attn[None], gain_mlp[None]],
        smem=1,
        cost=(2 * 480 * 640 * 1280, 3 * 640 * 1280 * 2, 0),
    )[0]
    other = send(own, Y_SWAP)
    forth1, back1, direct[0] = after((forth1, back1, direct[0]), own)

    forth2, back2 = send(forth1, FORTH), send(back1, BACK)
    rows_out = weight_rows(after((w_output, w_expand, w_contract), forth1), core)
    rows_back = weight_rows(after((w_query, w_key, w_value), forth1), core)
    chunks = [rows_out[128:416], rows_out[416:576], rows_out[576:]]
    chunks += [rows_back[:224], rows_back[224:384], rows_back[384:608], rows_back[608:]]
    passed.append(send(direct[0], CORE_SWAP))
    forth2, back2, other, passed[0], *chunks = after((forth2, back2, other, passed[0], *chunks))

    forth3, back3 = send(forth2, FORTH), send(back2, BACK)
    direct.append(send(after(chunks[:1], passed[0])[0], Y_SWAP))
    done = project(other, inputs)
    done = project(other, forth1, back1), done
    done = project(other, forth2, back2), done
    forth3, back3, direct[1] = after((forth3, back3, direct[1]), done)

    forth4, back4 = send(forth3[:cut], FORTH), send(back3[cut:], BACK)
    passed.append(send(direct[1], CORE_SWAP))
    direct.append(send(after(chunks[1:2], direct[1])[0], Y_SWAP))
    done = project(other, forth3, back3)
    forth4, back4, direct[2], passed[1] = after((forth4, back4, direct[2], passed[1]), done)
    passed.append(send(direct[2], CORE_SWAP))
    direct.append(send(after(chunks[2:3], direct[2])[0], Y_SWAP))
    project(other, forth4, back4)
    *spans, passed[2] = after((*mine, *partner, passed[2]))

    tall, flat_t = ((total, WIDE), BF), ((WIDE, total), BF)
    attended, q_t, k_n = call(
        forward_kernel,
        [((16, HEAD, rows), BF), flat_t, tall],
        [info, dealt, *spans],
        smem=2,
        scratch=[
            pltpu.VMEM((HEAD + 16, total), BF),
            pltpu.VMEM((1, total), F32),
            pltpu.SMEM((total // SPAN,), jnp.int32),
        ],
        cost=(2 * total * total * 256, 3 * total * 160, total * total // 2),
    )
    attended, direct[3] = after((attended, direct[3]))
    passed.append(send(direct[3], CORE_SWAP))
    direct_back = [send(after(chunks[3:4], direct[3])[0], Y_SWAP)]
    attn_in = gathered[-1]
    attn_in_partner, cot_partner = (send(value, CORE_SWAP) for value in after((attn_in, cot), attended))
    attn_t = lax.all_to_all(attended, "ctx", 0, 0).reshape(width, rows)
    k_t, q_n, v_n = call(
        turn_kernel,
        [((HEAD, total), BF), tall, tall],
        [info, dealt, *after(spans, attended)],
        smem=2,
        cost=(0, 6 * total * 256, 0),
    )
    attn_t, passed[3], attn_in_partner, cot_partner, direct_back[0] = after(
        (attn_t, passed[3], attn_in_partner, cot_partner, direct_back[0]), k_t
    )
    direct_back.append(send(after(chunks[4:5], attn_t)[0], Y_SWAP))
    whole_scratch = [pltpu.VMEM((width, width), BF)] * 3 + [pltpu.VMEM((16, width), F32)]
    wide, low = ((rows, width), F32), ((rows, width), BF)
    result, grad_mid, grad_attended_t, packed, rights = call(
        functools.partial(mlp_kernel, 4),
        [low, wide, ((width, rows), BF), ((3, rows, width), BF), low],
        [info, inputs, cot, attn_t, own, other, w_output, w_expand, w_contract, *direct, *passed],
        smem=1,
        anys=range(6, 17),
        scratch=whole_scratch + [pltpu.VMEM((2, rows, width), BF), pltpu.SemaphoreType.DMA((24,))],
        cost=(12 * rows * width * width, 6 * width * width, 0),
    )
    grad_attended_t, packed, direct_back[1] = after((grad_attended_t, packed, direct_back[1]))
    grad_out = lax.all_to_all(grad_attended_t.reshape(16, HEAD, rows), "ctx", 0, 0)
    packed_partner = send(packed, CORE_SWAP)
    direct_back.append(send(after(chunks[5:6], packed)[0], Y_SWAP))
    attn_t_partner = send(attn_t, CORE_SWAP)

    half_width = width // 2
    terms = call(
        outer_kernel,
        [((half_width, half_width), BF)] * 6,
        [info, packed, rights, packed_partner, attn_t, attn_t_partner, cot, cot_partner],
        smem=1,
        scratch=[
            pltpu.VMEM((width, 2 * rows), BF),
            pltpu.VMEM((2 * rows, half_width), BF),
            pltpu.VMEM((width, half_width), BF),
        ],
        cost=(6 * rows * width * width, 6 * width * width, 0),
    )
    moves = {"y": Y_SWAP, "x": X_SWAP, "near": NEAR_SWAP, "far": FAR_SWAP}

    def travel(values, done):
        return [send(value, moves[order[done]]) for value, order in zip(values, ORDERS)]

    def halving(kept, came, done):
        size = half_width >> done
        shapes = [((size, half_width), BF)] * 6 if done < 3 else [((3 * PART, half_width), BF)] * 2
        return call(
            functools.partial(round_kernel, done),
            shapes,
            [info, *kept, *came],
            smem=1,
            cost=(0, 12 * size * half_width, 0),
        )

    came = travel(terms[3:], 0)
    kept = terms[:3]
    grad_out, direct_back[2] = after((grad_out, direct_back[2]), kept[0])
    direct_back.append(send(after(chunks[6:], kept[0])[0], Y_SWAP))
    grads = call(
        backward_kernel,
        [((16, 3 * HEAD, rows), BF)],
        [info, dealt, q_t, k_n, k_t, q_n, v_n, attended, grad_out, scale_col],
        smem=2,
        scratch=[
            pltpu.VMEM((WIDE, total), BF),
            pltpu.VMEM((total, WIDE), BF),
            pltpu.VMEM((1, total), F32),
            pltpu.VMEM((HEAD, total), F32),
            pltpu.VMEM((BLOCK, WIDE), F32),
            pltpu.VMEM((BLOCK, WIDE), F32),
            pltpu.SMEM((total // SPAN,), jnp.int32),
        ],
        cost=(5 * total * total * 256, 6 * total * 160, total * total // 2),
    )[0]
    grads, direct_back[3], *came = after((grads, direct_back[3], *came))
    returned = lax.all_to_all(grads, "ctx", 0, 0)
    keep, away = call(
        weight_kernel,
        [((256, half_width), F32), ((256, half_width), BF)],
        [info, grads, own, other, attn_in, attn_in_partner],
        smem=1,
        anys=(4, 5),
        scratch=[
            pltpu.VMEM((3 * HEAD, total), BF),
            pltpu.VMEM((3 * HEAD, width), F32),
            pltpu.VMEM((3 * HEAD, width), F32),
            pltpu.VMEM((1, width), F32),
            pltpu.VMEM((total, width), BF),
            pltpu.SemaphoreType.DMA((8,)),
        ],
        cost=(2 * 240 * total * width, 2 * total * width, 0),
    )
    from_pair = send(away, Y_SWAP)
    terms = halving(kept, after(came, keep), 1)
    kept, came = terms[:3], travel(terms[3:], 1)
    keep = after((keep,), kept[0])[0]
    summed = (keep + from_pair.astype(F32)).astype(BF)
    passed_back = [send(value, CORE_SWAP) for value in after(direct_back, summed)]

    shard = ((half_width, width), F32)
    line = ((half_width,), F32)

    def stacked(values):
        stack = call(stack_kernel, [((len(values), *values[0].shape), BF)], values)[0]
        return stack, send(stack, CORE_SWAP)

    forth1, back1 = send(summed, FORTH), send(summed, BACK)
    forth2, back2 = send(forth1, FORTH), send(back1, BACK)
    terms = halving(kept, after(came, forth1), 2)
    kept, came = terms[:3], travel(terms[3:], 2)
    forth2, back2 = after((forth2, back2), kept[0], returned, *passed_back)
    forth3, back3 = send(forth2, FORTH), send(back2, BACK)
    near, near_partner = stacked([summed, forth1, back1, forth2, back2])
    terms = halving(kept, came, 3)
    far = send(terms[1], FAR_SWAP)
    forth3, back3 = after((forth3, back3), terms[0])
    last = [send(forth3[:128], FORTH), send(back3[128:], BACK)]
    beyond = [send(value, CORE_SWAP) for value in (forth3, back3)]
    piece = (terms[0].astype(F32) + far.astype(F32)).astype(BF)
    grad_inputs = call(
        functools.partial(input_kernel, 4),
        [low],
        [info, inputs, returned, grad_mid, own, other, w_query, w_key, w_value, *direct_back, *passed_back],
        smem=1,
        anys=range(6, 17),
        scratch=whole_scratch + [pltpu.SemaphoreType.DMA((24,))],
        cost=(6 * rows * width * width, 6 * width * width, 0),
    )[0]
    last = after(last, *beyond, grad_inputs, near_partner)
    piece = after((piece,), last[0])[0]
    query_pieces = [near, near_partner, forth3, back3, *last, *beyond, *(send(value, CORE_SWAP) for value in last)]

    forth1, back1 = send(piece, FORTH), send(piece, BACK)
    grad_query, grad_key, grad_value, grad_gain_attn, grad_scale = call(
        finish_kernel,
        [shard] * 3 + [line, ((1, HEAD), F32)],
        [info, *query_pieces, gain_attn[None], factor],
        smem=1,
        out_anys=range(3),
        scratch=[
            pltpu.VMEM((3, width, half_width), BF),
            pltpu.VMEM((2, 256, half_width), BF),
            pltpu.VMEM((3, half_width, width), F32),
            pltpu.SemaphoreType.DMA((3,)),
        ],
        cost=(6 * 640 * 640 * 1280, 3 * 640 * 1280 * 4, 0),
    )
    forth1, back1 = after((forth1, back1), grad_query)
    forth2, back2 = send(forth1, FORTH), send(back1, BACK)
    forth3, back3 = send(forth2, FORTH), send(back2, BACK)
    near, near_partner = stacked([piece, forth1, back1, forth2, back2])
    partial_out = call(
        spread_kernel,
        [((half_width, 128), F32), shard, shard, shard],
        [info, near, near_partner, w_expand],
        smem=1,
        out_anys=(1, 2, 3),
        scratch=[pltpu.VMEM((30, PART, half_width), F32), pltpu.SemaphoreType.DMA((30,))],
        cost=(0, 3 * 640 * 1280 * 4, 0),
    )
    forth3, back3 = after((forth3, back3), partial_out[0])
    last = [send(forth3[:112], FORTH), send(back3[112:], BACK)]
    beyond = [send(value, CORE_SWAP) for value in (forth3, back3)]
    last = after(last, *beyond)
    args = [info, forth3, back3, *last, *beyond, *(send(value, CORE_SWAP) for value in last)]
    args += [partial_out[0], gain_mlp[None], w_expand, *partial_out[1:]]
    grad_contract, grad_expand, grad_output, grad_gain_mlp = call(
        spread_last_kernel,
        [shard] * 3 + [line],
        args,
        smem=1,
        anys=range(len(args) - 3, len(args)),
        out_anys=range(3),
        aliases={len(args) - 3 + at: at for at in range(3)},
        scratch=[
            pltpu.VMEM((18, PART, half_width), F32),
            pltpu.VMEM((2, *piece.shape), BF),
            pltpu.VMEM((half_width, 128), F32),
            pltpu.SemaphoreType.DMA((18,)),
        ],
        cost=(0, 3 * 640 * 1280 * 4, 0),
    )
    return (
        result[None], grad_inputs[None], grad_gain_attn, grad_query, grad_key, grad_value, grad_output,
        grad_scale[0], grad_gain_mlp, grad_expand, grad_contract,
    )


def solution(mesh):
    in_specs = (
        P("wt", "ctx", None),
        P("wt", "ctx", None),
        P("wt", None),
        P("wt", None),
        P("wt"),
        P("wt", None),
        P("wt", None),
        P("wt", None),
        P("wt", None),
        P(),
        P("wt"),
        P("wt", None),
        P("wt", None),
    )
    out_specs = (
        P("wt", "ctx", None),
        P("wt", "ctx", None),
        P("wt"),
        P("wt", None),
        P("wt", None),
        P("wt", None),
        P("wt", None),
        P(),
        P("wt"),
        P("wt", None),
        P("wt", None),
    )
    body = ring_device if mesh.shape["ctx"] == HEADS and mesh.shape["wt"] == 2 else per_device
    return jax.shard_map(
        body, mesh=mesh, in_specs=in_specs, out_specs=out_specs, check_vma=False
    )
```

```python
import functools
import math

import jax
import jax.numpy as jnp
import numpy as np
from jax import lax
from jax.experimental import pallas as pl
from jax.experimental.pallas import tpu as pltpu
from jax.sharding import PartitionSpec as P

HEADS = 16
HEAD = 80
SPAN = 128
LONGEST = 4096


EPS = 1e-06
LOG2E = 1.442695041
NEG = -1e30


def normed(values, gain):
    return values * lax.rsqrt(jnp.mean(values * values, axis=-1, keepdims=True) + EPS) * gain


def locate(dealt_spans, seq_lengths, offset, count, slot_tokens):
    row_ids = offset + jnp.arange(count, dtype=jnp.int32)
    slot_ids = row_ids // SPAN
    matches = slot_ids[:, None] == jnp.arange(dealt_spans.shape[0], dtype=jnp.int32)[None, :]
    span_ids = jnp.sum(jnp.where(matches, dealt_spans[None, :], 0), axis=1)
    natural = span_ids * SPAN + row_ids % SPAN
    sequence = natural // slot_tokens
    position = natural % slot_tokens
    owners = sequence[:, None] == jnp.arange(seq_lengths.shape[0], dtype=jnp.int32)[None, :]
    limits = jnp.sum(jnp.where(owners, seq_lengths[None, :], 0), axis=1)
    return (sequence, position, position < limits)


def permitted(query_place, key_place):
    same_seq = query_place[0][:, None] == key_place[0][None, :]
    causal = key_place[1][None, :] <= query_place[1][:, None]
    return (same_seq & causal & key_place[2][None, :])[None]


def per_device(
    tokens,
    cotangent,
    deal,
    lengths,
    gain_attn,
    w_query,
    w_key,
    w_value,
    w_output,
    query_scale,
    gain_mlp,
    w_expand,
    w_contract,
):
    row_count = tokens.shape[1]
    feat_width = tokens.shape[2]
    group_rows = row_count * lax.axis_size("ctx")
    slot_tokens = min(LONGEST, group_rows)
    block_rows = min(512, group_rows)
    blocks = group_rows // block_rows
    dealt_spans = deal[0]
    seq_lengths = lengths[0]
    inputs = tokens[0].astype(jnp.float32)
    shards = (gain_attn, w_query, w_key, w_value, w_output, gain_mlp, w_expand, w_contract)
    gathered = (
        lax.all_gather(shards[0], "wt", axis=0, tiled=True),
        lax.all_gather(shards[1], "wt", axis=0, tiled=True),
        lax.all_gather(shards[2], "wt", axis=0, tiled=True),
        lax.all_gather(shards[3], "wt", axis=0, tiled=True),
        lax.all_gather(shards[4], "wt", axis=0, tiled=True),
        lax.all_gather(shards[5], "wt", axis=0, tiled=True),
        lax.all_gather(shards[6], "wt", axis=0, tiled=True),
        lax.all_gather(shards[7], "wt", axis=0, tiled=True),
    )
    gain_one = gathered[0].astype(jnp.float32)
    gain_two = gathered[5].astype(jnp.float32)
    query_place = locate(
        dealt_spans, seq_lengths, lax.axis_index("ctx") * row_count, row_count, slot_tokens
    )
    scale_row = LOG2E / math.sqrt(HEAD) * jax.nn.softplus(query_scale)
    attn_in = normed(inputs, gain_one).astype(jnp.bfloat16)
    query_lin = jnp.dot(attn_in, gathered[1], preferred_element_type=jnp.float32)
    queries = (query_lin.reshape(row_count, HEADS, HEAD) * scale_row).astype(jnp.bfloat16)
    key_own = jnp.dot(attn_in, gathered[2], preferred_element_type=jnp.float32).astype(jnp.bfloat16)
    value_own = jnp.dot(attn_in, gathered[3], preferred_element_type=jnp.float32).astype(
        jnp.bfloat16
    )
    portion = (
        lax.all_gather(key_own, "ctx", axis=0, tiled=True),
        lax.all_gather(value_own, "ctx", axis=0, tiled=True),
    )
    running = jnp.full((HEADS, row_count), NEG, jnp.float32)
    count = portion[0].shape[0]
    key_rows = portion[0].reshape(count, HEADS, HEAD)
    value_rows = portion[1].reshape(count, HEADS, HEAD)
    permit_mask = permitted(
        query_place, locate(dealt_spans, seq_lengths, jnp.int32(0), count, slot_tokens)
    )
    scores = jnp.einsum("qhd,khd->hqk", queries, key_rows, preferred_element_type=jnp.float32)
    scores = jnp.where(permit_mask, scores, NEG)
    newest = jnp.maximum(running, jnp.max(scores, axis=-1))
    weights = jnp.where(permit_mask, jnp.exp(scores - newest[..., None]), 0.0)
    running_total = jnp.sum(weights, axis=-1)
    update = jnp.einsum(
        "hqk,khd->qhd", weights.astype(jnp.bfloat16), value_rows, preferred_element_type=jnp.float32
    )
    summed = update
    running, running_total, summed = (newest, running_total, summed)
    log_norm = running + jnp.log(running_total)
    attended = summed / jnp.transpose(running_total)[:, :, None]
    attn_out = attended.reshape(row_count, feat_width).astype(jnp.bfloat16)
    mid = inputs + jnp.dot(attn_out, gathered[4], preferred_element_type=jnp.float32)
    mlp_in = normed(mid, gain_two).astype(jnp.bfloat16)
    expanded = jnp.dot(mlp_in, gathered[6], preferred_element_type=jnp.float32)
    activated = jax.nn.silu(expanded).astype(jnp.bfloat16)
    result = mid + jnp.dot(activated, gathered[7], preferred_element_type=jnp.float32)
    weights_back = (
        lax.all_gather(shards[0], "wt", axis=0, tiled=True),
        lax.all_gather(shards[1], "wt", axis=0, tiled=True),
        lax.all_gather(shards[2], "wt", axis=0, tiled=True),
        lax.all_gather(shards[3], "wt", axis=0, tiled=True),
        lax.all_gather(shards[4], "wt", axis=0, tiled=True),
        lax.all_gather(shards[5], "wt", axis=0, tiled=True),
        lax.all_gather(shards[6], "wt", axis=0, tiled=True),
        lax.all_gather(shards[7], "wt", axis=0, tiled=True),
    )
    whole_keys, whole_values = (
        lax.all_gather(key_own, "ctx", axis=0, tiled=True),
        lax.all_gather(value_own, "ctx", axis=0, tiled=True),
    )
    grad_result = cotangent[0].astype(jnp.float32)
    grad_branch = grad_result.astype(jnp.bfloat16)
    grad_contract = jnp.einsum(
        "tf,td->fd", activated, grad_branch, preferred_element_type=jnp.float32
    )
    grad_act = jnp.einsum(
        "td,fd->tf", grad_branch, weights_back[7], preferred_element_type=jnp.float32
    )
    sigmoid_gate = jax.nn.sigmoid(expanded)
    grad_expanded = (grad_act * sigmoid_gate * (1.0 + expanded * (1.0 - sigmoid_gate))).astype(
        jnp.bfloat16
    )
    grad_expand = jnp.einsum("td,tf->df", mlp_in, grad_expanded, preferred_element_type=jnp.float32)
    grad_mlp_in = jnp.einsum(
        "tf,df->td", grad_expanded, weights_back[6], preferred_element_type=jnp.float32
    )
    unused_two, pull_two = jax.vjp(normed, mid, gain_two)
    grad_mid_norm, grad_gain_two = pull_two(grad_mlp_in)
    grad_mid = grad_result + grad_mid_norm
    grad_mid_low = grad_mid.astype(jnp.bfloat16)
    grad_output_w = jnp.einsum(
        "td,te->de", attn_out, grad_mid_low, preferred_element_type=jnp.float32
    )
    grad_attended = jnp.einsum(
        "te,de->td", grad_mid_low, weights_back[4], preferred_element_type=jnp.float32
    ).astype(jnp.bfloat16)
    out_grad = grad_attended.reshape(row_count, HEADS, HEAD)
    delta = jnp.transpose(jnp.sum(out_grad.astype(jnp.float32) * attended, axis=-1))
    key_blocks = (
        jnp.arange(blocks, dtype=jnp.int32),
        whole_keys.reshape(blocks, block_rows, feat_width),
        whole_values.reshape(blocks, block_rows, feat_width),
    )
    query_zero = jnp.zeros((row_count, HEADS, HEAD), jnp.float32)

    def back_block(query_grad, block_in):
        offset = block_in[0] * block_rows
        key_rows = block_in[1].reshape(block_rows, HEADS, HEAD)
        value_rows = block_in[2].reshape(block_rows, HEADS, HEAD)
        permit_mask = permitted(
            query_place, locate(dealt_spans, seq_lengths, offset, block_rows, slot_tokens)
        )
        scores = jnp.einsum("qhd,khd->hqk", queries, key_rows, preferred_element_type=jnp.float32)
        probabilities = jnp.where(permit_mask, jnp.exp(scores - log_norm[..., None]), 0.0)
        value_grad = jnp.einsum(
            "hqk,qhd->khd",
            probabilities.astype(jnp.bfloat16),
            out_grad,
            preferred_element_type=jnp.float32,
        )
        prob_grad = jnp.einsum(
            "qhd,khd->hqk", out_grad, value_rows, preferred_element_type=jnp.float32
        )
        score_grad = (probabilities * (prob_grad - delta[..., None])).astype(jnp.bfloat16)
        query_grad = query_grad + jnp.einsum(
            "hqk,khd->qhd", score_grad, key_rows, preferred_element_type=jnp.float32
        )
        key_grad = jnp.einsum(
            "hqk,qhd->khd", score_grad, queries, preferred_element_type=jnp.float32
        )
        return (
            query_grad,
            (key_grad.reshape(block_rows, feat_width), value_grad.reshape(block_rows, feat_width)),
        )

    query_grad, key_terms = lax.scan(back_block, query_zero, key_blocks)
    key_sum, value_sum = (
        lax.psum_scatter(
            key_terms[0].reshape(group_rows, feat_width).astype(jnp.bfloat16),
            "ctx",
            scatter_dimension=0,
            tiled=True,
        ).astype(jnp.float32),
        lax.psum_scatter(
            key_terms[1].reshape(group_rows, feat_width).astype(jnp.bfloat16),
            "ctx",
            scatter_dimension=0,
            tiled=True,
        ).astype(jnp.float32),
    )
    grad_keys = key_sum.astype(jnp.bfloat16)
    grad_values = value_sum.astype(jnp.bfloat16)
    grad_query_lin = (query_grad * scale_row).reshape(row_count, feat_width).astype(jnp.bfloat16)
    grad_scale = (
        jnp.sum(query_grad * query_lin.reshape(row_count, HEADS, HEAD), axis=(0, 1))
        * (LOG2E / math.sqrt(HEAD))
        * jax.nn.sigmoid(query_scale)
    )
    grad_query_w = jnp.einsum(
        "td,te->de", attn_in, grad_query_lin, preferred_element_type=jnp.float32
    )
    grad_key_w = jnp.einsum("td,te->de", attn_in, grad_keys, preferred_element_type=jnp.float32)
    grad_value_w = jnp.einsum("td,te->de", attn_in, grad_values, preferred_element_type=jnp.float32)
    grad_attn_in = jnp.einsum(
        "te,de->td", grad_query_lin, weights_back[1], preferred_element_type=jnp.float32
    )
    grad_attn_in = grad_attn_in + jnp.einsum(
        "te,de->td", grad_keys, weights_back[2], preferred_element_type=jnp.float32
    )
    grad_attn_in = grad_attn_in + jnp.einsum(
        "te,de->td", grad_values, weights_back[3], preferred_element_type=jnp.float32
    )
    unused_one, pull_one = jax.vjp(normed, inputs, gain_one)
    grad_in_norm, grad_gain_one = pull_one(grad_attn_in)
    grad_inputs = (grad_mid + grad_in_norm).astype(jnp.bfloat16)
    terms = (
        grad_gain_one,
        grad_query_w,
        grad_key_w,
        grad_value_w,
        grad_output_w,
        jnp.tile(grad_scale, lax.axis_size("wt")),
        grad_gain_two,
        grad_expand,
        grad_contract,
    )
    shares = (
        lax.psum_scatter(
            terms[0].astype(jnp.bfloat16), "wt", scatter_dimension=0, tiled=True
        ).astype(jnp.float32),
        lax.psum_scatter(
            terms[1].astype(jnp.bfloat16), "wt", scatter_dimension=0, tiled=True
        ).astype(jnp.float32),
        lax.psum_scatter(
            terms[2].astype(jnp.bfloat16), "wt", scatter_dimension=0, tiled=True
        ).astype(jnp.float32),
        lax.psum_scatter(
            terms[3].astype(jnp.bfloat16), "wt", scatter_dimension=0, tiled=True
        ).astype(jnp.float32),
        lax.psum_scatter(
            terms[4].astype(jnp.bfloat16), "wt", scatter_dimension=0, tiled=True
        ).astype(jnp.float32),
        lax.psum_scatter(
            terms[5].astype(jnp.bfloat16), "wt", scatter_dimension=0, tiled=True
        ).astype(jnp.float32),
        lax.psum_scatter(
            terms[6].astype(jnp.bfloat16), "wt", scatter_dimension=0, tiled=True
        ).astype(jnp.float32),
        lax.psum_scatter(
            terms[7].astype(jnp.bfloat16), "wt", scatter_dimension=0, tiled=True
        ).astype(jnp.float32),
        lax.psum_scatter(
            terms[8].astype(jnp.bfloat16), "wt", scatter_dimension=0, tiled=True
        ).astype(jnp.float32),
    )
    totals = (
        lax.psum(shares[0].astype(jnp.bfloat16), "ctx").astype(jnp.float32),
        lax.psum(shares[1].astype(jnp.bfloat16), "ctx").astype(jnp.float32),
        lax.psum(shares[2].astype(jnp.bfloat16), "ctx").astype(jnp.float32),
        lax.psum(shares[3].astype(jnp.bfloat16), "ctx").astype(jnp.float32),
        lax.psum(shares[4].astype(jnp.bfloat16), "ctx").astype(jnp.float32),
        lax.psum(shares[5].astype(jnp.bfloat16), "ctx").astype(jnp.float32),
        lax.psum(shares[6].astype(jnp.bfloat16), "ctx").astype(jnp.float32),
        lax.psum(shares[7].astype(jnp.bfloat16), "ctx").astype(jnp.float32),
        lax.psum(shares[8].astype(jnp.bfloat16), "ctx").astype(jnp.float32),
    )
    return (
        result.astype(jnp.bfloat16)[None],
        grad_inputs[None],
        totals[0],
        totals[1],
        totals[2],
        totals[3],
        totals[4],
        totals[5],
        totals[6],
        totals[7],
        totals[8],
    )


BF = jnp.bfloat16
F32 = jnp.float32
NN = (((1,), (0,)), ((), ()))
NT = (((1,), (1,)), ((), ()))
AXES = ("ctx", "wt")
LIMIT = 56 * 1024 * 1024

RING = ((0, 0), (1, 0), (2, 0), (3, 0), (3, 1), (2, 1), (1, 1), (0, 1))
PLACE = {chip: at for at, chip in enumerate(RING)}
OFFSETS = (0, -1, 1, -2, 2, -3, 3, 4)


def flat(z, x, core, y):
    return ((z * 2 + x) * 2 + core) * 2 + y


def pairs(move):
    return [
        (flat(z, x, core, y), flat(*move(z, x, core, y)))
        for z in range(4)
        for x in range(2)
        for core in range(2)
        for y in range(2)
    ]


def turned(by):
    def move(z, x, core, y):
        return (*RING[(PLACE[(z, x)] + by) % 8], core, y)

    return move


CORE_SWAP = pairs(lambda z, x, core, y: (z, x, 1 - core, y))
Y_SWAP = pairs(lambda z, x, core, y: (z, x, core, 1 - y))
X_SWAP = pairs(lambda z, x, core, y: (z, 1 - x, core, y))
NEAR_SWAP = pairs(lambda z, x, core, y: (z ^ 1, x, core, y))
FAR_SWAP = pairs(lambda z, x, core, y: (z ^ 2, x, core, y))
FORTH = pairs(turned(1))
BACK = pairs(turned(-1))


def slot_table():
    rows = []
    for c in range(16):
        z, x, core = c // 4, (c // 2) % 2, c % 2
        chips = [RING[(PLACE[(z, x)] + by) % 8] for by in OFFSETS]
        own = [(a * 2 + b) * 2 + core for a, b in chips]
        rows.append(own + [dev ^ 1 for dev in own])
    return np.asarray(rows, np.int32)


def send(value, moves):
    return lax.ppermute(value, AXES, moves)


def mm(left, right, dims=NN):
    return lax.dot_general(left, right, dims, preferred_element_type=F32)


def call(body, outs, args, smem=0, anys=(), scratch=(), cost=None, out_anys=(), aliases=None):
    whole, anywhere = pl.BlockSpec(memory_space=pltpu.VMEM), pl.BlockSpec(memory_space=pl.ANY)
    specs = [pl.BlockSpec(memory_space=pltpu.SMEM)] * smem
    specs += [anywhere if at in anys else whole for at in range(smem, len(args))]
    estimate = None
    if cost is not None:
        estimate = pl.CostEstimate(flops=int(cost[0]), bytes_accessed=int(cost[1]), transcendentals=int(cost[2]))
    return pl.pallas_call(
        body,
        out_shape=[jax.ShapeDtypeStruct(shape, kind) for shape, kind in outs],
        in_specs=specs,
        out_specs=[anywhere if at in out_anys else whole for at in range(len(outs))],
        scratch_shapes=list(scratch),
        input_output_aliases=aliases or {},
        cost_estimate=estimate,
        compiler_params=pltpu.CompilerParams(vmem_limit_bytes=LIMIT),
    )(*args)


def half(y, width=640):
    return pl.ds(pl.multiple_of(y * width, 128), width)


def pick_kernel(info, wq, wk, wv, gain_a, gain_m, out):
    chip = info[2]
    cols = lax.broadcasted_iota(jnp.int32, (2 * HEAD, wq.shape[1]), 1)
    rows = lax.broadcasted_iota(jnp.int32, (2 * HEAD, wq.shape[1]), 0)
    chosen = jnp.where(cols == rows + chip * (2 * HEAD), 1.0, 0.0).astype(BF)
    for at, ref in enumerate((wq, wk, wv)):
        both = mm(chosen, ref[...], NT).astype(BF)
        out[at * HEAD : (at + 1) * HEAD] = both[:HEAD]
        out[3 * HEAD + at * HEAD : 3 * HEAD + (at + 1) * HEAD] = both[HEAD:]
    line = lax.broadcasted_iota(jnp.int32, (16, gain_a.shape[1]), 0)
    tail = jnp.where(line == 0, gain_a[...].astype(F32), 0.0)
    tail = jnp.where(line == 1, gain_m[...].astype(F32), tail)
    out[6 * HEAD :] = tail.astype(BF)


def project_kernel(count, start, info, *refs):
    xs = refs[:count]
    own, other, scale = refs[count : count + 3]
    whole, mine, partner, attn_in, weight, gain, lines, sem = refs[-8:]
    y, core = info[0], info[1]
    weight[:, half(y)] = own[: 6 * HEAD]
    weight[:, half(1 - y)] = other[: 6 * HEAD]
    gain[:, half(y)] = own[6 * HEAD :].astype(F32)
    gain[:, half(1 - y)] = other[6 * HEAD :].astype(F32)
    row = 0
    for ref in xs:
        values = ref[...].astype(F32)
        scaled = values * lax.rsqrt(jnp.mean(values * values, axis=-1, keepdims=True) + EPS)
        attn_in[row : row + ref.shape[0]] = (scaled * gain[0:1]).astype(BF)
        row += ref.shape[0]
    copy = pltpu.make_async_copy(attn_in, whole.at[pl.ds(start, row)], sem)
    copy.start()
    lin = mm(weight[...], attn_in[...], NT)
    for head in range(2):
        base = head * 3 * HEAD
        lines[base : base + HEAD] = (lin[base : base + HEAD] * scale[...]).astype(BF)
        lines[base + HEAD : base + 3 * HEAD] = lin[base + HEAD : base + 3 * HEAD].astype(BF)
    mine[...] = lines[pl.ds(pl.multiple_of(core * 3 * HEAD, 16), 3 * HEAD)]
    partner[...] = lines[pl.ds(pl.multiple_of((1 - core) * 3 * HEAD, 16), 3 * HEAD)]
    copy.wait()


def span_slots(pieces):
    return [(ref, col) for ref in pieces for col in range(0, ref.shape[1], SPAN)]


def natural_span(info, deal, slot):
    return deal[2 * info[4 + slot // 2] + slot % 2]


def at_span(span):
    return pl.ds(pl.multiple_of(span * SPAN, SPAN), SPAN)


BLOCK = 1024
WIDE = 128


def block_at(at):
    return pl.ds(pl.multiple_of(at * BLOCK, BLOCK), BLOCK)


def in_parts(line):
    high = line.astype(BF)
    rest = line - high.astype(F32)
    middle = rest.astype(BF)
    low = (rest - middle.astype(F32)).astype(BF)
    at = lax.broadcasted_iota(jnp.int32, (16, line.shape[1]), 0)
    rows = jnp.where(at == 0, high.astype(F32), 0.0)
    rows = jnp.where(at == 1, middle.astype(F32), rows)
    return jnp.where(at == 2, low.astype(F32), rows).astype(BF)


def ones_behind(ref):
    at = lax.broadcasted_iota(jnp.int32, ref.shape, 1)
    ref[...] = jnp.where((at >= HEAD) & (at < HEAD + 3), 1.0, 0.0).astype(BF)


def forward_kernel(info, deal, *refs):
    pieces = refs[:10]
    out, queries, keys, values, lse, dealt = refs[10:]
    total = queries.shape[1]
    length = info[3]
    spans = total // SPAN
    blocks = total // BLOCK

    @pl.loop(0, spans)
    def _(at):
        dealt[deal[at]] = at

    line = lax.broadcasted_iota(jnp.int32, (16, total), 0)
    values[HEAD:] = jnp.where(line == 0, 1.0, 0.0).astype(BF)
    queries[HEAD:] = jnp.zeros((WIDE - HEAD, total), BF)
    ones_behind(keys)
    longest = jnp.zeros((1, SPAN), F32)
    for slot, (ref, col) in enumerate(span_slots(pieces)):
        where = at_span(natural_span(info, deal, slot))
        key = ref[HEAD : 2 * HEAD, col : col + SPAN]
        queries[:HEAD, where] = ref[:HEAD, col : col + SPAN]
        keys[where, :HEAD] = key.T
        values[:HEAD, where] = ref[2 * HEAD :, col : col + SPAN]
        sizes = key.astype(F32)
        longest = jnp.maximum(longest, jnp.sum(sizes * sizes, axis=0, keepdims=True))
    longest = jnp.max(longest, axis=1, keepdims=True)

    key_at = lax.broadcasted_iota(jnp.int32, (BLOCK, BLOCK), 0)
    query_at = lax.broadcasted_iota(jnp.int32, (BLOCK, BLOCK), 1)

    def scores_of(masked, i, j):
        scores = mm(keys[block_at(j), :], queries[:, block_at(i)])
        if masked:
            key_pos = j * BLOCK + key_at
            allowed = (key_pos <= i * BLOCK + query_at) & (key_pos < length)
            scores = jnp.where(allowed, scores, NEG)
        return scores

    def finish(i, peak, acc):
        here = block_at(i)
        norm = acc[HEAD : HEAD + 1]
        lse[:, here] = peak + jnp.log(norm)
        attended = (acc[:HEAD] / norm).astype(BF)
        for part in range(BLOCK // SPAN):
            row = dealt[i * (BLOCK // SPAN) + part]
            out[row // 2, :, at_span(row % 2)] = attended[:, part * SPAN : (part + 1) * SPAN]
        return jnp.min(norm)

    def bounded(i, least):
        here = block_at(i)
        query = queries[:HEAD, here].astype(F32)
        bound = jnp.sqrt(jnp.sum(query * query, axis=0, keepdims=True) * longest) - 40.0
        shift = in_parts(-bound)
        queries[HEAD : HEAD + 16, here] = shift

        def step(masked, j, acc):
            weights = jnp.exp(scores_of(masked, i, j)).astype(BF)
            return acc + mm(values[:, block_at(j)], weights)

        def tile(low, first):
            keys_at = pl.ds(pl.multiple_of(i * BLOCK + low, BLOCK // 2), BLOCK // 2)
            queries_at = pl.ds(pl.multiple_of(i * BLOCK + first, BLOCK // 2), BLOCK - first)
            scores = mm(keys[keys_at, :], queries[:, queries_at])
            local = key_at[: BLOCK // 2, first:] + low
            allowed = (local <= query_at[: BLOCK // 2, first:]) & (i * BLOCK + local < length)
            weights = jnp.exp(jnp.where(allowed, scores, NEG)).astype(BF)
            return mm(values[:, keys_at], weights)

        split = jnp.minimum(i, length // BLOCK)
        acc = lax.fori_loop(0, split, functools.partial(step, False), jnp.zeros((HEAD + 16, BLOCK), F32))
        acc = lax.fori_loop(split, i, functools.partial(step, True), acc)
        acc += tile(0, 0)
        later = acc[:, BLOCK // 2 :] + tile(BLOCK // 2, BLOCK // 2)
        acc = jnp.concatenate([acc[:, : BLOCK // 2], later], axis=1)
        exact = jnp.sum(shift.astype(F32), axis=0, keepdims=True)
        return jnp.minimum(least, finish(i, -exact, acc))

    least = lax.fori_loop(0, blocks, bounded, jnp.float32(1.0))

    @pl.when(jnp.logical_not(least > 1e-26))
    def _():
        queries[HEAD:] = jnp.zeros((WIDE - HEAD, total), BF)

        @pl.loop(0, blocks)
        def _(i):
            def step(j, carry):
                peak, acc = carry
                scores = scores_of(True, i, j)
                newest = jnp.maximum(peak, jnp.max(scores, axis=0, keepdims=True))
                weights = jnp.exp(scores - newest).astype(BF)
                return newest, acc * jnp.exp(peak - newest) + mm(values[:, block_at(j)], weights)

            start = (jnp.full((1, BLOCK), NEG, F32), jnp.zeros((HEAD + 16, BLOCK), F32))
            finish(i, *lax.fori_loop(0, i + 1, step, start))

    queries[HEAD : HEAD + 16] = in_parts(-lse[...])


def turn_kernel(info, deal, *refs):
    pieces, (k_t, q_n, v_n) = refs[:10], refs[10:]
    q_n[...] = jnp.zeros_like(q_n)
    ones_behind(v_n)
    for slot, (ref, col) in enumerate(span_slots(pieces)):
        where = at_span(natural_span(info, deal, slot))
        cols = slice(col, col + SPAN)
        k_t[:, where] = ref[HEAD : 2 * HEAD, cols]
        q_n[where, :HEAD] = ref[:HEAD, cols].T
        v_n[where, :HEAD] = ref[2 * HEAD :, cols].T


def backward_kernel(info, deal, *refs):
    q_t, k_n, k_t, q_n, v_n, attended, grad_out, scale, out, g_t, g_n, delta, dq_t, dk, dv, dealt = refs
    total = q_t.shape[1]
    length = info[3]
    spans = total // SPAN
    blocks = total // BLOCK

    @pl.loop(0, spans)
    def _(at):
        dealt[deal[at]] = at

    g_n[...] = jnp.zeros_like(g_n)
    g_t[HEAD:] = jnp.zeros((WIDE - HEAD, total), BF)
    for row in range(spans):
        where = at_span(deal[row])
        cols = slice(row % 2 * SPAN, row % 2 * SPAN + SPAN)
        grad = grad_out[row // 2, :, cols]
        g_t[:HEAD, where] = grad
        g_n[where, :HEAD] = grad.T
        product = grad.astype(F32) * attended[row // 2, :, cols].astype(F32)
        delta[:, where] = jnp.sum(product, axis=0, keepdims=True)
    g_t[HEAD : HEAD + 16] = in_parts(-delta[...])
    dq_t[...] = jnp.zeros_like(dq_t)

    key_at = lax.broadcasted_iota(jnp.int32, (BLOCK, BLOCK), 0)
    query_at = lax.broadcasted_iota(jnp.int32, (BLOCK, BLOCK), 1)

    @pl.loop(0, blocks)
    def _(j):
        there = block_at(j)
        dk[...] = jnp.zeros_like(dk)
        dv[...] = jnp.zeros_like(dv)

        def tile(masked, i, low, first, size):
            keys = pl.ds(pl.multiple_of(j * BLOCK + low, BLOCK // 2), size)
            here = pl.ds(pl.multiple_of(i * BLOCK + first, BLOCK // 2), BLOCK - first)
            probs = jnp.exp(mm(k_n[keys, :], q_t[:, here]))
            if masked:
                key_pos = j * BLOCK + low + key_at[:size, first:]
                allowed = (key_pos <= i * BLOCK + query_at[:size, first:]) & (key_pos < length)
                probs = jnp.where(allowed, probs, 0.0)
            probs = probs.astype(BF)
            grad_scores = probs * mm(v_n[keys, :], g_t[:, here]).astype(BF)
            rows = slice(low, low + size)
            dv[rows] += mm(probs, g_n[here, :])
            dk[rows] += mm(grad_scores, q_n[here, :])
            dq_t[:, here] += mm(k_t[:, keys], grad_scores)

        def step(masked, i, carry):
            tile(masked, i, 0, 0, BLOCK)
            return carry

        tile(True, j, 0, 0, BLOCK // 2)
        tile(True, j, BLOCK // 2, BLOCK // 2, BLOCK // 2)
        split = jnp.where((j + 1) * BLOCK <= length, j + 1, blocks)
        lax.fori_loop(j + 1, split, functools.partial(step, True), 0)
        lax.fori_loop(split, blocks, functools.partial(step, False), 0)
        for part in range(BLOCK // SPAN):
            row = dealt[j * (BLOCK // SPAN) + part]
            rows = slice(part * SPAN, (part + 1) * SPAN)
            out[row // 2, HEAD : 2 * HEAD, at_span(row % 2)] = dk[rows].T[:HEAD].astype(BF)
            out[row // 2, 2 * HEAD :, at_span(row % 2)] = dv[rows].T[:HEAD].astype(BF)

    for row in range(spans):
        cols = slice(row % 2 * SPAN, row % 2 * SPAN + SPAN)
        out[row // 2, :HEAD, cols] = (dq_t[:, at_span(deal[row])] * scale[...]).astype(BF)


def load_weights(info, own, direct, passed, wholes, sems):
    y, core = info[0], info[1]
    started = []
    count = 0
    for at, whole in enumerate(wholes):
        rows, part = own[at].shape[0], own[at].shape[0] // 2
        far = (1 - y) * rows
        places = [(own[at], y * rows)]
        for chunks, base in ((direct, far + core * part), (passed, far + (1 - core) * part)):
            start = 0
            for chunk in chunks:
                low, high = max(start, at * part), min(start + chunk.shape[0], at * part + part)
                if low < high:
                    places.append((chunk.at[pl.ds(low - start, high - low)], base + low - at * part))
                start += chunk.shape[0]
        copies = []
        for ref, start in places:
            target = whole.at[pl.ds(pl.multiple_of(start, 16), ref.shape[0])]
            copies.append(pltpu.make_async_copy(ref, target, sems.at[count]))
            copies[-1].start()
            count += 1
        started.append(copies)
    return started


def arrive(copies):
    for copy in copies:
        copy.wait()


def mlp_kernel(chunks, info, tokens, cotangent, attn_t, own, other, *refs):
    shards, direct, passed = refs[:3], refs[3 : 3 + chunks], refs[3 + chunks : 3 + 2 * chunks]
    refs = refs[3 + 2 * chunks :]
    outs = refs[:5]
    w_output, w_expand, w_contract, gain, right, sems = refs[5:]
    result, grad_mid_out, grad_attended_t, away, rights = outs
    y, core = info[0], info[1]
    loads = load_weights(info, shards, direct, passed, (w_output, w_expand, w_contract), sems)
    gain[:, half(y)] = own[6 * HEAD :].astype(F32)
    gain[:, half(1 - y)] = other[6 * HEAD :].astype(F32)
    gains = gain[1:2]
    attn = attn_t[...].T
    arrive(loads[0])
    mid = tokens[...].astype(F32) + mm(attn, w_output[...])
    rate = lax.rsqrt(jnp.mean(mid * mid, axis=-1, keepdims=True) + EPS)
    mlp_in = (mid * rate * gains).astype(BF)
    away[1] = mlp_in
    arrive(loads[1])
    expanded = mm(mlp_in, w_expand[...])
    gate = jax.nn.sigmoid(expanded)
    act = (expanded * gate).astype(BF)
    away[0] = act
    arrive(loads[2])
    result[...] = (mid + mm(act, w_contract[...])).astype(BF)
    grad_act = mm(cotangent[...], w_contract[...], NT)
    grad_expanded = (grad_act * gate * (1.0 + expanded * (1.0 - gate))).astype(BF)
    right[0] = grad_expanded
    grad_mlp_in = mm(grad_expanded, w_expand[...], NT) * gains
    inner = jnp.mean(grad_mlp_in * mid, axis=-1, keepdims=True)
    grad_mid = cotangent[...].astype(F32) + rate * grad_mlp_in - mid * (rate * rate * rate * inner)
    grad_mid_out[...] = grad_mid
    low = grad_mid.astype(BF)
    right[1] = low
    grad_attended_t[...] = mm(w_output[...], low, NT).astype(BF)
    for at in range(2):
        rights[:, at * 640 : at * 640 + 640] = right[at, :, half(core)]
        away[2, :, at * 640 : at * 640 + 640] = right[at, :, half(1 - core)]


BITS = ("y", "x", "far", "near")
ORDERS = (("y", "x", "near", "far"), ("x", "near", "y", "far"), ("near", "y", "x", "far"))
BIT_AT = {"y": 0, "x": 20, "near": 21, "far": 22}
PART = 80


def left_bits(order, done):
    return [name for name in BITS if name not in order[:done]]


def halves(info, order, done):
    left = left_bits(order, done)
    name = order[done]
    bit = info[BIT_AT[name]]
    stride = 1 << (len(left) - 1 - left.index(name))
    count = 1 << len(left)
    bases = [block for block in range(count) if block & stride == 0]
    return [(base + bit * stride, base + (1 - bit) * stride) for base in bases]


def rows_of(block):
    start = block * PART
    return pl.ds(start if isinstance(block, int) else pl.multiple_of(start, 16), PART)


def outer_kernel(info, own, rights, partner, attn_t, attn_t_partner, cot, cot_partner, *refs):
    outs, (left, right, full) = refs[:6], refs[6:]
    core = info[1]
    rows = cot.shape[0]
    for at in range(3):
        if at < 2:
            left[:, :rows] = own[at].T
            left[:, rows:] = partner[at].T
        else:
            left[:, :rows] = attn_t[...]
            left[:, rows:] = attn_t_partner[...]
        if at == 0:
            right[:rows] = cot[:, half(core)]
            right[rows:] = cot_partner[:, half(core)]
        else:
            cols = slice((at - 1) * 640, at * 640)
            right[:rows] = rights[:, cols]
            right[rows:] = partner[2, :, cols]
        full[...] = mm(left[...], right[...]).astype(BF)
        for to, (kept, sent) in enumerate(halves(info, ORDERS[at], 0)):
            outs[at][rows_of(to)] = full[rows_of(kept)]
            outs[3 + at][rows_of(to)] = full[rows_of(sent)]


def round_kernel(done, info, *refs):
    kept, came, outs = refs[:3], refs[3:6], refs[6:]
    for at in range(3):
        for to, (mine, theirs) in enumerate(halves(info, ORDERS[at], done)):
            if len(outs) == 6:
                stay, away, target = outs[at], outs[3 + at], rows_of(to)
            else:
                stay, away, target = outs[0], outs[1], rows_of(at)
            for out, block in ((stay, mine), (away, theirs)):
                total = kept[at][rows_of(block)].astype(F32) + came[at][rows_of(block)].astype(F32)
                out[target] = total.astype(BF)


def folded(products):
    return sum(products[:, at : at + 128] for at in range(0, products.shape[1], 128))


def row_sums(products):
    ones = jnp.ones((16, products.shape[1]), BF)
    high = products.astype(BF)
    low = (products - high.astype(F32)).astype(BF)
    return mm(ones, high, NT) + mm(ones, low, NT)


def stack_kernel(*refs):
    for at, ref in enumerate(refs[:-1]):
        refs[-1][at] = ref[...]


def joined(pieces, last):
    count = len(pieces) // 2
    ready = []
    for colour in range(2):
        group = pieces[colour * count : colour * count + count]
        cut = group[-2].shape[0]
        last[colour, :cut] = group[-2][...]
        last[colour, cut:] = group[-1][...]
        ready += [*group[:-2], last.at[colour]]
    return ready


def slot_of(at, count, first):
    return first + at if at < count else 8 + first + at - count


def scatter(info, refs, first, blocks, sems, outs, expand, sums):
    copies = []
    for at, ref in enumerate(refs):
        dev = info[4 + slot_of(at, len(refs) // 2, first)]
        block = ((dev // 2) % 2) * 4 + dev // 4
        rows = pl.ds(pl.multiple_of(block * PART, 16), PART)
        for way in range(3):
            blocks[3 * at + way] = ref[way * PART : (way + 1) * PART].astype(F32)
            target = outs[way].at[rows, half(dev % 2)]
            copies.append(pltpu.make_async_copy(blocks.at[3 * at + way], target, sems.at[3 * at + way]))
            copies[-1].start()
        sums[rows] += folded(blocks[3 * at + 1] * expand[rows, half(dev % 2)].astype(F32))
    return copies


def spread_kernel(info, near, near_partner, expand, sums, *refs):
    outs, (blocks, sems) = refs[:3], refs[3:]
    pieces = [stack.at[at] for stack in (near, near_partner) for at in range(5)]
    sums[...] = jnp.zeros_like(sums)
    arrive(scatter(info, pieces, 0, blocks, sems, outs, expand, sums))


def spread_last_kernel(info, *refs):
    pieces, (before, gain, expand), (*outs, grad_gain), refs = refs[:8], refs[8:11], refs[14:18], refs[18:]
    blocks, last, sums, sems = refs
    sums[...] = before[...]
    copies = scatter(info, joined(pieces, last), 5, blocks, sems, outs, expand, sums)
    size = sums.shape[0]
    grad_gain[...] = (row_sums(sums[...])[0:1] / gain[...].astype(F32)).reshape(size)
    arrive(copies)


def weight_kernel(info, grads, own, other, *refs):
    inputs = refs[:2]
    keep, away, lines, weight, total, gain_sums, attn_in, sems = refs[2:]
    y, core = info[0], info[1]
    rows = attn_in.shape[0] // 8
    loads = []
    for at in range(8):
        source = inputs[at // 4].at[pl.ds(at % 4 * rows, rows)]
        loads.append(pltpu.make_async_copy(source, attn_in.at[pl.ds(at * rows, rows)], sems.at[at]))
        loads[-1].start()
    for slot in range(16):
        lines[:, slot * 256 : slot * 256 + 256] = grads[info[4 + slot]]
    mine = pl.ds(pl.multiple_of(core * 3 * HEAD, 16), 3 * HEAD)
    weight[:, half(y)] = own[mine].astype(F32)
    weight[:, half(1 - y)] = other[mine].astype(F32)
    total[...] = jnp.zeros_like(total)
    for at in range(4):
        loads[2 * at].wait()
        loads[2 * at + 1].wait()
        part = slice(2 * at * rows, 2 * (at + 1) * rows)
        total[...] += mm(lines[:, part], attn_in[part])
    keep[: 3 * HEAD] = total[:, half(y)]
    away[: 3 * HEAD] = total[:, half(1 - y)].astype(BF)
    weight[...] *= total[...]
    scale_sums = row_sums(weight[:HEAD])[0:1]
    gain_sums[...] = jnp.sum(weight[...], axis=0, keepdims=True)
    line = lax.broadcasted_iota(jnp.int32, (16, keep.shape[1]), 0)
    keep[3 * HEAD :] = jnp.where(line == 1, gain_sums[:, half(y)], 0.0)
    away[3 * HEAD :] = jnp.where(line == 1, gain_sums[:, half(1 - y)], 0.0).astype(BF)
    keep[3 * HEAD : 3 * HEAD + 1, :HEAD] = scale_sums
    first = lax.broadcasted_iota(jnp.int32, (16, HEAD), 0) == 0
    behind = jnp.where(line == 1, gain_sums[:, half(1 - y)], 0.0)[:, :HEAD]
    away[3 * HEAD :, :HEAD] = jnp.where(first, scale_sums, behind).astype(BF)


def finish_kernel(info, near, near_partner, *refs):
    pieces, (gain, factor), outs, refs = refs[:8], refs[8:10], refs[10:13], refs[13:]
    grad_gain, grad_scale, stacks, last, turned, sems = refs
    extra = jnp.zeros((16, last.shape[2]), F32)
    early = [stack.at[at] for stack in (near, near_partner) for at in range(5)]
    for first, group in ((0, early), (5, joined(pieces, last))):
        for at, ref in enumerate(group):
            rows = pl.ds(pl.multiple_of(info[4 + slot_of(at, len(group) // 2, first)] * HEAD, 16), HEAD)
            for way in range(3):
                stacks[way, rows] = ref[way * HEAD : (way + 1) * HEAD]
            extra += ref[3 * HEAD :].astype(F32)
    grad_scale[...] = extra[0:1, :HEAD] * factor[...]
    size = turned.shape[1]
    grad_gain[...] = (extra[1:2] / gain[...].astype(F32)).reshape(size)
    same = lax.broadcasted_iota(jnp.int32, (size, size), 0) == lax.broadcasted_iota(jnp.int32, (size, size), 1)
    unit = jnp.where(same, 1.0, 0.0).astype(BF)
    copies = []
    for at, out in enumerate(outs):
        turned[at] = mm(unit, stacks[at], NT)
        copies.append(pltpu.make_async_copy(turned.at[at], out, sems.at[at]))
        copies[-1].start()
    arrive(copies)


def input_kernel(chunks, info, tokens, grads, grad_mid, own, other, *refs):
    shards, direct, passed = refs[:3], refs[3 : 3 + chunks], refs[3 + chunks : 3 + 2 * chunks]
    out, *weights, gain, sems = refs[3 + 2 * chunks :]
    y = info[0]
    loads = load_weights(info, shards, direct, passed, weights, sems)
    gain[:, half(y)] = own[6 * HEAD :].astype(F32)
    gain[:, half(1 - y)] = other[6 * HEAD :].astype(F32)
    heads, width = grads.shape[0], grads.shape[2]
    values = tokens[...].astype(F32)
    rate = lax.rsqrt(jnp.mean(values * values, axis=-1, keepdims=True) + EPS)
    turned_grad = None
    for at, ref in enumerate(weights):
        part = grads[:, at * HEAD : (at + 1) * HEAD, :].reshape(heads * HEAD, width)
        arrive(loads[at])
        product = mm(ref[...], part)
        turned_grad = product if turned_grad is None else turned_grad + product
    grad = turned_grad.T * gain[0:1]
    inner = jnp.mean(grad * values, axis=-1, keepdims=True)
    out[...] = (grad_mid[...] + rate * grad - values * (rate * rate * rate * inner)).astype(BF)


def after(values, *others):
    return lax.optimization_barrier((tuple(values), others))[0]


def weight_rows(shards, core):
    size = shards[0].shape[0] // 2
    return jnp.concatenate([lax.dynamic_slice_in_dim(shard, core * size, size, 0) for shard in shards], axis=0)


def ring_device(
    tokens, cotangent, deal, lengths, gain_attn, w_query, w_key, w_value, w_output, query_scale,
    gain_mlp, w_expand, w_contract
):
    rows, width = tokens.shape[1:]
    c, y = lax.axis_index("ctx"), lax.axis_index("wt")
    core, x, z = c % 2, (c // 2) % 2, c // 4
    table = lax.dynamic_index_in_dim(jnp.asarray(slot_table()), c, 0, keepdims=False)
    head = jnp.stack([y, core, c // 2, lengths[0, 0]]).astype(jnp.int32)
    info = jnp.concatenate([head, table, jnp.stack([x, z % 2, z // 2]).astype(jnp.int32)])
    dealt = deal[0]
    total = rows * 16
    softplus = jax.nn.softplus(query_scale)
    scale_col = (LOG2E / math.sqrt(HEAD) * softplus)[:, None]
    factor = (jax.nn.sigmoid(query_scale) / softplus)[None, :]
    inputs = tokens[0]
    cot = cotangent[0]
    cut = rows // 2
    mine, partner, gathered = [], [], []

    def project(other, *group):
        count = sum(part.shape[0] for part in group)
        start = sum(piece.shape[1] for piece in mine)
        args = [info, *group, own, other, scale_col]
        got = call(
            functools.partial(project_kernel, len(group), start),
            [((8 * rows, width), BF), ((3 * HEAD, count), BF), ((3 * HEAD, count), BF)],
            args + gathered[-1:],
            smem=1,
            anys=range(len(args), len(args) + 1),
            out_anys=(0,),
            aliases={len(args): 0} if gathered else None,
            scratch=[
                pltpu.VMEM((count, width), BF),
                pltpu.VMEM((6 * HEAD, width), BF),
                pltpu.VMEM((16, width), F32),
                pltpu.VMEM((6 * HEAD, count), BF),
                pltpu.SemaphoreType.DMA,
            ],
            cost=(2 * 480 * 1280 * count, 4 * 1280 * count, 0),
        )
        gathered.append(got[0])
        mine.append(got[1])
        partner.append(send(got[2], CORE_SWAP))
        return got[1]

    forth1, back1 = send(inputs, FORTH), send(inputs, BACK)
    size = width // 4
    first_rows = lax.dynamic_slice_in_dim(w_output, core * size, 128, 0)
    direct, passed = [send(first_rows, Y_SWAP)], []
    own = call(
        pick_kernel,
        [((6 * HEAD + 16, width // 2), BF)],
        [info, w_query, w_key, w_value, gain_attn[None], gain_mlp[None]],
        smem=1,
        cost=(2 * 480 * 640 * 1280, 3 * 640 * 1280 * 2, 0),
    )[0]
    other = send(own, Y_SWAP)
    forth1, back1, direct[0] = after((forth1, back1, direct[0]), own)

    forth2, back2 = send(forth1, FORTH), send(back1, BACK)
    rows_out = weight_rows(after((w_output, w_expand, w_contract), forth1), core)
    rows_back = weight_rows(after((w_query, w_key, w_value), forth1), core)
    chunks = [rows_out[128:448], rows_out[448:624], rows_out[624:]]
    chunks += [rows_back[:224], rows_back[224:384], rows_back[384:608], rows_back[608:]]
    passed.append(send(direct[0], CORE_SWAP))
    forth2, back2, other, passed[0], *chunks = after((forth2, back2, other, passed[0], *chunks))

    forth3, back3 = send(forth2, FORTH), send(back2, BACK)
    direct.append(send(after(chunks[:1], passed[0])[0], Y_SWAP))
    done = project(other, inputs)
    done = project(other, forth1, back1), done
    done = project(other, forth2, back2), done
    forth3, back3, direct[1] = after((forth3, back3, direct[1]), done)

    forth4, back4 = send(forth3[:cut], FORTH), send(back3[cut:], BACK)
    passed.append(send(direct[1], CORE_SWAP))
    direct.append(send(after(chunks[1:2], direct[1])[0], Y_SWAP))
    done = project(other, forth3, back3)
    forth4, back4, direct[2], passed[1] = after((forth4, back4, direct[2], passed[1]), done)
    passed.append(send(direct[2], CORE_SWAP))
    direct.append(send(after(chunks[2:3], direct[2])[0], Y_SWAP))
    project(other, forth4, back4)
    *spans, passed[2] = after((*mine, *partner, passed[2]))

    tall, flat_t = ((total, WIDE), BF), ((WIDE, total), BF)
    attended, q_t, k_n = call(
        forward_kernel,
        [((16, HEAD, rows), BF), flat_t, tall],
        [info, dealt, *spans],
        smem=2,
        scratch=[
            pltpu.VMEM((HEAD + 16, total), BF),
            pltpu.VMEM((1, total), F32),
            pltpu.SMEM((total // SPAN,), jnp.int32),
        ],
        cost=(2 * total * total * 256, 3 * total * 160, total * total // 2),
    )
    attended, direct[3] = after((attended, direct[3]))
    passed.append(send(direct[3], CORE_SWAP))
    direct_back = [send(after(chunks[3:4], direct[3])[0], Y_SWAP)]
    attn_in = gathered[-1]
    attn_in_partner, cot_partner = (send(value, CORE_SWAP) for value in after((attn_in, cot), attended))
    attn_t = lax.all_to_all(attended, "ctx", 0, 0).reshape(width, rows)
    k_t, q_n, v_n = call(
        turn_kernel,
        [((HEAD, total), BF), tall, tall],
        [info, dealt, *after(spans, attended)],
        smem=2,
        cost=(0, 6 * total * 256, 0),
    )
    attn_t, passed[3], attn_in_partner, cot_partner, direct_back[0] = after(
        (attn_t, passed[3], attn_in_partner, cot_partner, direct_back[0]), k_t
    )
    direct_back.append(send(after(chunks[4:5], attn_t)[0], Y_SWAP))
    whole_scratch = [pltpu.VMEM((width, width), BF)] * 3 + [pltpu.VMEM((16, width), F32)]
    wide, low = ((rows, width), F32), ((rows, width), BF)
    result, grad_mid, grad_attended_t, packed, rights = call(
        functools.partial(mlp_kernel, 4),
        [low, wide, ((width, rows), BF), ((3, rows, width), BF), low],
        [info, inputs, cot, attn_t, own, other, w_output, w_expand, w_contract, *direct, *passed],
        smem=1,
        anys=range(6, 17),
        scratch=whole_scratch + [pltpu.VMEM((2, rows, width), BF), pltpu.SemaphoreType.DMA((24,))],
        cost=(12 * rows * width * width, 6 * width * width, 0),
    )
    grad_attended_t, packed, direct_back[1] = after((grad_attended_t, packed, direct_back[1]))
    grad_out = lax.all_to_all(grad_attended_t.reshape(16, HEAD, rows), "ctx", 0, 0)
    packed_partner = send(packed, CORE_SWAP)
    direct_back.append(send(after(chunks[5:6], packed)[0], Y_SWAP))
    attn_t_partner = send(attn_t, CORE_SWAP)

    half_width = width // 2
    terms = call(
        outer_kernel,
        [((half_width, half_width), BF)] * 6,
        [info, packed, rights, packed_partner, attn_t, attn_t_partner, cot, cot_partner],
        smem=1,
        scratch=[
            pltpu.VMEM((width, 2 * rows), BF),
            pltpu.VMEM((2 * rows, half_width), BF),
            pltpu.VMEM((width, half_width), BF),
        ],
        cost=(6 * rows * width * width, 6 * width * width, 0),
    )
    moves = {"y": Y_SWAP, "x": X_SWAP, "near": NEAR_SWAP, "far": FAR_SWAP}

    def travel(values, done):
        return [send(value, moves[order[done]]) for value, order in zip(values, ORDERS)]

    def halving(kept, came, done):
        size = half_width >> done
        shapes = [((size, half_width), BF)] * 6 if done < 3 else [((3 * PART, half_width), BF)] * 2
        return call(
            functools.partial(round_kernel, done),
            shapes,
            [info, *kept, *came],
            smem=1,
            cost=(0, 12 * size * half_width, 0),
        )

    came = travel(terms[3:], 0)
    kept = terms[:3]
    grad_out, direct_back[2] = after((grad_out, direct_back[2]), kept[0])
    direct_back.append(send(after(chunks[6:], kept[0])[0], Y_SWAP))
    grads = call(
        backward_kernel,
        [((16, 3 * HEAD, rows), BF)],
        [info, dealt, q_t, k_n, k_t, q_n, v_n, attended, grad_out, scale_col],
        smem=2,
        scratch=[
            pltpu.VMEM((WIDE, total), BF),
            pltpu.VMEM((total, WIDE), BF),
            pltpu.VMEM((1, total), F32),
            pltpu.VMEM((HEAD, total), F32),
            pltpu.VMEM((BLOCK, WIDE), F32),
            pltpu.VMEM((BLOCK, WIDE), F32),
            pltpu.SMEM((total // SPAN,), jnp.int32),
        ],
        cost=(5 * total * total * 256, 6 * total * 160, total * total // 2),
    )[0]
    grads, *came = after((grads, *came))
    returned = lax.all_to_all(grads, "ctx", 0, 0)
    keep, away = call(
        weight_kernel,
        [((256, half_width), F32), ((256, half_width), BF)],
        [info, grads, own, other, attn_in, attn_in_partner],
        smem=1,
        anys=(4, 5),
        scratch=[
            pltpu.VMEM((3 * HEAD, total), BF),
            pltpu.VMEM((3 * HEAD, width), F32),
            pltpu.VMEM((3 * HEAD, width), F32),
            pltpu.VMEM((1, width), F32),
            pltpu.VMEM((total, width), BF),
            pltpu.SemaphoreType.DMA((8,)),
        ],
        cost=(2 * 240 * total * width, 2 * total * width, 0),
    )
    from_pair = send(away, Y_SWAP)
    terms = halving(kept, after(came, keep), 1)
    kept, came = terms[:3], travel(terms[3:], 1)
    keep = after((keep,), kept[0])[0]
    summed = (keep + from_pair.astype(F32)).astype(BF)
    passed_back = [send(value, CORE_SWAP) for value in after(direct_back, summed)]

    shard = ((half_width, width), F32)
    line = ((half_width,), F32)

    def stacked(values):
        stack = call(stack_kernel, [((len(values), *values[0].shape), BF)], values)[0]
        return stack, send(stack, CORE_SWAP)

    forth1, back1 = send(summed, FORTH), send(summed, BACK)
    forth2, back2 = send(forth1, FORTH), send(back1, BACK)
    terms = halving(kept, after(came, forth1), 2)
    kept, came = terms[:3], travel(terms[3:], 2)
    forth2, back2 = after((forth2, back2), kept[0], returned, *passed_back)
    forth3, back3 = send(forth2, FORTH), send(back2, BACK)
    near, near_partner = stacked([summed, forth1, back1, forth2, back2])
    terms = halving(kept, came, 3)
    far = send(terms[1], FAR_SWAP)
    forth3, back3 = after((forth3, back3), terms[0])
    last = [send(forth3[:128], FORTH), send(back3[128:], BACK)]
    beyond = [send(value, CORE_SWAP) for value in (forth3, back3)]
    piece = (terms[0].astype(F32) + far.astype(F32)).astype(BF)
    grad_inputs = call(
        functools.partial(input_kernel, 4),
        [low],
        [info, inputs, returned, grad_mid, own, other, w_query, w_key, w_value, *direct_back, *passed_back],
        smem=1,
        anys=range(6, 17),
        scratch=whole_scratch + [pltpu.SemaphoreType.DMA((24,))],
        cost=(6 * rows * width * width, 6 * width * width, 0),
    )[0]
    last = after(last, *beyond, grad_inputs, near_partner)
    piece = after((piece,), last[0])[0]
    query_pieces = [near, near_partner, forth3, back3, *last, *beyond, *(send(value, CORE_SWAP) for value in last)]

    forth1, back1 = send(piece, FORTH), send(piece, BACK)
    grad_query, grad_key, grad_value, grad_gain_attn, grad_scale = call(
        finish_kernel,
        [shard] * 3 + [line, ((1, HEAD), F32)],
        [info, *query_pieces, gain_attn[None], factor],
        smem=1,
        out_anys=range(3),
        scratch=[
            pltpu.VMEM((3, width, half_width), BF),
            pltpu.VMEM((2, 256, half_width), BF),
            pltpu.VMEM((3, half_width, width), F32),
            pltpu.SemaphoreType.DMA((3,)),
        ],
        cost=(6 * 640 * 640 * 1280, 3 * 640 * 1280 * 4, 0),
    )
    forth1, back1 = after((forth1, back1), grad_query)
    forth2, back2 = send(forth1, FORTH), send(back1, BACK)
    forth3, back3 = send(forth2, FORTH), send(back2, BACK)
    near, near_partner = stacked([piece, forth1, back1, forth2, back2])
    partial_out = call(
        spread_kernel,
        [((half_width, 128), F32), shard, shard, shard],
        [info, near, near_partner, w_expand],
        smem=1,
        out_anys=(1, 2, 3),
        scratch=[pltpu.VMEM((30, PART, half_width), F32), pltpu.SemaphoreType.DMA((30,))],
        cost=(0, 3 * 640 * 1280 * 4, 0),
    )
    forth3, back3 = after((forth3, back3), partial_out[0])
    last = [send(forth3[:112], FORTH), send(back3[112:], BACK)]
    beyond = [send(value, CORE_SWAP) for value in (forth3, back3)]
    last = after(last, *beyond)
    args = [info, forth3, back3, *last, *beyond, *(send(value, CORE_SWAP) for value in last)]
    args += [partial_out[0], gain_mlp[None], w_expand, *partial_out[1:]]
    grad_contract, grad_expand, grad_output, grad_gain_mlp = call(
        spread_last_kernel,
        [shard] * 3 + [line],
        args,
        smem=1,
        anys=range(len(args) - 3, len(args)),
        out_anys=range(3),
        aliases={len(args) - 3 + at: at for at in range(3)},
        scratch=[
            pltpu.VMEM((18, PART, half_width), F32),
            pltpu.VMEM((2, *piece.shape), BF),
            pltpu.VMEM((half_width, 128), F32),
            pltpu.SemaphoreType.DMA((18,)),
        ],
        cost=(0, 3 * 640 * 1280 * 4, 0),
    )
    return (
        result[None], grad_inputs[None], grad_gain_attn, grad_query, grad_key, grad_value, grad_output,
        grad_scale[0], grad_gain_mlp, grad_expand, grad_contract,
    )


def solution(mesh):
    in_specs = (
        P("wt", "ctx", None),
        P("wt", "ctx", None),
        P("wt", None),
        P("wt", None),
        P("wt"),
        P("wt", None),
        P("wt", None),
        P("wt", None),
        P("wt", None),
        P(),
        P("wt"),
        P("wt", None),
        P("wt", None),
    )
    out_specs = (
        P("wt", "ctx", None),
        P("wt", "ctx", None),
        P("wt"),
        P("wt", None),
        P("wt", None),
        P("wt", None),
        P("wt", None),
        P(),
        P("wt"),
        P("wt", None),
        P("wt", None),
    )
    body = ring_device if mesh.shape["ctx"] == HEADS and mesh.shape["wt"] == 2 else per_device
    return jax.shard_map(
        body, mesh=mesh, in_specs=in_specs, out_specs=out_specs, check_vma=False
    )
```

```python
import functools
import math

import jax
import jax.numpy as jnp
import numpy as np
from jax import lax
from jax.experimental import pallas as pl
from jax.experimental.pallas import tpu as pltpu
from jax.sharding import PartitionSpec as P

HEADS = 16
HEAD = 80
SPAN = 128
LONGEST = 4096


EPS = 1e-06
LOG2E = 1.442695041
NEG = -1e30


def normed(values, gain):
    return values * lax.rsqrt(jnp.mean(values * values, axis=-1, keepdims=True) + EPS) * gain


def locate(dealt_spans, seq_lengths, offset, count, slot_tokens):
    row_ids = offset + jnp.arange(count, dtype=jnp.int32)
    slot_ids = row_ids // SPAN
    matches = slot_ids[:, None] == jnp.arange(dealt_spans.shape[0], dtype=jnp.int32)[None, :]
    span_ids = jnp.sum(jnp.where(matches, dealt_spans[None, :], 0), axis=1)
    natural = span_ids * SPAN + row_ids % SPAN
    sequence = natural // slot_tokens
    position = natural % slot_tokens
    owners = sequence[:, None] == jnp.arange(seq_lengths.shape[0], dtype=jnp.int32)[None, :]
    limits = jnp.sum(jnp.where(owners, seq_lengths[None, :], 0), axis=1)
    return (sequence, position, position < limits)


def permitted(query_place, key_place):
    same_seq = query_place[0][:, None] == key_place[0][None, :]
    causal = key_place[1][None, :] <= query_place[1][:, None]
    return (same_seq & causal & key_place[2][None, :])[None]


def per_device(
    tokens,
    cotangent,
    deal,
    lengths,
    gain_attn,
    w_query,
    w_key,
    w_value,
    w_output,
    query_scale,
    gain_mlp,
    w_expand,
    w_contract,
):
    row_count = tokens.shape[1]
    feat_width = tokens.shape[2]
    group_rows = row_count * lax.axis_size("ctx")
    slot_tokens = min(LONGEST, group_rows)
    block_rows = min(512, group_rows)
    blocks = group_rows // block_rows
    dealt_spans = deal[0]
    seq_lengths = lengths[0]
    inputs = tokens[0].astype(jnp.float32)
    shards = (gain_attn, w_query, w_key, w_value, w_output, gain_mlp, w_expand, w_contract)
    gathered = (
        lax.all_gather(shards[0], "wt", axis=0, tiled=True),
        lax.all_gather(shards[1], "wt", axis=0, tiled=True),
        lax.all_gather(shards[2], "wt", axis=0, tiled=True),
        lax.all_gather(shards[3], "wt", axis=0, tiled=True),
        lax.all_gather(shards[4], "wt", axis=0, tiled=True),
        lax.all_gather(shards[5], "wt", axis=0, tiled=True),
        lax.all_gather(shards[6], "wt", axis=0, tiled=True),
        lax.all_gather(shards[7], "wt", axis=0, tiled=True),
    )
    gain_one = gathered[0].astype(jnp.float32)
    gain_two = gathered[5].astype(jnp.float32)
    query_place = locate(
        dealt_spans, seq_lengths, lax.axis_index("ctx") * row_count, row_count, slot_tokens
    )
    scale_row = LOG2E / math.sqrt(HEAD) * jax.nn.softplus(query_scale)
    attn_in = normed(inputs, gain_one).astype(jnp.bfloat16)
    query_lin = jnp.dot(attn_in, gathered[1], preferred_element_type=jnp.float32)
    queries = (query_lin.reshape(row_count, HEADS, HEAD) * scale_row).astype(jnp.bfloat16)
    key_own = jnp.dot(attn_in, gathered[2], preferred_element_type=jnp.float32).astype(jnp.bfloat16)
    value_own = jnp.dot(attn_in, gathered[3], preferred_element_type=jnp.float32).astype(
        jnp.bfloat16
    )
    portion = (
        lax.all_gather(key_own, "ctx", axis=0, tiled=True),
        lax.all_gather(value_own, "ctx", axis=0, tiled=True),
    )
    running = jnp.full((HEADS, row_count), NEG, jnp.float32)
    count = portion[0].shape[0]
    key_rows = portion[0].reshape(count, HEADS, HEAD)
    value_rows = portion[1].reshape(count, HEADS, HEAD)
    permit_mask = permitted(
        query_place, locate(dealt_spans, seq_lengths, jnp.int32(0), count, slot_tokens)
    )
    scores = jnp.einsum("qhd,khd->hqk", queries, key_rows, preferred_element_type=jnp.float32)
    scores = jnp.where(permit_mask, scores, NEG)
    newest = jnp.maximum(running, jnp.max(scores, axis=-1))
    weights = jnp.where(permit_mask, jnp.exp(scores - newest[..., None]), 0.0)
    running_total = jnp.sum(weights, axis=-1)
    update = jnp.einsum(
        "hqk,khd->qhd", weights.astype(jnp.bfloat16), value_rows, preferred_element_type=jnp.float32
    )
    summed = update
    running, running_total, summed = (newest, running_total, summed)
    log_norm = running + jnp.log(running_total)
    attended = summed / jnp.transpose(running_total)[:, :, None]
    attn_out = attended.reshape(row_count, feat_width).astype(jnp.bfloat16)
    mid = inputs + jnp.dot(attn_out, gathered[4], preferred_element_type=jnp.float32)
    mlp_in = normed(mid, gain_two).astype(jnp.bfloat16)
    expanded = jnp.dot(mlp_in, gathered[6], preferred_element_type=jnp.float32)
    activated = jax.nn.silu(expanded).astype(jnp.bfloat16)
    result = mid + jnp.dot(activated, gathered[7], preferred_element_type=jnp.float32)
    weights_back = (
        lax.all_gather(shards[0], "wt", axis=0, tiled=True),
        lax.all_gather(shards[1], "wt", axis=0, tiled=True),
        lax.all_gather(shards[2], "wt", axis=0, tiled=True),
        lax.all_gather(shards[3], "wt", axis=0, tiled=True),
        lax.all_gather(shards[4], "wt", axis=0, tiled=True),
        lax.all_gather(shards[5], "wt", axis=0, tiled=True),
        lax.all_gather(shards[6], "wt", axis=0, tiled=True),
        lax.all_gather(shards[7], "wt", axis=0, tiled=True),
    )
    whole_keys, whole_values = (
        lax.all_gather(key_own, "ctx", axis=0, tiled=True),
        lax.all_gather(value_own, "ctx", axis=0, tiled=True),
    )
    grad_result = cotangent[0].astype(jnp.float32)
    grad_branch = grad_result.astype(jnp.bfloat16)
    grad_contract = jnp.einsum(
        "tf,td->fd", activated, grad_branch, preferred_element_type=jnp.float32
    )
    grad_act = jnp.einsum(
        "td,fd->tf", grad_branch, weights_back[7], preferred_element_type=jnp.float32
    )
    sigmoid_gate = jax.nn.sigmoid(expanded)
    grad_expanded = (grad_act * sigmoid_gate * (1.0 + expanded * (1.0 - sigmoid_gate))).astype(
        jnp.bfloat16
    )
    grad_expand = jnp.einsum("td,tf->df", mlp_in, grad_expanded, preferred_element_type=jnp.float32)
    grad_mlp_in = jnp.einsum(
        "tf,df->td", grad_expanded, weights_back[6], preferred_element_type=jnp.float32
    )
    unused_two, pull_two = jax.vjp(normed, mid, gain_two)
    grad_mid_norm, grad_gain_two = pull_two(grad_mlp_in)
    grad_mid = grad_result + grad_mid_norm
    grad_mid_low = grad_mid.astype(jnp.bfloat16)
    grad_output_w = jnp.einsum(
        "td,te->de", attn_out, grad_mid_low, preferred_element_type=jnp.float32
    )
    grad_attended = jnp.einsum(
        "te,de->td", grad_mid_low, weights_back[4], preferred_element_type=jnp.float32
    ).astype(jnp.bfloat16)
    out_grad = grad_attended.reshape(row_count, HEADS, HEAD)
    delta = jnp.transpose(jnp.sum(out_grad.astype(jnp.float32) * attended, axis=-1))
    key_blocks = (
        jnp.arange(blocks, dtype=jnp.int32),
        whole_keys.reshape(blocks, block_rows, feat_width),
        whole_values.reshape(blocks, block_rows, feat_width),
    )
    query_zero = jnp.zeros((row_count, HEADS, HEAD), jnp.float32)

    def back_block(query_grad, block_in):
        offset = block_in[0] * block_rows
        key_rows = block_in[1].reshape(block_rows, HEADS, HEAD)
        value_rows = block_in[2].reshape(block_rows, HEADS, HEAD)
        permit_mask = permitted(
            query_place, locate(dealt_spans, seq_lengths, offset, block_rows, slot_tokens)
        )
        scores = jnp.einsum("qhd,khd->hqk", queries, key_rows, preferred_element_type=jnp.float32)
        probabilities = jnp.where(permit_mask, jnp.exp(scores - log_norm[..., None]), 0.0)
        value_grad = jnp.einsum(
            "hqk,qhd->khd",
            probabilities.astype(jnp.bfloat16),
            out_grad,
            preferred_element_type=jnp.float32,
        )
        prob_grad = jnp.einsum(
            "qhd,khd->hqk", out_grad, value_rows, preferred_element_type=jnp.float32
        )
        score_grad = (probabilities * (prob_grad - delta[..., None])).astype(jnp.bfloat16)
        query_grad = query_grad + jnp.einsum(
            "hqk,khd->qhd", score_grad, key_rows, preferred_element_type=jnp.float32
        )
        key_grad = jnp.einsum(
            "hqk,qhd->khd", score_grad, queries, preferred_element_type=jnp.float32
        )
        return (
            query_grad,
            (key_grad.reshape(block_rows, feat_width), value_grad.reshape(block_rows, feat_width)),
        )

    query_grad, key_terms = lax.scan(back_block, query_zero, key_blocks)
    key_sum, value_sum = (
        lax.psum_scatter(
            key_terms[0].reshape(group_rows, feat_width).astype(jnp.bfloat16),
            "ctx",
            scatter_dimension=0,
            tiled=True,
        ).astype(jnp.float32),
        lax.psum_scatter(
            key_terms[1].reshape(group_rows, feat_width).astype(jnp.bfloat16),
            "ctx",
            scatter_dimension=0,
            tiled=True,
        ).astype(jnp.float32),
    )
    grad_keys = key_sum.astype(jnp.bfloat16)
    grad_values = value_sum.astype(jnp.bfloat16)
    grad_query_lin = (query_grad * scale_row).reshape(row_count, feat_width).astype(jnp.bfloat16)
    grad_scale = (
        jnp.sum(query_grad * query_lin.reshape(row_count, HEADS, HEAD), axis=(0, 1))
        * (LOG2E / math.sqrt(HEAD))
        * jax.nn.sigmoid(query_scale)
    )
    grad_query_w = jnp.einsum(
        "td,te->de", attn_in, grad_query_lin, preferred_element_type=jnp.float32
    )
    grad_key_w = jnp.einsum("td,te->de", attn_in, grad_keys, preferred_element_type=jnp.float32)
    grad_value_w = jnp.einsum("td,te->de", attn_in, grad_values, preferred_element_type=jnp.float32)
    grad_attn_in = jnp.einsum(
        "te,de->td", grad_query_lin, weights_back[1], preferred_element_type=jnp.float32
    )
    grad_attn_in = grad_attn_in + jnp.einsum(
        "te,de->td", grad_keys, weights_back[2], preferred_element_type=jnp.float32
    )
    grad_attn_in = grad_attn_in + jnp.einsum(
        "te,de->td", grad_values, weights_back[3], preferred_element_type=jnp.float32
    )
    unused_one, pull_one = jax.vjp(normed, inputs, gain_one)
    grad_in_norm, grad_gain_one = pull_one(grad_attn_in)
    grad_inputs = (grad_mid + grad_in_norm).astype(jnp.bfloat16)
    terms = (
        grad_gain_one,
        grad_query_w,
        grad_key_w,
        grad_value_w,
        grad_output_w,
        jnp.tile(grad_scale, lax.axis_size("wt")),
        grad_gain_two,
        grad_expand,
        grad_contract,
    )
    shares = (
        lax.psum_scatter(
            terms[0].astype(jnp.bfloat16), "wt", scatter_dimension=0, tiled=True
        ).astype(jnp.float32),
        lax.psum_scatter(
            terms[1].astype(jnp.bfloat16), "wt", scatter_dimension=0, tiled=True
        ).astype(jnp.float32),
        lax.psum_scatter(
            terms[2].astype(jnp.bfloat16), "wt", scatter_dimension=0, tiled=True
        ).astype(jnp.float32),
        lax.psum_scatter(
            terms[3].astype(jnp.bfloat16), "wt", scatter_dimension=0, tiled=True
        ).astype(jnp.float32),
        lax.psum_scatter(
            terms[4].astype(jnp.bfloat16), "wt", scatter_dimension=0, tiled=True
        ).astype(jnp.float32),
        lax.psum_scatter(
            terms[5].astype(jnp.bfloat16), "wt", scatter_dimension=0, tiled=True
        ).astype(jnp.float32),
        lax.psum_scatter(
            terms[6].astype(jnp.bfloat16), "wt", scatter_dimension=0, tiled=True
        ).astype(jnp.float32),
        lax.psum_scatter(
            terms[7].astype(jnp.bfloat16), "wt", scatter_dimension=0, tiled=True
        ).astype(jnp.float32),
        lax.psum_scatter(
            terms[8].astype(jnp.bfloat16), "wt", scatter_dimension=0, tiled=True
        ).astype(jnp.float32),
    )
    totals = (
        lax.psum(shares[0].astype(jnp.bfloat16), "ctx").astype(jnp.float32),
        lax.psum(shares[1].astype(jnp.bfloat16), "ctx").astype(jnp.float32),
        lax.psum(shares[2].astype(jnp.bfloat16), "ctx").astype(jnp.float32),
        lax.psum(shares[3].astype(jnp.bfloat16), "ctx").astype(jnp.float32),
        lax.psum(shares[4].astype(jnp.bfloat16), "ctx").astype(jnp.float32),
        lax.psum(shares[5].astype(jnp.bfloat16), "ctx").astype(jnp.float32),
        lax.psum(shares[6].astype(jnp.bfloat16), "ctx").astype(jnp.float32),
        lax.psum(shares[7].astype(jnp.bfloat16), "ctx").astype(jnp.float32),
        lax.psum(shares[8].astype(jnp.bfloat16), "ctx").astype(jnp.float32),
    )
    return (
        result.astype(jnp.bfloat16)[None],
        grad_inputs[None],
        totals[0],
        totals[1],
        totals[2],
        totals[3],
        totals[4],
        totals[5],
        totals[6],
        totals[7],
        totals[8],
    )


BF = jnp.bfloat16
F32 = jnp.float32
NN = (((1,), (0,)), ((), ()))
NT = (((1,), (1,)), ((), ()))
AXES = ("ctx", "wt")
LIMIT = 56 * 1024 * 1024

RING = ((0, 0), (1, 0), (2, 0), (3, 0), (3, 1), (2, 1), (1, 1), (0, 1))
PLACE = {chip: at for at, chip in enumerate(RING)}
OFFSETS = (0, -1, 1, -2, 2, -3, 3, 4)


def flat(z, x, core, y):
    return ((z * 2 + x) * 2 + core) * 2 + y


def pairs(move):
    return [
        (flat(z, x, core, y), flat(*move(z, x, core, y)))
        for z in range(4)
        for x in range(2)
        for core in range(2)
        for y in range(2)
    ]


def turned(by):
    def move(z, x, core, y):
        return (*RING[(PLACE[(z, x)] + by) % 8], core, y)

    return move


CORE_SWAP = pairs(lambda z, x, core, y: (z, x, 1 - core, y))
Y_SWAP = pairs(lambda z, x, core, y: (z, x, core, 1 - y))
X_SWAP = pairs(lambda z, x, core, y: (z, 1 - x, core, y))
NEAR_SWAP = pairs(lambda z, x, core, y: (z ^ 1, x, core, y))
FAR_SWAP = pairs(lambda z, x, core, y: (z ^ 2, x, core, y))
FORTH = pairs(turned(1))
BACK = pairs(turned(-1))


def slot_table():
    rows = []
    for c in range(16):
        z, x, core = c // 4, (c // 2) % 2, c % 2
        chips = [RING[(PLACE[(z, x)] + by) % 8] for by in OFFSETS]
        own = [(a * 2 + b) * 2 + core for a, b in chips]
        rows.append(own + [dev ^ 1 for dev in own])
    return np.asarray(rows, np.int32)


def send(value, moves):
    return lax.ppermute(value, AXES, moves)


def mm(left, right, dims=NN):
    return lax.dot_general(left, right, dims, preferred_element_type=F32)


def call(body, outs, args, smem=0, anys=(), scratch=(), cost=None, out_anys=(), aliases=None):
    whole, anywhere = pl.BlockSpec(memory_space=pltpu.VMEM), pl.BlockSpec(memory_space=pl.ANY)
    specs = [pl.BlockSpec(memory_space=pltpu.SMEM)] * smem
    specs += [anywhere if at in anys else whole for at in range(smem, len(args))]
    estimate = None
    if cost is not None:
        estimate = pl.CostEstimate(flops=int(cost[0]), bytes_accessed=int(cost[1]), transcendentals=int(cost[2]))
    return pl.pallas_call(
        body,
        out_shape=[jax.ShapeDtypeStruct(shape, kind) for shape, kind in outs],
        in_specs=specs,
        out_specs=[anywhere if at in out_anys else whole for at in range(len(outs))],
        scratch_shapes=list(scratch),
        input_output_aliases=aliases or {},
        cost_estimate=estimate,
        compiler_params=pltpu.CompilerParams(vmem_limit_bytes=LIMIT),
    )(*args)


def half(y, width=640):
    return pl.ds(pl.multiple_of(y * width, 128), width)


def pick_kernel(info, wq, wk, wv, gain_a, gain_m, out):
    chip = info[2]
    cols = lax.broadcasted_iota(jnp.int32, (2 * HEAD, wq.shape[1]), 1)
    rows = lax.broadcasted_iota(jnp.int32, (2 * HEAD, wq.shape[1]), 0)
    chosen = jnp.where(cols == rows + chip * (2 * HEAD), 1.0, 0.0).astype(BF)
    for at, ref in enumerate((wq, wk, wv)):
        both = mm(chosen, ref[...], NT).astype(BF)
        out[at * HEAD : (at + 1) * HEAD] = both[:HEAD]
        out[3 * HEAD + at * HEAD : 3 * HEAD + (at + 1) * HEAD] = both[HEAD:]
    line = lax.broadcasted_iota(jnp.int32, (16, gain_a.shape[1]), 0)
    tail = jnp.where(line == 0, gain_a[...].astype(F32), 0.0)
    tail = jnp.where(line == 1, gain_m[...].astype(F32), tail)
    out[6 * HEAD :] = tail.astype(BF)


def project_kernel(count, start, info, *refs):
    xs = refs[:count]
    own, other, scale = refs[count : count + 3]
    whole, mine, partner, attn_in, weight, gain, lines, sem = refs[-8:]
    y, core = info[0], info[1]
    weight[:, half(y)] = own[: 6 * HEAD]
    weight[:, half(1 - y)] = other[: 6 * HEAD]
    gain[:, half(y)] = own[6 * HEAD :].astype(F32)
    gain[:, half(1 - y)] = other[6 * HEAD :].astype(F32)
    row = 0
    for ref in xs:
        values = ref[...].astype(F32)
        scaled = values * lax.rsqrt(jnp.mean(values * values, axis=-1, keepdims=True) + EPS)
        attn_in[row : row + ref.shape[0]] = (scaled * gain[0:1]).astype(BF)
        row += ref.shape[0]
    copy = pltpu.make_async_copy(attn_in, whole.at[pl.ds(start, row)], sem)
    copy.start()
    lin = mm(weight[...], attn_in[...], NT)
    for head in range(2):
        base = head * 3 * HEAD
        lines[base : base + HEAD] = (lin[base : base + HEAD] * scale[...]).astype(BF)
        lines[base + HEAD : base + 3 * HEAD] = lin[base + HEAD : base + 3 * HEAD].astype(BF)
    mine[...] = lines[pl.ds(pl.multiple_of(core * 3 * HEAD, 16), 3 * HEAD)]
    partner[...] = lines[pl.ds(pl.multiple_of((1 - core) * 3 * HEAD, 16), 3 * HEAD)]
    copy.wait()


def span_slots(pieces):
    return [(ref, col) for ref in pieces for col in range(0, ref.shape[1], SPAN)]


def natural_span(info, deal, slot):
    return deal[2 * info[4 + slot // 2] + slot % 2]


def at_span(span):
    return pl.ds(pl.multiple_of(span * SPAN, SPAN), SPAN)


BLOCK = 1024
WIDE = 128


def block_at(at):
    return pl.ds(pl.multiple_of(at * BLOCK, BLOCK), BLOCK)


def in_parts(line):
    high = line.astype(BF)
    rest = line - high.astype(F32)
    middle = rest.astype(BF)
    low = (rest - middle.astype(F32)).astype(BF)
    at = lax.broadcasted_iota(jnp.int32, (16, line.shape[1]), 0)
    rows = jnp.where(at == 0, high.astype(F32), 0.0)
    rows = jnp.where(at == 1, middle.astype(F32), rows)
    return jnp.where(at == 2, low.astype(F32), rows).astype(BF)


def ones_behind(ref):
    at = lax.broadcasted_iota(jnp.int32, ref.shape, 1)
    ref[...] = jnp.where((at >= HEAD) & (at < HEAD + 3), 1.0, 0.0).astype(BF)


def forward_kernel(info, deal, *refs):
    pieces = refs[:10]
    out, queries, keys, values, lse, dealt = refs[10:]
    total = queries.shape[1]
    length = info[3]
    spans = total // SPAN
    blocks = total // BLOCK

    @pl.loop(0, spans)
    def _(at):
        dealt[deal[at]] = at

    line = lax.broadcasted_iota(jnp.int32, (16, total), 0)
    values[HEAD:] = jnp.where(line == 0, 1.0, 0.0).astype(BF)
    queries[HEAD:] = jnp.zeros((WIDE - HEAD, total), BF)
    ones_behind(keys)
    longest = jnp.zeros((1, SPAN), F32)
    for slot, (ref, col) in enumerate(span_slots(pieces)):
        where = at_span(natural_span(info, deal, slot))
        key = ref[HEAD : 2 * HEAD, col : col + SPAN]
        queries[:HEAD, where] = ref[:HEAD, col : col + SPAN]
        keys[where, :HEAD] = key.T
        values[:HEAD, where] = ref[2 * HEAD :, col : col + SPAN]
        sizes = key.astype(F32)
        longest = jnp.maximum(longest, jnp.sum(sizes * sizes, axis=0, keepdims=True))
    longest = jnp.max(longest, axis=1, keepdims=True)

    key_at = lax.broadcasted_iota(jnp.int32, (BLOCK, BLOCK), 0)
    query_at = lax.broadcasted_iota(jnp.int32, (BLOCK, BLOCK), 1)

    def scores_of(masked, i, j):
        scores = mm(keys[block_at(j), :], queries[:, block_at(i)])
        if masked:
            key_pos = j * BLOCK + key_at
            allowed = (key_pos <= i * BLOCK + query_at) & (key_pos < length)
            scores = jnp.where(allowed, scores, NEG)
        return scores

    def finish(i, peak, acc):
        here = block_at(i)
        norm = acc[HEAD : HEAD + 1]
        lse[:, here] = peak + jnp.log(norm)
        attended = (acc[:HEAD] / norm).astype(BF)
        for part in range(BLOCK // SPAN):
            row = dealt[i * (BLOCK // SPAN) + part]
            out[row // 2, :, at_span(row % 2)] = attended[:, part * SPAN : (part + 1) * SPAN]
        return jnp.min(norm)

    def bounded(i, least):
        here = block_at(i)
        query = queries[:HEAD, here].astype(F32)
        bound = jnp.sqrt(jnp.sum(query * query, axis=0, keepdims=True) * longest) - 40.0
        shift = in_parts(-bound)
        queries[HEAD : HEAD + 16, here] = shift

        def step(masked, j, acc):
            weights = jnp.exp(scores_of(masked, i, j)).astype(BF)
            return acc + mm(values[:, block_at(j)], weights)

        def tile(low, first):
            keys_at = pl.ds(pl.multiple_of(i * BLOCK + low, BLOCK // 2), BLOCK // 2)
            queries_at = pl.ds(pl.multiple_of(i * BLOCK + first, BLOCK // 2), BLOCK - first)
            scores = mm(keys[keys_at, :], queries[:, queries_at])
            local = key_at[: BLOCK // 2, first:] + low
            allowed = (local <= query_at[: BLOCK // 2, first:]) & (i * BLOCK + local < length)
            weights = jnp.exp(jnp.where(allowed, scores, NEG)).astype(BF)
            return mm(values[:, keys_at], weights)

        split = jnp.minimum(i, length // BLOCK)
        acc = lax.fori_loop(0, split, functools.partial(step, False), jnp.zeros((HEAD + 16, BLOCK), F32))
        acc = lax.fori_loop(split, i, functools.partial(step, True), acc)
        acc += tile(0, 0)
        later = acc[:, BLOCK // 2 :] + tile(BLOCK // 2, BLOCK // 2)
        acc = jnp.concatenate([acc[:, : BLOCK // 2], later], axis=1)
        exact = jnp.sum(shift.astype(F32), axis=0, keepdims=True)
        return jnp.minimum(least, finish(i, -exact, acc))

    least = lax.fori_loop(0, blocks, bounded, jnp.float32(1.0))

    @pl.when(jnp.logical_not(least > 1e-26))
    def _():
        queries[HEAD:] = jnp.zeros((WIDE - HEAD, total), BF)

        @pl.loop(0, blocks)
        def _(i):
            def step(j, carry):
                peak, acc = carry
                scores = scores_of(True, i, j)
                newest = jnp.maximum(peak, jnp.max(scores, axis=0, keepdims=True))
                weights = jnp.exp(scores - newest).astype(BF)
                return newest, acc * jnp.exp(peak - newest) + mm(values[:, block_at(j)], weights)

            start = (jnp.full((1, BLOCK), NEG, F32), jnp.zeros((HEAD + 16, BLOCK), F32))
            finish(i, *lax.fori_loop(0, i + 1, step, start))

    queries[HEAD : HEAD + 16] = in_parts(-lse[...])


def turn_kernel(info, deal, *refs):
    pieces, (k_t, q_n, v_n) = refs[:10], refs[10:]
    q_n[...] = jnp.zeros_like(q_n)
    ones_behind(v_n)
    for slot, (ref, col) in enumerate(span_slots(pieces)):
        where = at_span(natural_span(info, deal, slot))
        cols = slice(col, col + SPAN)
        k_t[:, where] = ref[HEAD : 2 * HEAD, cols]
        q_n[where, :HEAD] = ref[:HEAD, cols].T
        v_n[where, :HEAD] = ref[2 * HEAD :, cols].T


def backward_kernel(info, deal, *refs):
    q_t, k_n, k_t, q_n, v_n, attended, grad_out, scale, out, g_t, g_n, delta, dq_t, dk, dv, dealt = refs
    total = q_t.shape[1]
    length = info[3]
    spans = total // SPAN
    blocks = total // BLOCK

    @pl.loop(0, spans)
    def _(at):
        dealt[deal[at]] = at

    g_n[...] = jnp.zeros_like(g_n)
    g_t[HEAD:] = jnp.zeros((WIDE - HEAD, total), BF)
    for row in range(spans):
        where = at_span(deal[row])
        cols = slice(row % 2 * SPAN, row % 2 * SPAN + SPAN)
        grad = grad_out[row // 2, :, cols]
        g_t[:HEAD, where] = grad
        g_n[where, :HEAD] = grad.T
        product = grad.astype(F32) * attended[row // 2, :, cols].astype(F32)
        delta[:, where] = jnp.sum(product, axis=0, keepdims=True)
    g_t[HEAD : HEAD + 16] = in_parts(-delta[...])
    dq_t[...] = jnp.zeros_like(dq_t)

    key_at = lax.broadcasted_iota(jnp.int32, (BLOCK, BLOCK), 0)
    query_at = lax.broadcasted_iota(jnp.int32, (BLOCK, BLOCK), 1)

    @pl.loop(0, blocks)
    def _(j):
        there = block_at(j)
        dk[...] = jnp.zeros_like(dk)
        dv[...] = jnp.zeros_like(dv)

        def tile(masked, i, low, first, size):
            keys = pl.ds(pl.multiple_of(j * BLOCK + low, BLOCK // 4), size)
            here = pl.ds(pl.multiple_of(i * BLOCK + first, BLOCK // 4), BLOCK - first)
            probs = jnp.exp(mm(k_n[keys, :], q_t[:, here]))
            if masked:
                key_pos = j * BLOCK + low + key_at[:size, first:]
                allowed = (key_pos <= i * BLOCK + query_at[:size, first:]) & (key_pos < length)
                probs = jnp.where(allowed, probs, 0.0)
            probs = probs.astype(BF)
            grad_scores = probs * mm(v_n[keys, :], g_t[:, here]).astype(BF)
            rows = slice(low, low + size)
            dv[rows] += mm(probs, g_n[here, :])
            dk[rows] += mm(grad_scores, q_n[here, :])
            dq_t[:, here] += mm(k_t[:, keys], grad_scores)

        def step(masked, i, carry):
            tile(masked, i, 0, 0, BLOCK)
            return carry

        for low in range(0, BLOCK, BLOCK // 4):
            tile(True, j, low, low, BLOCK // 4)
        split = jnp.where((j + 1) * BLOCK <= length, j + 1, blocks)
        lax.fori_loop(j + 1, split, functools.partial(step, True), 0)
        lax.fori_loop(split, blocks, functools.partial(step, False), 0)
        for part in range(BLOCK // SPAN):
            row = dealt[j * (BLOCK // SPAN) + part]
            rows = slice(part * SPAN, (part + 1) * SPAN)
            out[row // 2, HEAD : 2 * HEAD, at_span(row % 2)] = dk[rows].T[:HEAD].astype(BF)
            out[row // 2, 2 * HEAD :, at_span(row % 2)] = dv[rows].T[:HEAD].astype(BF)

    for row in range(spans):
        cols = slice(row % 2 * SPAN, row % 2 * SPAN + SPAN)
        out[row // 2, :HEAD, cols] = (dq_t[:, at_span(deal[row])] * scale[...]).astype(BF)


def load_weights(info, own, direct, passed, wholes, sems):
    y, core = info[0], info[1]
    started = []
    count = 0
    for at, whole in enumerate(wholes):
        rows, part = own[at].shape[0], own[at].shape[0] // 2
        far = (1 - y) * rows
        places = [(own[at], y * rows)]
        for chunks, base in ((direct, far + core * part), (passed, far + (1 - core) * part)):
            start = 0
            for chunk in chunks:
                low, high = max(start, at * part), min(start + chunk.shape[0], at * part + part)
                if low < high:
                    places.append((chunk.at[pl.ds(low - start, high - low)], base + low - at * part))
                start += chunk.shape[0]
        copies = []
        for ref, start in places:
            target = whole.at[pl.ds(pl.multiple_of(start, 16), ref.shape[0])]
            copies.append(pltpu.make_async_copy(ref, target, sems.at[count]))
            copies[-1].start()
            count += 1
        started.append(copies)
    return started


def arrive(copies):
    for copy in copies:
        copy.wait()


def mlp_kernel(chunks, info, tokens, cotangent, attn_t, own, other, *refs):
    shards, direct, passed = refs[:3], refs[3 : 3 + chunks], refs[3 + chunks : 3 + 2 * chunks]
    refs = refs[3 + 2 * chunks :]
    outs = refs[:5]
    w_output, w_expand, w_contract, gain, right, sems = refs[5:]
    result, grad_mid_out, grad_attended_t, away, rights = outs
    y, core = info[0], info[1]
    loads = load_weights(info, shards, direct, passed, (w_output, w_expand, w_contract), sems)
    gain[:, half(y)] = own[6 * HEAD :].astype(F32)
    gain[:, half(1 - y)] = other[6 * HEAD :].astype(F32)
    gains = gain[1:2]
    attn = attn_t[...].T
    arrive(loads[0])
    mid = tokens[...].astype(F32) + mm(attn, w_output[...])
    rate = lax.rsqrt(jnp.mean(mid * mid, axis=-1, keepdims=True) + EPS)
    mlp_in = (mid * rate * gains).astype(BF)
    away[1] = mlp_in
    arrive(loads[1])
    expanded = mm(mlp_in, w_expand[...])
    gate = jax.nn.sigmoid(expanded)
    act = (expanded * gate).astype(BF)
    away[0] = act
    arrive(loads[2])
    result[...] = (mid + mm(act, w_contract[...])).astype(BF)
    grad_act = mm(cotangent[...], w_contract[...], NT)
    grad_expanded = (grad_act * gate * (1.0 + expanded * (1.0 - gate))).astype(BF)
    right[0] = grad_expanded
    grad_mlp_in = mm(grad_expanded, w_expand[...], NT) * gains
    inner = jnp.mean(grad_mlp_in * mid, axis=-1, keepdims=True)
    grad_mid = cotangent[...].astype(F32) + rate * grad_mlp_in - mid * (rate * rate * rate * inner)
    grad_mid_out[...] = grad_mid
    low = grad_mid.astype(BF)
    right[1] = low
    grad_attended_t[...] = mm(w_output[...], low, NT).astype(BF)
    for at in range(2):
        rights[:, at * 640 : at * 640 + 640] = right[at, :, half(core)]
        away[2, :, at * 640 : at * 640 + 640] = right[at, :, half(1 - core)]


BITS = ("y", "x", "far", "near")
ORDERS = (("y", "x", "near", "far"), ("x", "near", "y", "far"), ("near", "y", "x", "far"))
BIT_AT = {"y": 0, "x": 20, "near": 21, "far": 22}
PART = 80


def left_bits(order, done):
    return [name for name in BITS if name not in order[:done]]


def halves(info, order, done):
    left = left_bits(order, done)
    name = order[done]
    bit = info[BIT_AT[name]]
    stride = 1 << (len(left) - 1 - left.index(name))
    count = 1 << len(left)
    bases = [block for block in range(count) if block & stride == 0]
    return [(base + bit * stride, base + (1 - bit) * stride) for base in bases]


def rows_of(block):
    start = block * PART
    return pl.ds(start if isinstance(block, int) else pl.multiple_of(start, 16), PART)


def outer_kernel(info, own, rights, partner, attn_t, attn_t_partner, cot, cot_partner, *refs):
    outs, (left, right, full) = refs[:6], refs[6:]
    core = info[1]
    rows = cot.shape[0]
    for at in range(3):
        if at < 2:
            left[:, :rows] = own[at].T
            left[:, rows:] = partner[at].T
        else:
            left[:, :rows] = attn_t[...]
            left[:, rows:] = attn_t_partner[...]
        if at == 0:
            right[:rows] = cot[:, half(core)]
            right[rows:] = cot_partner[:, half(core)]
        else:
            cols = slice((at - 1) * 640, at * 640)
            right[:rows] = rights[:, cols]
            right[rows:] = partner[2, :, cols]
        full[...] = mm(left[...], right[...]).astype(BF)
        for to, (kept, sent) in enumerate(halves(info, ORDERS[at], 0)):
            outs[at][rows_of(to)] = full[rows_of(kept)]
            outs[3 + at][rows_of(to)] = full[rows_of(sent)]


def round_kernel(done, info, *refs):
    kept, came, outs = refs[:3], refs[3:6], refs[6:]
    for at in range(3):
        for to, (mine, theirs) in enumerate(halves(info, ORDERS[at], done)):
            if len(outs) == 6:
                stay, away, target = outs[at], outs[3 + at], rows_of(to)
            else:
                stay, away, target = outs[0], outs[1], rows_of(at)
            for out, block in ((stay, mine), (away, theirs)):
                total = kept[at][rows_of(block)].astype(F32) + came[at][rows_of(block)].astype(F32)
                out[target] = total.astype(BF)


def folded(products):
    return sum(products[:, at : at + 128] for at in range(0, products.shape[1], 128))


def row_sums(products):
    ones = jnp.ones((16, products.shape[1]), BF)
    high = products.astype(BF)
    low = (products - high.astype(F32)).astype(BF)
    return mm(ones, high, NT) + mm(ones, low, NT)


def stack_kernel(*refs):
    for at, ref in enumerate(refs[:-1]):
        refs[-1][at] = ref[...]


def joined(pieces, last):
    count = len(pieces) // 2
    ready = []
    for colour in range(2):
        group = pieces[colour * count : colour * count + count]
        cut = group[-2].shape[0]
        last[colour, :cut] = group[-2][...]
        last[colour, cut:] = group[-1][...]
        ready += [*group[:-2], last.at[colour]]
    return ready


def slot_of(at, count, first):
    return first + at if at < count else 8 + first + at - count


def scatter(info, refs, first, blocks, sems, outs, expand, sums):
    copies = []
    for at, ref in enumerate(refs):
        dev = info[4 + slot_of(at, len(refs) // 2, first)]
        block = ((dev // 2) % 2) * 4 + dev // 4
        rows = pl.ds(pl.multiple_of(block * PART, 16), PART)
        for way in range(3):
            blocks[3 * at + way] = ref[way * PART : (way + 1) * PART].astype(F32)
            target = outs[way].at[rows, half(dev % 2)]
            copies.append(pltpu.make_async_copy(blocks.at[3 * at + way], target, sems.at[3 * at + way]))
            copies[-1].start()
        sums[rows] += folded(blocks[3 * at + 1] * expand[rows, half(dev % 2)].astype(F32))
    return copies


def spread_kernel(info, near, near_partner, expand, sums, *refs):
    outs, (blocks, sems) = refs[:3], refs[3:]
    pieces = [stack.at[at] for stack in (near, near_partner) for at in range(5)]
    sums[...] = jnp.zeros_like(sums)
    arrive(scatter(info, pieces, 0, blocks, sems, outs, expand, sums))


def spread_last_kernel(info, *refs):
    pieces, (before, gain, expand), (*outs, grad_gain), refs = refs[:8], refs[8:11], refs[14:18], refs[18:]
    blocks, last, sums, sems = refs
    sums[...] = before[...]
    copies = scatter(info, joined(pieces, last), 5, blocks, sems, outs, expand, sums)
    size = sums.shape[0]
    grad_gain[...] = (row_sums(sums[...])[0:1] / gain[...].astype(F32)).reshape(size)
    arrive(copies)


def weight_kernel(info, grads, own, other, *refs):
    inputs = refs[:2]
    keep, away, lines, weight, total, gain_sums, attn_in, sems = refs[2:]
    y, core = info[0], info[1]
    rows = attn_in.shape[0] // 8
    loads = []
    for at in range(8):
        source = inputs[at // 4].at[pl.ds(at % 4 * rows, rows)]
        loads.append(pltpu.make_async_copy(source, attn_in.at[pl.ds(at * rows, rows)], sems.at[at]))
        loads[-1].start()
    for slot in range(16):
        lines[:, slot * 256 : slot * 256 + 256] = grads[info[4 + slot]]
    mine = pl.ds(pl.multiple_of(core * 3 * HEAD, 16), 3 * HEAD)
    weight[:, half(y)] = own[mine].astype(F32)
    weight[:, half(1 - y)] = other[mine].astype(F32)
    total[...] = jnp.zeros_like(total)
    for at in range(4):
        loads[2 * at].wait()
        loads[2 * at + 1].wait()
        part = slice(2 * at * rows, 2 * (at + 1) * rows)
        total[...] += mm(lines[:, part], attn_in[part])
    keep[: 3 * HEAD] = total[:, half(y)]
    away[: 3 * HEAD] = total[:, half(1 - y)].astype(BF)
    weight[...] *= total[...]
    scale_sums = row_sums(weight[:HEAD])[0:1]
    gain_sums[...] = jnp.sum(weight[...], axis=0, keepdims=True)
    line = lax.broadcasted_iota(jnp.int32, (16, keep.shape[1]), 0)
    keep[3 * HEAD :] = jnp.where(line == 1, gain_sums[:, half(y)], 0.0)
    away[3 * HEAD :] = jnp.where(line == 1, gain_sums[:, half(1 - y)], 0.0).astype(BF)
    keep[3 * HEAD : 3 * HEAD + 1, :HEAD] = scale_sums
    first = lax.broadcasted_iota(jnp.int32, (16, HEAD), 0) == 0
    behind = jnp.where(line == 1, gain_sums[:, half(1 - y)], 0.0)[:, :HEAD]
    away[3 * HEAD :, :HEAD] = jnp.where(first, scale_sums, behind).astype(BF)


def finish_kernel(info, near, near_partner, *refs):
    pieces, (gain, factor), outs, refs = refs[:8], refs[8:10], refs[10:13], refs[13:]
    grad_gain, grad_scale, stacks, last, turned, sems = refs
    extra = jnp.zeros((16, last.shape[2]), F32)
    early = [stack.at[at] for stack in (near, near_partner) for at in range(5)]
    for first, group in ((0, early), (5, joined(pieces, last))):
        for at, ref in enumerate(group):
            rows = pl.ds(pl.multiple_of(info[4 + slot_of(at, len(group) // 2, first)] * HEAD, 16), HEAD)
            for way in range(3):
                stacks[way, rows] = ref[way * HEAD : (way + 1) * HEAD]
            extra += ref[3 * HEAD :].astype(F32)
    grad_scale[...] = extra[0:1, :HEAD] * factor[...]
    size = turned.shape[1]
    grad_gain[...] = (extra[1:2] / gain[...].astype(F32)).reshape(size)
    same = lax.broadcasted_iota(jnp.int32, (size, size), 0) == lax.broadcasted_iota(jnp.int32, (size, size), 1)
    unit = jnp.where(same, 1.0, 0.0).astype(BF)
    copies = []
    for at, out in enumerate(outs):
        turned[at] = mm(unit, stacks[at], NT)
        copies.append(pltpu.make_async_copy(turned.at[at], out, sems.at[at]))
        copies[-1].start()
    arrive(copies)


def input_kernel(chunks, info, tokens, grads, grad_mid, own, other, *refs):
    shards, direct, passed = refs[:3], refs[3 : 3 + chunks], refs[3 + chunks : 3 + 2 * chunks]
    out, *weights, gain, sems = refs[3 + 2 * chunks :]
    y = info[0]
    loads = load_weights(info, shards, direct, passed, weights, sems)
    gain[:, half(y)] = own[6 * HEAD :].astype(F32)
    gain[:, half(1 - y)] = other[6 * HEAD :].astype(F32)
    heads, width = grads.shape[0], grads.shape[2]
    values = tokens[...].astype(F32)
    rate = lax.rsqrt(jnp.mean(values * values, axis=-1, keepdims=True) + EPS)
    turned_grad = None
    for at, ref in enumerate(weights):
        part = grads[:, at * HEAD : (at + 1) * HEAD, :].reshape(heads * HEAD, width)
        arrive(loads[at])
        product = mm(ref[...], part)
        turned_grad = product if turned_grad is None else turned_grad + product
    grad = turned_grad.T * gain[0:1]
    inner = jnp.mean(grad * values, axis=-1, keepdims=True)
    out[...] = (grad_mid[...] + rate * grad - values * (rate * rate * rate * inner)).astype(BF)


def after(values, *others):
    return lax.optimization_barrier((tuple(values), others))[0]


def weight_rows(shards, core):
    size = shards[0].shape[0] // 2
    return jnp.concatenate([lax.dynamic_slice_in_dim(shard, core * size, size, 0) for shard in shards], axis=0)


def ring_device(
    tokens, cotangent, deal, lengths, gain_attn, w_query, w_key, w_value, w_output, query_scale,
    gain_mlp, w_expand, w_contract
):
    rows, width = tokens.shape[1:]
    c, y = lax.axis_index("ctx"), lax.axis_index("wt")
    core, x, z = c % 2, (c // 2) % 2, c // 4
    table = lax.dynamic_index_in_dim(jnp.asarray(slot_table()), c, 0, keepdims=False)
    head = jnp.stack([y, core, c // 2, lengths[0, 0]]).astype(jnp.int32)
    info = jnp.concatenate([head, table, jnp.stack([x, z % 2, z // 2]).astype(jnp.int32)])
    dealt = deal[0]
    total = rows * 16
    softplus = jax.nn.softplus(query_scale)
    scale_col = (LOG2E / math.sqrt(HEAD) * softplus)[:, None]
    factor = (jax.nn.sigmoid(query_scale) / softplus)[None, :]
    inputs = tokens[0]
    cot = cotangent[0]
    cut = rows // 2
    mine, partner, gathered = [], [], []

    def project(other, *group):
        count = sum(part.shape[0] for part in group)
        start = sum(piece.shape[1] for piece in mine)
        args = [info, *group, own, other, scale_col]
        got = call(
            functools.partial(project_kernel, len(group), start),
            [((8 * rows, width), BF), ((3 * HEAD, count), BF), ((3 * HEAD, count), BF)],
            args + gathered[-1:],
            smem=1,
            anys=range(len(args), len(args) + 1),
            out_anys=(0,),
            aliases={len(args): 0} if gathered else None,
            scratch=[
                pltpu.VMEM((count, width), BF),
                pltpu.VMEM((6 * HEAD, width), BF),
                pltpu.VMEM((16, width), F32),
                pltpu.VMEM((6 * HEAD, count), BF),
                pltpu.SemaphoreType.DMA,
            ],
            cost=(2 * 480 * 1280 * count, 4 * 1280 * count, 0),
        )
        gathered.append(got[0])
        mine.append(got[1])
        partner.append(send(got[2], CORE_SWAP))
        return got[1]

    forth1, back1 = send(inputs, FORTH), send(inputs, BACK)
    size = width // 4
    first_rows = lax.dynamic_slice_in_dim(w_output, core * size, 128, 0)
    direct, passed = [send(first_rows, Y_SWAP)], []
    own = call(
        pick_kernel,
        [((6 * HEAD + 16, width // 2), BF)],
        [info, w_query, w_key, w_value, gain_attn[None], gain_mlp[None]],
        smem=1,
        cost=(2 * 480 * 640 * 1280, 3 * 640 * 1280 * 2, 0),
    )[0]
    other = send(own, Y_SWAP)
    forth1, back1, direct[0] = after((forth1, back1, direct[0]), own)

    forth2, back2 = send(forth1, FORTH), send(back1, BACK)
    rows_out = weight_rows(after((w_output, w_expand, w_contract), forth1), core)
    rows_back = weight_rows(after((w_query, w_key, w_value), forth1), core)
    chunks = [rows_out[128:448], rows_out[448:624], rows_out[624:]]
    chunks += [rows_back[:224], rows_back[224:384], rows_back[384:608], rows_back[608:]]
    passed.append(send(direct[0], CORE_SWAP))
    forth2, back2, other, passed[0], *chunks = after((forth2, back2, other, passed[0], *chunks))

    forth3, back3 = send(forth2, FORTH), send(back2, BACK)
    direct.append(send(after(chunks[:1], passed[0])[0], Y_SWAP))
    done = project(other, inputs)
    done = project(other, forth1, back1), done
    done = project(other, forth2, back2), done
    forth3, back3, direct[1] = after((forth3, back3, direct[1]), done)

    forth4, back4 = send(forth3[:cut], FORTH), send(back3[cut:], BACK)
    passed.append(send(direct[1], CORE_SWAP))
    direct.append(send(after(chunks[1:2], direct[1])[0], Y_SWAP))
    done = project(other, forth3, back3)
    forth4, back4, direct[2], passed[1] = after((forth4, back4, direct[2], passed[1]), done)
    passed.append(send(direct[2], CORE_SWAP))
    direct.append(send(after(chunks[2:3], direct[2])[0], Y_SWAP))
    project(other, forth4, back4)
    *spans, passed[2] = after((*mine, *partner, passed[2]))

    tall, flat_t = ((total, WIDE), BF), ((WIDE, total), BF)
    attended, q_t, k_n = call(
        forward_kernel,
        [((16, HEAD, rows), BF), flat_t, tall],
        [info, dealt, *spans],
        smem=2,
        scratch=[
            pltpu.VMEM((HEAD + 16, total), BF),
            pltpu.VMEM((1, total), F32),
            pltpu.SMEM((total // SPAN,), jnp.int32),
        ],
        cost=(2 * total * total * 256, 3 * total * 160, total * total // 2),
    )
    attended, direct[3] = after((attended, direct[3]))
    passed.append(send(direct[3], CORE_SWAP))
    direct_back = [send(after(chunks[3:4], direct[3])[0], Y_SWAP)]
    attn_in = gathered[-1]
    attn_in_partner, cot_partner = (send(value, CORE_SWAP) for value in after((attn_in, cot), attended))
    attn_t = lax.all_to_all(attended, "ctx", 0, 0).reshape(width, rows)
    k_t, q_n, v_n = call(
        turn_kernel,
        [((HEAD, total), BF), tall, tall],
        [info, dealt, *after(spans, attended)],
        smem=2,
        cost=(0, 6 * total * 256, 0),
    )
    attn_t, passed[3], attn_in_partner, cot_partner, direct_back[0] = after(
        (attn_t, passed[3], attn_in_partner, cot_partner, direct_back[0]), k_t
    )
    direct_back.append(send(after(chunks[4:5], attn_t)[0], Y_SWAP))
    whole_scratch = [pltpu.VMEM((width, width), BF)] * 3 + [pltpu.VMEM((16, width), F32)]
    wide, low = ((rows, width), F32), ((rows, width), BF)
    result, grad_mid, grad_attended_t, packed, rights = call(
        functools.partial(mlp_kernel, 4),
        [low, wide, ((width, rows), BF), ((3, rows, width), BF), low],
        [info, inputs, cot, attn_t, own, other, w_output, w_expand, w_contract, *direct, *passed],
        smem=1,
        anys=range(6, 17),
        scratch=whole_scratch + [pltpu.VMEM((2, rows, width), BF), pltpu.SemaphoreType.DMA((24,))],
        cost=(12 * rows * width * width, 6 * width * width, 0),
    )
    grad_attended_t, packed, direct_back[1] = after((grad_attended_t, packed, direct_back[1]))
    grad_out = lax.all_to_all(grad_attended_t.reshape(16, HEAD, rows), "ctx", 0, 0)
    packed_partner = send(packed, CORE_SWAP)
    direct_back.append(send(after(chunks[5:6], packed)[0], Y_SWAP))
    attn_t_partner = send(attn_t, CORE_SWAP)

    half_width = width // 2
    terms = call(
        outer_kernel,
        [((half_width, half_width), BF)] * 6,
        [info, packed, rights, packed_partner, attn_t, attn_t_partner, cot, cot_partner],
        smem=1,
        scratch=[
            pltpu.VMEM((width, 2 * rows), BF),
            pltpu.VMEM((2 * rows, half_width), BF),
            pltpu.VMEM((width, half_width), BF),
        ],
        cost=(6 * rows * width * width, 6 * width * width, 0),
    )
    moves = {"y": Y_SWAP, "x": X_SWAP, "near": NEAR_SWAP, "far": FAR_SWAP}

    def travel(values, done):
        return [send(value, moves[order[done]]) for value, order in zip(values, ORDERS)]

    def halving(kept, came, done):
        size = half_width >> done
        shapes = [((size, half_width), BF)] * 6 if done < 3 else [((3 * PART, half_width), BF)] * 2
        return call(
            functools.partial(round_kernel, done),
            shapes,
            [info, *kept, *came],
            smem=1,
            cost=(0, 12 * size * half_width, 0),
        )

    came = travel(terms[3:], 0)
    kept = terms[:3]
    grad_out, direct_back[2] = after((grad_out, direct_back[2]), kept[0])
    grads = call(
        backward_kernel,
        [((16, 3 * HEAD, rows), BF)],
        [info, dealt, q_t, k_n, k_t, q_n, v_n, attended, grad_out, scale_col],
        smem=2,
        scratch=[
            pltpu.VMEM((WIDE, total), BF),
            pltpu.VMEM((total, WIDE), BF),
            pltpu.VMEM((1, total), F32),
            pltpu.VMEM((HEAD, total), F32),
            pltpu.VMEM((BLOCK, WIDE), F32),
            pltpu.VMEM((BLOCK, WIDE), F32),
            pltpu.SMEM((total // SPAN,), jnp.int32),
        ],
        cost=(5 * total * total * 256, 6 * total * 160, total * total // 2),
    )[0]
    grads, *came = after((grads, *came))
    returned = lax.all_to_all(grads, "ctx", 0, 0)
    keep, away = call(
        weight_kernel,
        [((256, half_width), F32), ((256, half_width), BF)],
        [info, grads, own, other, attn_in, attn_in_partner],
        smem=1,
        anys=(4, 5),
        scratch=[
            pltpu.VMEM((3 * HEAD, total), BF),
            pltpu.VMEM((3 * HEAD, width), F32),
            pltpu.VMEM((3 * HEAD, width), F32),
            pltpu.VMEM((1, width), F32),
            pltpu.VMEM((total, width), BF),
            pltpu.SemaphoreType.DMA((8,)),
        ],
        cost=(2 * 240 * total * width, 2 * total * width, 0),
    )
    from_pair = send(away, Y_SWAP)
    terms = halving(kept, after(came, keep), 1)
    kept, came = terms[:3], travel(terms[3:], 1)
    keep = after((keep,), kept[0])[0]
    summed = (keep + from_pair.astype(F32)).astype(BF)
    passed_back = [send(value, CORE_SWAP) for value in after(direct_back, summed)]
    direct_back.append(send(after(chunks[6:], summed)[0], Y_SWAP))

    shard = ((half_width, width), F32)
    line = ((half_width,), F32)

    def stacked(values):
        stack = call(stack_kernel, [((len(values), *values[0].shape), BF)], values)[0]
        return stack, send(stack, CORE_SWAP)

    forth1, back1 = send(summed, FORTH), send(summed, BACK)
    forth2, back2 = send(forth1, FORTH), send(back1, BACK)
    terms = halving(kept, after(came, forth1), 2)
    kept, came = terms[:3], travel(terms[3:], 2)
    forth2, back2, direct_back[3] = after((forth2, back2, direct_back[3]), kept[0], returned, *passed_back)
    passed_back.append(send(direct_back[3], CORE_SWAP))
    forth3, back3 = send(forth2, FORTH), send(back2, BACK)
    near, near_partner = stacked([*after((summed, forth1, back1, forth2, back2), *came)])
    terms = halving(kept, came, 3)
    far = send(terms[1], FAR_SWAP)
    forth3, back3 = after((forth3, back3), terms[0])
    last = [send(forth3[:128], FORTH), send(back3[128:], BACK)]
    beyond = [send(value, CORE_SWAP) for value in (forth3, back3)]
    piece = (terms[0].astype(F32) + far.astype(F32)).astype(BF)
    grad_inputs = call(
        functools.partial(input_kernel, 4),
        [low],
        [info, inputs, returned, grad_mid, own, other, w_query, w_key, w_value, *direct_back, *passed_back],
        smem=1,
        anys=range(6, 17),
        scratch=whole_scratch + [pltpu.SemaphoreType.DMA((24,))],
        cost=(6 * rows * width * width, 6 * width * width, 0),
    )[0]
    last = after(last, *beyond, grad_inputs, near_partner)
    piece = after((piece,), last[0])[0]
    query_pieces = [near, near_partner, forth3, back3, *last, *beyond, *(send(value, CORE_SWAP) for value in last)]

    forth1, back1 = send(piece, FORTH), send(piece, BACK)
    grad_query, grad_key, grad_value, grad_gain_attn, grad_scale = call(
        finish_kernel,
        [shard] * 3 + [line, ((1, HEAD), F32)],
        [info, *query_pieces, gain_attn[None], factor],
        smem=1,
        out_anys=range(3),
        scratch=[
            pltpu.VMEM((3, width, half_width), BF),
            pltpu.VMEM((2, 256, half_width), BF),
            pltpu.VMEM((3, half_width, width), F32),
            pltpu.SemaphoreType.DMA((3,)),
        ],
        cost=(6 * 640 * 640 * 1280, 3 * 640 * 1280 * 4, 0),
    )
    forth1, back1 = after((forth1, back1), grad_query)
    forth2, back2 = send(forth1, FORTH), send(back1, BACK)
    forth3, back3 = send(forth2, FORTH), send(back2, BACK)
    near, near_partner = stacked([piece, forth1, back1, forth2, back2])
    partial_out = call(
        spread_kernel,
        [((half_width, 128), F32), shard, shard, shard],
        [info, near, near_partner, w_expand],
        smem=1,
        out_anys=(1, 2, 3),
        scratch=[pltpu.VMEM((30, PART, half_width), F32), pltpu.SemaphoreType.DMA((30,))],
        cost=(0, 3 * 640 * 1280 * 4, 0),
    )
    forth3, back3 = after((forth3, back3), partial_out[0])
    last = [send(forth3[:112], FORTH), send(back3[112:], BACK)]
    beyond = [send(value, CORE_SWAP) for value in (forth3, back3)]
    last = after(last, *beyond)
    args = [info, forth3, back3, *last, *beyond, *(send(value, CORE_SWAP) for value in last)]
    args += [partial_out[0], gain_mlp[None], w_expand, *partial_out[1:]]
    grad_contract, grad_expand, grad_output, grad_gain_mlp = call(
        spread_last_kernel,
        [shard] * 3 + [line],
        args,
        smem=1,
        anys=range(len(args) - 3, len(args)),
        out_anys=range(3),
        aliases={len(args) - 3 + at: at for at in range(3)},
        scratch=[
            pltpu.VMEM((18, PART, half_width), F32),
            pltpu.VMEM((2, *piece.shape), BF),
            pltpu.VMEM((half_width, 128), F32),
            pltpu.SemaphoreType.DMA((18,)),
        ],
        cost=(0, 3 * 640 * 1280 * 4, 0),
    )
    return (
        result[None], grad_inputs[None], grad_gain_attn, grad_query, grad_key, grad_value, grad_output,
        grad_scale[0], grad_gain_mlp, grad_expand, grad_contract,
    )


def solution(mesh):
    in_specs = (
        P("wt", "ctx", None),
        P("wt", "ctx", None),
        P("wt", None),
        P("wt", None),
        P("wt"),
        P("wt", None),
        P("wt", None),
        P("wt", None),
        P("wt", None),
        P(),
        P("wt"),
        P("wt", None),
        P("wt", None),
    )
    out_specs = (
        P("wt", "ctx", None),
        P("wt", "ctx", None),
        P("wt"),
        P("wt", None),
        P("wt", None),
        P("wt", None),
        P("wt", None),
        P(),
        P("wt"),
        P("wt", None),
        P("wt", None),
    )
    body = ring_device if mesh.shape["ctx"] == HEADS and mesh.shape["wt"] == 2 else per_device
    return jax.shard_map(
        body, mesh=mesh, in_specs=in_specs, out_specs=out_specs, check_vma=False
    )
```

```python
import functools
import math

import jax
import jax.numpy as jnp
import numpy as np
from jax import lax
from jax.experimental import pallas as pl
from jax.experimental.pallas import tpu as pltpu
from jax.sharding import PartitionSpec as P

HEADS = 16
HEAD = 80
SPAN = 128
LONGEST = 4096


EPS = 1e-06
LOG2E = 1.442695041
NEG = -1e30


def normed(values, gain):
    return values * lax.rsqrt(jnp.mean(values * values, axis=-1, keepdims=True) + EPS) * gain


def locate(dealt_spans, seq_lengths, offset, count, slot_tokens):
    row_ids = offset + jnp.arange(count, dtype=jnp.int32)
    slot_ids = row_ids // SPAN
    matches = slot_ids[:, None] == jnp.arange(dealt_spans.shape[0], dtype=jnp.int32)[None, :]
    span_ids = jnp.sum(jnp.where(matches, dealt_spans[None, :], 0), axis=1)
    natural = span_ids * SPAN + row_ids % SPAN
    sequence = natural // slot_tokens
    position = natural % slot_tokens
    owners = sequence[:, None] == jnp.arange(seq_lengths.shape[0], dtype=jnp.int32)[None, :]
    limits = jnp.sum(jnp.where(owners, seq_lengths[None, :], 0), axis=1)
    return (sequence, position, position < limits)


def permitted(query_place, key_place):
    same_seq = query_place[0][:, None] == key_place[0][None, :]
    causal = key_place[1][None, :] <= query_place[1][:, None]
    return (same_seq & causal & key_place[2][None, :])[None]


def per_device(
    tokens,
    cotangent,
    deal,
    lengths,
    gain_attn,
    w_query,
    w_key,
    w_value,
    w_output,
    query_scale,
    gain_mlp,
    w_expand,
    w_contract,
):
    row_count = tokens.shape[1]
    feat_width = tokens.shape[2]
    group_rows = row_count * lax.axis_size("ctx")
    slot_tokens = min(LONGEST, group_rows)
    block_rows = min(512, group_rows)
    blocks = group_rows // block_rows
    dealt_spans = deal[0]
    seq_lengths = lengths[0]
    inputs = tokens[0].astype(jnp.float32)
    shards = (gain_attn, w_query, w_key, w_value, w_output, gain_mlp, w_expand, w_contract)
    gathered = (
        lax.all_gather(shards[0], "wt", axis=0, tiled=True),
        lax.all_gather(shards[1], "wt", axis=0, tiled=True),
        lax.all_gather(shards[2], "wt", axis=0, tiled=True),
        lax.all_gather(shards[3], "wt", axis=0, tiled=True),
        lax.all_gather(shards[4], "wt", axis=0, tiled=True),
        lax.all_gather(shards[5], "wt", axis=0, tiled=True),
        lax.all_gather(shards[6], "wt", axis=0, tiled=True),
        lax.all_gather(shards[7], "wt", axis=0, tiled=True),
    )
    gain_one = gathered[0].astype(jnp.float32)
    gain_two = gathered[5].astype(jnp.float32)
    query_place = locate(
        dealt_spans, seq_lengths, lax.axis_index("ctx") * row_count, row_count, slot_tokens
    )
    scale_row = LOG2E / math.sqrt(HEAD) * jax.nn.softplus(query_scale)
    attn_in = normed(inputs, gain_one).astype(jnp.bfloat16)
    query_lin = jnp.dot(attn_in, gathered[1], preferred_element_type=jnp.float32)
    queries = (query_lin.reshape(row_count, HEADS, HEAD) * scale_row).astype(jnp.bfloat16)
    key_own = jnp.dot(attn_in, gathered[2], preferred_element_type=jnp.float32).astype(jnp.bfloat16)
    value_own = jnp.dot(attn_in, gathered[3], preferred_element_type=jnp.float32).astype(
        jnp.bfloat16
    )
    portion = (
        lax.all_gather(key_own, "ctx", axis=0, tiled=True),
        lax.all_gather(value_own, "ctx", axis=0, tiled=True),
    )
    running = jnp.full((HEADS, row_count), NEG, jnp.float32)
    count = portion[0].shape[0]
    key_rows = portion[0].reshape(count, HEADS, HEAD)
    value_rows = portion[1].reshape(count, HEADS, HEAD)
    permit_mask = permitted(
        query_place, locate(dealt_spans, seq_lengths, jnp.int32(0), count, slot_tokens)
    )
    scores = jnp.einsum("qhd,khd->hqk", queries, key_rows, preferred_element_type=jnp.float32)
    scores = jnp.where(permit_mask, scores, NEG)
    newest = jnp.maximum(running, jnp.max(scores, axis=-1))
    weights = jnp.where(permit_mask, jnp.exp(scores - newest[..., None]), 0.0)
    running_total = jnp.sum(weights, axis=-1)
    update = jnp.einsum(
        "hqk,khd->qhd", weights.astype(jnp.bfloat16), value_rows, preferred_element_type=jnp.float32
    )
    summed = update
    running, running_total, summed = (newest, running_total, summed)
    log_norm = running + jnp.log(running_total)
    attended = summed / jnp.transpose(running_total)[:, :, None]
    attn_out = attended.reshape(row_count, feat_width).astype(jnp.bfloat16)
    mid = inputs + jnp.dot(attn_out, gathered[4], preferred_element_type=jnp.float32)
    mlp_in = normed(mid, gain_two).astype(jnp.bfloat16)
    expanded = jnp.dot(mlp_in, gathered[6], preferred_element_type=jnp.float32)
    activated = jax.nn.silu(expanded).astype(jnp.bfloat16)
    result = mid + jnp.dot(activated, gathered[7], preferred_element_type=jnp.float32)
    weights_back = (
        lax.all_gather(shards[0], "wt", axis=0, tiled=True),
        lax.all_gather(shards[1], "wt", axis=0, tiled=True),
        lax.all_gather(shards[2], "wt", axis=0, tiled=True),
        lax.all_gather(shards[3], "wt", axis=0, tiled=True),
        lax.all_gather(shards[4], "wt", axis=0, tiled=True),
        lax.all_gather(shards[5], "wt", axis=0, tiled=True),
        lax.all_gather(shards[6], "wt", axis=0, tiled=True),
        lax.all_gather(shards[7], "wt", axis=0, tiled=True),
    )
    whole_keys, whole_values = (
        lax.all_gather(key_own, "ctx", axis=0, tiled=True),
        lax.all_gather(value_own, "ctx", axis=0, tiled=True),
    )
    grad_result = cotangent[0].astype(jnp.float32)
    grad_branch = grad_result.astype(jnp.bfloat16)
    grad_contract = jnp.einsum(
        "tf,td->fd", activated, grad_branch, preferred_element_type=jnp.float32
    )
    grad_act = jnp.einsum(
        "td,fd->tf", grad_branch, weights_back[7], preferred_element_type=jnp.float32
    )
    sigmoid_gate = jax.nn.sigmoid(expanded)
    grad_expanded = (grad_act * sigmoid_gate * (1.0 + expanded * (1.0 - sigmoid_gate))).astype(
        jnp.bfloat16
    )
    grad_expand = jnp.einsum("td,tf->df", mlp_in, grad_expanded, preferred_element_type=jnp.float32)
    grad_mlp_in = jnp.einsum(
        "tf,df->td", grad_expanded, weights_back[6], preferred_element_type=jnp.float32
    )
    unused_two, pull_two = jax.vjp(normed, mid, gain_two)
    grad_mid_norm, grad_gain_two = pull_two(grad_mlp_in)
    grad_mid = grad_result + grad_mid_norm
    grad_mid_low = grad_mid.astype(jnp.bfloat16)
    grad_output_w = jnp.einsum(
        "td,te->de", attn_out, grad_mid_low, preferred_element_type=jnp.float32
    )
    grad_attended = jnp.einsum(
        "te,de->td", grad_mid_low, weights_back[4], preferred_element_type=jnp.float32
    ).astype(jnp.bfloat16)
    out_grad = grad_attended.reshape(row_count, HEADS, HEAD)
    delta = jnp.transpose(jnp.sum(out_grad.astype(jnp.float32) * attended, axis=-1))
    key_blocks = (
        jnp.arange(blocks, dtype=jnp.int32),
        whole_keys.reshape(blocks, block_rows, feat_width),
        whole_values.reshape(blocks, block_rows, feat_width),
    )
    query_zero = jnp.zeros((row_count, HEADS, HEAD), jnp.float32)

    def back_block(query_grad, block_in):
        offset = block_in[0] * block_rows
        key_rows = block_in[1].reshape(block_rows, HEADS, HEAD)
        value_rows = block_in[2].reshape(block_rows, HEADS, HEAD)
        permit_mask = permitted(
            query_place, locate(dealt_spans, seq_lengths, offset, block_rows, slot_tokens)
        )
        scores = jnp.einsum("qhd,khd->hqk", queries, key_rows, preferred_element_type=jnp.float32)
        probabilities = jnp.where(permit_mask, jnp.exp(scores - log_norm[..., None]), 0.0)
        value_grad = jnp.einsum(
            "hqk,qhd->khd",
            probabilities.astype(jnp.bfloat16),
            out_grad,
            preferred_element_type=jnp.float32,
        )
        prob_grad = jnp.einsum(
            "qhd,khd->hqk", out_grad, value_rows, preferred_element_type=jnp.float32
        )
        score_grad = (probabilities * (prob_grad - delta[..., None])).astype(jnp.bfloat16)
        query_grad = query_grad + jnp.einsum(
            "hqk,khd->qhd", score_grad, key_rows, preferred_element_type=jnp.float32
        )
        key_grad = jnp.einsum(
            "hqk,qhd->khd", score_grad, queries, preferred_element_type=jnp.float32
        )
        return (
            query_grad,
            (key_grad.reshape(block_rows, feat_width), value_grad.reshape(block_rows, feat_width)),
        )

    query_grad, key_terms = lax.scan(back_block, query_zero, key_blocks)
    key_sum, value_sum = (
        lax.psum_scatter(
            key_terms[0].reshape(group_rows, feat_width).astype(jnp.bfloat16),
            "ctx",
            scatter_dimension=0,
            tiled=True,
        ).astype(jnp.float32),
        lax.psum_scatter(
            key_terms[1].reshape(group_rows, feat_width).astype(jnp.bfloat16),
            "ctx",
            scatter_dimension=0,
            tiled=True,
        ).astype(jnp.float32),
    )
    grad_keys = key_sum.astype(jnp.bfloat16)
    grad_values = value_sum.astype(jnp.bfloat16)
    grad_query_lin = (query_grad * scale_row).reshape(row_count, feat_width).astype(jnp.bfloat16)
    grad_scale = (
        jnp.sum(query_grad * query_lin.reshape(row_count, HEADS, HEAD), axis=(0, 1))
        * (LOG2E / math.sqrt(HEAD))
        * jax.nn.sigmoid(query_scale)
    )
    grad_query_w = jnp.einsum(
        "td,te->de", attn_in, grad_query_lin, preferred_element_type=jnp.float32
    )
    grad_key_w = jnp.einsum("td,te->de", attn_in, grad_keys, preferred_element_type=jnp.float32)
    grad_value_w = jnp.einsum("td,te->de", attn_in, grad_values, preferred_element_type=jnp.float32)
    grad_attn_in = jnp.einsum(
        "te,de->td", grad_query_lin, weights_back[1], preferred_element_type=jnp.float32
    )
    grad_attn_in = grad_attn_in + jnp.einsum(
        "te,de->td", grad_keys, weights_back[2], preferred_element_type=jnp.float32
    )
    grad_attn_in = grad_attn_in + jnp.einsum(
        "te,de->td", grad_values, weights_back[3], preferred_element_type=jnp.float32
    )
    unused_one, pull_one = jax.vjp(normed, inputs, gain_one)
    grad_in_norm, grad_gain_one = pull_one(grad_attn_in)
    grad_inputs = (grad_mid + grad_in_norm).astype(jnp.bfloat16)
    terms = (
        grad_gain_one,
        grad_query_w,
        grad_key_w,
        grad_value_w,
        grad_output_w,
        jnp.tile(grad_scale, lax.axis_size("wt")),
        grad_gain_two,
        grad_expand,
        grad_contract,
    )
    shares = (
        lax.psum_scatter(
            terms[0].astype(jnp.bfloat16), "wt", scatter_dimension=0, tiled=True
        ).astype(jnp.float32),
        lax.psum_scatter(
            terms[1].astype(jnp.bfloat16), "wt", scatter_dimension=0, tiled=True
        ).astype(jnp.float32),
        lax.psum_scatter(
            terms[2].astype(jnp.bfloat16), "wt", scatter_dimension=0, tiled=True
        ).astype(jnp.float32),
        lax.psum_scatter(
            terms[3].astype(jnp.bfloat16), "wt", scatter_dimension=0, tiled=True
        ).astype(jnp.float32),
        lax.psum_scatter(
            terms[4].astype(jnp.bfloat16), "wt", scatter_dimension=0, tiled=True
        ).astype(jnp.float32),
        lax.psum_scatter(
            terms[5].astype(jnp.bfloat16), "wt", scatter_dimension=0, tiled=True
        ).astype(jnp.float32),
        lax.psum_scatter(
            terms[6].astype(jnp.bfloat16), "wt", scatter_dimension=0, tiled=True
        ).astype(jnp.float32),
        lax.psum_scatter(
            terms[7].astype(jnp.bfloat16), "wt", scatter_dimension=0, tiled=True
        ).astype(jnp.float32),
        lax.psum_scatter(
            terms[8].astype(jnp.bfloat16), "wt", scatter_dimension=0, tiled=True
        ).astype(jnp.float32),
    )
    totals = (
        lax.psum(shares[0].astype(jnp.bfloat16), "ctx").astype(jnp.float32),
        lax.psum(shares[1].astype(jnp.bfloat16), "ctx").astype(jnp.float32),
        lax.psum(shares[2].astype(jnp.bfloat16), "ctx").astype(jnp.float32),
        lax.psum(shares[3].astype(jnp.bfloat16), "ctx").astype(jnp.float32),
        lax.psum(shares[4].astype(jnp.bfloat16), "ctx").astype(jnp.float32),
        lax.psum(shares[5].astype(jnp.bfloat16), "ctx").astype(jnp.float32),
        lax.psum(shares[6].astype(jnp.bfloat16), "ctx").astype(jnp.float32),
        lax.psum(shares[7].astype(jnp.bfloat16), "ctx").astype(jnp.float32),
        lax.psum(shares[8].astype(jnp.bfloat16), "ctx").astype(jnp.float32),
    )
    return (
        result.astype(jnp.bfloat16)[None],
        grad_inputs[None],
        totals[0],
        totals[1],
        totals[2],
        totals[3],
        totals[4],
        totals[5],
        totals[6],
        totals[7],
        totals[8],
    )


BF = jnp.bfloat16
F32 = jnp.float32
NN = (((1,), (0,)), ((), ()))
NT = (((1,), (1,)), ((), ()))
AXES = ("ctx", "wt")
LIMIT = 56 * 1024 * 1024

RING = ((0, 0), (1, 0), (2, 0), (3, 0), (3, 1), (2, 1), (1, 1), (0, 1))
PLACE = {chip: at for at, chip in enumerate(RING)}
OFFSETS = (0, -1, 1, -2, 2, -3, 3, 4)


def flat(z, x, core, y):
    return ((z * 2 + x) * 2 + core) * 2 + y


def pairs(move):
    return [
        (flat(z, x, core, y), flat(*move(z, x, core, y)))
        for z in range(4)
        for x in range(2)
        for core in range(2)
        for y in range(2)
    ]


def turned(by):
    def move(z, x, core, y):
        return (*RING[(PLACE[(z, x)] + by) % 8], core, y)

    return move


CORE_SWAP = pairs(lambda z, x, core, y: (z, x, 1 - core, y))
Y_SWAP = pairs(lambda z, x, core, y: (z, x, core, 1 - y))
X_SWAP = pairs(lambda z, x, core, y: (z, 1 - x, core, y))
NEAR_SWAP = pairs(lambda z, x, core, y: (z ^ 1, x, core, y))
FAR_SWAP = pairs(lambda z, x, core, y: (z ^ 2, x, core, y))
FORTH = pairs(turned(1))
BACK = pairs(turned(-1))


def slot_table():
    rows = []
    for c in range(16):
        z, x, core = c // 4, (c // 2) % 2, c % 2
        chips = [RING[(PLACE[(z, x)] + by) % 8] for by in OFFSETS]
        own = [(a * 2 + b) * 2 + core for a, b in chips]
        rows.append(own + [dev ^ 1 for dev in own])
    return np.asarray(rows, np.int32)


def send(value, moves):
    return lax.ppermute(value, AXES, moves)


def mm(left, right, dims=NN):
    return lax.dot_general(left, right, dims, preferred_element_type=F32)


def call(body, outs, args, smem=0, anys=(), scratch=(), cost=None, out_anys=(), aliases=None):
    whole, anywhere = pl.BlockSpec(memory_space=pltpu.VMEM), pl.BlockSpec(memory_space=pl.ANY)
    specs = [pl.BlockSpec(memory_space=pltpu.SMEM)] * smem
    specs += [anywhere if at in anys else whole for at in range(smem, len(args))]
    estimate = None
    if cost is not None:
        estimate = pl.CostEstimate(flops=int(cost[0]), bytes_accessed=int(cost[1]), transcendentals=int(cost[2]))
    return pl.pallas_call(
        body,
        out_shape=[jax.ShapeDtypeStruct(shape, kind) for shape, kind in outs],
        in_specs=specs,
        out_specs=[anywhere if at in out_anys else whole for at in range(len(outs))],
        scratch_shapes=list(scratch),
        input_output_aliases=aliases or {},
        cost_estimate=estimate,
        compiler_params=pltpu.CompilerParams(vmem_limit_bytes=LIMIT),
    )(*args)


def half(y, width=640):
    return pl.ds(pl.multiple_of(y * width, 128), width)


def pick_kernel(info, wq, wk, wv, gain_a, gain_m, out):
    chip = info[2]
    cols = lax.broadcasted_iota(jnp.int32, (2 * HEAD, wq.shape[1]), 1)
    rows = lax.broadcasted_iota(jnp.int32, (2 * HEAD, wq.shape[1]), 0)
    chosen = jnp.where(cols == rows + chip * (2 * HEAD), 1.0, 0.0).astype(BF)
    for at, ref in enumerate((wq, wk, wv)):
        both = mm(chosen, ref[...], NT).astype(BF)
        out[at * HEAD : (at + 1) * HEAD] = both[:HEAD]
        out[3 * HEAD + at * HEAD : 3 * HEAD + (at + 1) * HEAD] = both[HEAD:]
    line = lax.broadcasted_iota(jnp.int32, (16, gain_a.shape[1]), 0)
    tail = jnp.where(line == 0, gain_a[...].astype(F32), 0.0)
    tail = jnp.where(line == 1, gain_m[...].astype(F32), tail)
    out[6 * HEAD :] = tail.astype(BF)


def project_kernel(count, start, info, *refs):
    xs = refs[:count]
    own, other, scale = refs[count : count + 3]
    whole, mine, partner, attn_in, weight, gain, lines, sem = refs[-8:]
    y, core = info[0], info[1]
    weight[:, half(y)] = own[: 6 * HEAD]
    weight[:, half(1 - y)] = other[: 6 * HEAD]
    gain[:, half(y)] = own[6 * HEAD :].astype(F32)
    gain[:, half(1 - y)] = other[6 * HEAD :].astype(F32)
    row = 0
    for ref in xs:
        values = ref[...].astype(F32)
        scaled = values * lax.rsqrt(jnp.mean(values * values, axis=-1, keepdims=True) + EPS)
        attn_in[row : row + ref.shape[0]] = (scaled * gain[0:1]).astype(BF)
        row += ref.shape[0]
    copy = pltpu.make_async_copy(attn_in, whole.at[pl.ds(start, row)], sem)
    copy.start()
    lin = mm(weight[...], attn_in[...], NT)
    for head in range(2):
        base = head * 3 * HEAD
        lines[base : base + HEAD] = (lin[base : base + HEAD] * scale[...]).astype(BF)
        lines[base + HEAD : base + 3 * HEAD] = lin[base + HEAD : base + 3 * HEAD].astype(BF)
    mine[...] = lines[pl.ds(pl.multiple_of(core * 3 * HEAD, 16), 3 * HEAD)]
    partner[...] = lines[pl.ds(pl.multiple_of((1 - core) * 3 * HEAD, 16), 3 * HEAD)]
    copy.wait()


def span_slots(pieces):
    return [(ref, col) for ref in pieces for col in range(0, ref.shape[1], SPAN)]


def natural_span(info, deal, slot):
    return deal[2 * info[4 + slot // 2] + slot % 2]


def at_span(span):
    return pl.ds(pl.multiple_of(span * SPAN, SPAN), SPAN)


BLOCK = 1024
WIDE = 128


def block_at(at):
    return pl.ds(pl.multiple_of(at * BLOCK, BLOCK), BLOCK)


def in_parts(line):
    high = line.astype(BF)
    rest = line - high.astype(F32)
    middle = rest.astype(BF)
    low = (rest - middle.astype(F32)).astype(BF)
    at = lax.broadcasted_iota(jnp.int32, (16, line.shape[1]), 0)
    rows = jnp.where(at == 0, high.astype(F32), 0.0)
    rows = jnp.where(at == 1, middle.astype(F32), rows)
    return jnp.where(at == 2, low.astype(F32), rows).astype(BF)


def ones_behind(ref):
    at = lax.broadcasted_iota(jnp.int32, ref.shape, 1)
    ref[...] = jnp.where((at >= HEAD) & (at < HEAD + 3), 1.0, 0.0).astype(BF)


def forward_kernel(info, deal, *refs):
    pieces = refs[:10]
    out, queries, keys, values, lse, dealt = refs[10:]
    total = queries.shape[1]
    length = info[3]
    spans = total // SPAN
    blocks = total // BLOCK

    @pl.loop(0, spans)
    def _(at):
        dealt[deal[at]] = at

    line = lax.broadcasted_iota(jnp.int32, (16, total), 0)
    values[HEAD:] = jnp.where(line == 0, 1.0, 0.0).astype(BF)
    queries[HEAD:] = jnp.zeros((WIDE - HEAD, total), BF)
    ones_behind(keys)
    longest = jnp.zeros((1, SPAN), F32)
    for slot, (ref, col) in enumerate(span_slots(pieces)):
        where = at_span(natural_span(info, deal, slot))
        key = ref[HEAD : 2 * HEAD, col : col + SPAN]
        queries[:HEAD, where] = ref[:HEAD, col : col + SPAN]
        keys[where, :HEAD] = key.T
        values[:HEAD, where] = ref[2 * HEAD :, col : col + SPAN]
        sizes = key.astype(F32)
        longest = jnp.maximum(longest, jnp.sum(sizes * sizes, axis=0, keepdims=True))
    longest = jnp.max(longest, axis=1, keepdims=True)

    key_at = lax.broadcasted_iota(jnp.int32, (BLOCK, BLOCK), 0)
    query_at = lax.broadcasted_iota(jnp.int32, (BLOCK, BLOCK), 1)

    def scores_of(masked, i, j):
        scores = mm(keys[block_at(j), :], queries[:, block_at(i)])
        if masked:
            key_pos = j * BLOCK + key_at
            allowed = (key_pos <= i * BLOCK + query_at) & (key_pos < length)
            scores = jnp.where(allowed, scores, NEG)
        return scores

    def finish(i, peak, acc):
        here = block_at(i)
        norm = acc[HEAD : HEAD + 1]
        lse[:, here] = peak + jnp.log(norm)
        attended = (acc[:HEAD] / norm).astype(BF)
        for part in range(BLOCK // SPAN):
            row = dealt[i * (BLOCK // SPAN) + part]
            out[row // 2, :, at_span(row % 2)] = attended[:, part * SPAN : (part + 1) * SPAN]
        return jnp.min(norm)

    def bounded(i, least):
        here = block_at(i)
        query = queries[:HEAD, here].astype(F32)
        bound = jnp.sqrt(jnp.sum(query * query, axis=0, keepdims=True) * longest) - 40.0
        shift = in_parts(-bound)
        queries[HEAD : HEAD + 16, here] = shift

        def step(masked, j, acc):
            weights = jnp.exp(scores_of(masked, i, j)).astype(BF)
            return acc + mm(values[:, block_at(j)], weights)

        def tile(low, first):
            keys_at = pl.ds(pl.multiple_of(i * BLOCK + low, BLOCK // 2), BLOCK // 2)
            queries_at = pl.ds(pl.multiple_of(i * BLOCK + first, BLOCK // 2), BLOCK - first)
            scores = mm(keys[keys_at, :], queries[:, queries_at])
            local = key_at[: BLOCK // 2, first:] + low
            allowed = (local <= query_at[: BLOCK // 2, first:]) & (i * BLOCK + local < length)
            weights = jnp.exp(jnp.where(allowed, scores, NEG)).astype(BF)
            return mm(values[:, keys_at], weights)

        split = jnp.minimum(i, length // BLOCK)
        acc = lax.fori_loop(0, split, functools.partial(step, False), jnp.zeros((HEAD + 16, BLOCK), F32))
        acc = lax.fori_loop(split, i, functools.partial(step, True), acc)
        acc += tile(0, 0)
        later = acc[:, BLOCK // 2 :] + tile(BLOCK // 2, BLOCK // 2)
        acc = jnp.concatenate([acc[:, : BLOCK // 2], later], axis=1)
        exact = jnp.sum(shift.astype(F32), axis=0, keepdims=True)
        return jnp.minimum(least, finish(i, -exact, acc))

    least = lax.fori_loop(0, blocks, bounded, jnp.float32(1.0))

    @pl.when(jnp.logical_not(least > 1e-26))
    def _():
        queries[HEAD:] = jnp.zeros((WIDE - HEAD, total), BF)

        @pl.loop(0, blocks)
        def _(i):
            def step(j, carry):
                peak, acc = carry
                scores = scores_of(True, i, j)
                newest = jnp.maximum(peak, jnp.max(scores, axis=0, keepdims=True))
                weights = jnp.exp(scores - newest).astype(BF)
                return newest, acc * jnp.exp(peak - newest) + mm(values[:, block_at(j)], weights)

            start = (jnp.full((1, BLOCK), NEG, F32), jnp.zeros((HEAD + 16, BLOCK), F32))
            finish(i, *lax.fori_loop(0, i + 1, step, start))

    queries[HEAD : HEAD + 16] = in_parts(-lse[...])


def turn_kernel(info, deal, *refs):
    pieces, (k_t, q_n, v_n) = refs[:10], refs[10:]
    q_n[...] = jnp.zeros_like(q_n)
    ones_behind(v_n)
    for slot, (ref, col) in enumerate(span_slots(pieces)):
        where = at_span(natural_span(info, deal, slot))
        cols = slice(col, col + SPAN)
        k_t[:, where] = ref[HEAD : 2 * HEAD, cols]
        q_n[where, :HEAD] = ref[:HEAD, cols].T
        v_n[where, :HEAD] = ref[2 * HEAD :, cols].T


def backward_kernel(info, deal, *refs):
    q_t, k_n, k_t, q_n, v_n, attended, grad_out, scale, out, g_t, g_n, delta, dq_t, dk, dv, dealt = refs
    total = q_t.shape[1]
    length = info[3]
    spans = total // SPAN
    blocks = total // BLOCK

    @pl.loop(0, spans)
    def _(at):
        dealt[deal[at]] = at

    g_n[...] = jnp.zeros_like(g_n)
    g_t[HEAD:] = jnp.zeros((WIDE - HEAD, total), BF)
    for row in range(spans):
        where = at_span(deal[row])
        cols = slice(row % 2 * SPAN, row % 2 * SPAN + SPAN)
        grad = grad_out[row // 2, :, cols]
        g_t[:HEAD, where] = grad
        g_n[where, :HEAD] = grad.T
        product = grad.astype(F32) * attended[row // 2, :, cols].astype(F32)
        delta[:, where] = jnp.sum(product, axis=0, keepdims=True)
    g_t[HEAD : HEAD + 16] = in_parts(-delta[...])
    dq_t[...] = jnp.zeros_like(dq_t)

    key_at = lax.broadcasted_iota(jnp.int32, (BLOCK, BLOCK), 0)
    query_at = lax.broadcasted_iota(jnp.int32, (BLOCK, BLOCK), 1)

    @pl.loop(0, blocks)
    def _(j):
        there = block_at(j)
        dk[...] = jnp.zeros_like(dk)
        dv[...] = jnp.zeros_like(dv)

        def tile(masked, i, low, first, size):
            keys = pl.ds(pl.multiple_of(j * BLOCK + low, BLOCK // 2), size)
            here = pl.ds(pl.multiple_of(i * BLOCK + first, BLOCK // 2), BLOCK - first)
            probs = jnp.exp(mm(k_n[keys, :], q_t[:, here]))
            if masked:
                key_pos = j * BLOCK + low + key_at[:size, first:]
                allowed = (key_pos <= i * BLOCK + query_at[:size, first:]) & (key_pos < length)
                probs = jnp.where(allowed, probs, 0.0)
            probs = probs.astype(BF)
            grad_scores = probs * mm(v_n[keys, :], g_t[:, here]).astype(BF)
            rows = slice(low, low + size)
            dv[rows] += mm(probs, g_n[here, :])
            dk[rows] += mm(grad_scores, q_n[here, :])
            dq_t[:, here] += mm(k_t[:, keys], grad_scores)

        def step(masked, i, carry):
            tile(masked, i, 0, 0, BLOCK)
            return carry

        tile(True, j, 0, 0, BLOCK // 2)
        tile(True, j, BLOCK // 2, BLOCK // 2, BLOCK // 2)
        split = jnp.where((j + 1) * BLOCK <= length, j + 1, blocks)
        lax.fori_loop(j + 1, split, functools.partial(step, True), 0)
        lax.fori_loop(split, blocks, functools.partial(step, False), 0)
        for part in range(BLOCK // SPAN):
            row = dealt[j * (BLOCK // SPAN) + part]
            rows = slice(part * SPAN, (part + 1) * SPAN)
            out[row // 2, HEAD : 2 * HEAD, at_span(row % 2)] = dk[rows].T[:HEAD].astype(BF)
            out[row // 2, 2 * HEAD :, at_span(row % 2)] = dv[rows].T[:HEAD].astype(BF)

    for row in range(spans):
        cols = slice(row % 2 * SPAN, row % 2 * SPAN + SPAN)
        out[row // 2, :HEAD, cols] = (dq_t[:, at_span(deal[row])] * scale[...]).astype(BF)


def load_weights(info, own, direct, passed, wholes, sems):
    y, core = info[0], info[1]
    started = []
    count = 0
    for at, whole in enumerate(wholes):
        rows, part = own[at].shape[0], own[at].shape[0] // 2
        far = (1 - y) * rows
        places = [(own[at], y * rows)]
        for chunks, base in ((direct, far + core * part), (passed, far + (1 - core) * part)):
            start = 0
            for chunk in chunks:
                low, high = max(start, at * part), min(start + chunk.shape[0], at * part + part)
                if low < high:
                    places.append((chunk.at[pl.ds(low - start, high - low)], base + low - at * part))
                start += chunk.shape[0]
        copies = []
        for ref, start in places:
            target = whole.at[pl.ds(pl.multiple_of(start, 16), ref.shape[0])]
            copies.append(pltpu.make_async_copy(ref, target, sems.at[count]))
            copies[-1].start()
            count += 1
        started.append(copies)
    return started


def arrive(copies):
    for copy in copies:
        copy.wait()


def mlp_kernel(chunks, info, tokens, cotangent, attn_t, own, other, *refs):
    shards, direct, passed = refs[:3], refs[3 : 3 + chunks], refs[3 + chunks : 3 + 2 * chunks]
    refs = refs[3 + 2 * chunks :]
    outs = refs[:5]
    w_output, w_expand, w_contract, gain, right, sems = refs[5:]
    result, grad_mid_out, grad_attended_t, away, rights = outs
    y, core = info[0], info[1]
    loads = load_weights(info, shards, direct, passed, (w_output, w_expand, w_contract), sems)
    gain[:, half(y)] = own[6 * HEAD :].astype(F32)
    gain[:, half(1 - y)] = other[6 * HEAD :].astype(F32)
    gains = gain[1:2]
    attn = attn_t[...].T
    arrive(loads[0])
    mid = tokens[...].astype(F32) + mm(attn, w_output[...])
    rate = lax.rsqrt(jnp.mean(mid * mid, axis=-1, keepdims=True) + EPS)
    mlp_in = (mid * rate * gains).astype(BF)
    away[1] = mlp_in
    arrive(loads[1])
    expanded = mm(mlp_in, w_expand[...])
    gate = jax.nn.sigmoid(expanded)
    act = (expanded * gate).astype(BF)
    away[0] = act
    arrive(loads[2])
    result[...] = (mid + mm(act, w_contract[...])).astype(BF)
    grad_act = mm(cotangent[...], w_contract[...], NT)
    grad_expanded = (grad_act * gate * (1.0 + expanded * (1.0 - gate))).astype(BF)
    right[0] = grad_expanded
    grad_mlp_in = mm(grad_expanded, w_expand[...], NT) * gains
    inner = jnp.mean(grad_mlp_in * mid, axis=-1, keepdims=True)
    grad_mid = cotangent[...].astype(F32) + rate * grad_mlp_in - mid * (rate * rate * rate * inner)
    grad_mid_out[...] = grad_mid
    low = grad_mid.astype(BF)
    right[1] = low
    grad_attended_t[...] = mm(w_output[...], low, NT).astype(BF)
    for at in range(2):
        rights[:, at * 640 : at * 640 + 640] = right[at, :, half(core)]
        away[2, :, at * 640 : at * 640 + 640] = right[at, :, half(1 - core)]


BITS = ("y", "x", "far", "near")
ORDERS = (("y", "x", "near", "far"), ("x", "near", "y", "far"), ("near", "y", "x", "far"))
BIT_AT = {"y": 0, "x": 20, "near": 21, "far": 22}
PART = 80


def left_bits(order, done):
    return [name for name in BITS if name not in order[:done]]


def halves(info, order, done):
    left = left_bits(order, done)
    name = order[done]
    bit = info[BIT_AT[name]]
    stride = 1 << (len(left) - 1 - left.index(name))
    count = 1 << len(left)
    bases = [block for block in range(count) if block & stride == 0]
    return [(base + bit * stride, base + (1 - bit) * stride) for base in bases]


def rows_of(block):
    start = block * PART
    return pl.ds(start if isinstance(block, int) else pl.multiple_of(start, 16), PART)


def outer_kernel(info, own, rights, partner, attn_t, attn_t_partner, cot, cot_partner, *refs):
    outs, (left, right, full) = refs[:6], refs[6:]
    core = info[1]
    rows = cot.shape[0]
    for at in range(3):
        if at < 2:
            left[:, :rows] = own[at].T
            left[:, rows:] = partner[at].T
        else:
            left[:, :rows] = attn_t[...]
            left[:, rows:] = attn_t_partner[...]
        if at == 0:
            right[:rows] = cot[:, half(core)]
            right[rows:] = cot_partner[:, half(core)]
        else:
            cols = slice((at - 1) * 640, at * 640)
            right[:rows] = rights[:, cols]
            right[rows:] = partner[2, :, cols]
        full[...] = mm(left[...], right[...]).astype(BF)
        for to, (kept, sent) in enumerate(halves(info, ORDERS[at], 0)):
            outs[at][rows_of(to)] = full[rows_of(kept)]
            outs[3 + at][rows_of(to)] = full[rows_of(sent)]


def round_kernel(done, info, *refs):
    kept, came, outs = refs[:3], refs[3:6], refs[6:]
    for at in range(3):
        for to, (mine, theirs) in enumerate(halves(info, ORDERS[at], done)):
            if len(outs) == 6:
                stay, away, target = outs[at], outs[3 + at], rows_of(to)
            else:
                stay, away, target = outs[0], outs[1], rows_of(at)
            for out, block in ((stay, mine), (away, theirs)):
                total = kept[at][rows_of(block)].astype(F32) + came[at][rows_of(block)].astype(F32)
                out[target] = total.astype(BF)


def folded(products):
    return sum(products[:, at : at + 128] for at in range(0, products.shape[1], 128))


def row_sums(products):
    ones = jnp.ones((16, products.shape[1]), BF)
    high = products.astype(BF)
    low = (products - high.astype(F32)).astype(BF)
    return mm(ones, high, NT) + mm(ones, low, NT)


def stack_kernel(*refs):
    for at, ref in enumerate(refs[:-1]):
        refs[-1][at] = ref[...]


def joined(pieces, last):
    count = len(pieces) // 2
    ready = []
    for colour in range(2):
        group = pieces[colour * count : colour * count + count]
        cut = group[-2].shape[0]
        last[colour, :cut] = group[-2][...]
        last[colour, cut:] = group[-1][...]
        ready += [*group[:-2], last.at[colour]]
    return ready


def slot_of(at, count, first):
    return first + at if at < count else 8 + first + at - count


def scatter(info, refs, first, blocks, sems, outs, expand, sums):
    copies = []
    for at, ref in enumerate(refs):
        dev = info[4 + slot_of(at, len(refs) // 2, first)]
        block = ((dev // 2) % 2) * 4 + dev // 4
        rows = pl.ds(pl.multiple_of(block * PART, 16), PART)
        for way in range(3):
            blocks[3 * at + way] = ref[way * PART : (way + 1) * PART].astype(F32)
            target = outs[way].at[rows, half(dev % 2)]
            copies.append(pltpu.make_async_copy(blocks.at[3 * at + way], target, sems.at[3 * at + way]))
            copies[-1].start()
        sums[rows] += folded(blocks[3 * at + 1] * expand[rows, half(dev % 2)].astype(F32))
    return copies


def spread_kernel(info, *refs):
    pieces, (expand, sums), outs, (blocks, sems) = refs[:10], refs[10:12], refs[12:15], refs[15:]
    sums[...] = jnp.zeros_like(sums)
    arrive(scatter(info, pieces, 0, blocks, sems, outs, expand, sums))


def spread_last_kernel(info, *refs):
    pieces, (before, gain, expand), (*outs, grad_gain), refs = refs[:8], refs[8:11], refs[14:18], refs[18:]
    blocks, last, sums, sems = refs
    sums[...] = before[...]
    copies = scatter(info, joined(pieces, last), 5, blocks, sems, outs, expand, sums)
    size = sums.shape[0]
    grad_gain[...] = (row_sums(sums[...])[0:1] / gain[...].astype(F32)).reshape(size)
    arrive(copies)


def weight_kernel(info, grads, own, other, *refs):
    inputs = refs[:2]
    keep, away, lines, weight, total, gain_sums, attn_in, sems = refs[2:]
    y, core = info[0], info[1]
    rows = attn_in.shape[0] // 8
    loads = []
    for at in range(8):
        source = inputs[at // 4].at[pl.ds(at % 4 * rows, rows)]
        loads.append(pltpu.make_async_copy(source, attn_in.at[pl.ds(at * rows, rows)], sems.at[at]))
        loads[-1].start()
    for slot in range(16):
        lines[:, slot * 256 : slot * 256 + 256] = grads[info[4 + slot]]
    mine = pl.ds(pl.multiple_of(core * 3 * HEAD, 16), 3 * HEAD)
    weight[:, half(y)] = own[mine].astype(F32)
    weight[:, half(1 - y)] = other[mine].astype(F32)
    total[...] = jnp.zeros_like(total)
    for at in range(4):
        loads[2 * at].wait()
        loads[2 * at + 1].wait()
        part = slice(2 * at * rows, 2 * (at + 1) * rows)
        total[...] += mm(lines[:, part], attn_in[part])
    keep[: 3 * HEAD] = total[:, half(y)]
    away[: 3 * HEAD] = total[:, half(1 - y)].astype(BF)
    weight[...] *= total[...]
    scale_sums = row_sums(weight[:HEAD])[0:1]
    gain_sums[...] = jnp.sum(weight[...], axis=0, keepdims=True)
    line = lax.broadcasted_iota(jnp.int32, (16, keep.shape[1]), 0)
    keep[3 * HEAD :] = jnp.where(line == 1, gain_sums[:, half(y)], 0.0)
    away[3 * HEAD :] = jnp.where(line == 1, gain_sums[:, half(1 - y)], 0.0).astype(BF)
    keep[3 * HEAD : 3 * HEAD + 1, :HEAD] = scale_sums
    first = lax.broadcasted_iota(jnp.int32, (16, HEAD), 0) == 0
    behind = jnp.where(line == 1, gain_sums[:, half(1 - y)], 0.0)[:, :HEAD]
    away[3 * HEAD :, :HEAD] = jnp.where(first, scale_sums, behind).astype(BF)


def finish_kernel(info, near, near_partner, *refs):
    pieces, (gain, factor), outs, refs = refs[:8], refs[8:10], refs[10:13], refs[13:]
    grad_gain, grad_scale, stacks, last, turned, sems = refs
    extra = jnp.zeros((16, last.shape[2]), F32)
    early = [stack.at[at] for stack in (near, near_partner) for at in range(5)]
    for first, group in ((0, early), (5, joined(pieces, last))):
        for at, ref in enumerate(group):
            rows = pl.ds(pl.multiple_of(info[4 + slot_of(at, len(group) // 2, first)] * HEAD, 16), HEAD)
            for way in range(3):
                stacks[way, rows] = ref[way * HEAD : (way + 1) * HEAD]
            extra += ref[3 * HEAD :].astype(F32)
    grad_scale[...] = extra[0:1, :HEAD] * factor[...]
    size = turned.shape[1]
    grad_gain[...] = (extra[1:2] / gain[...].astype(F32)).reshape(size)
    same = lax.broadcasted_iota(jnp.int32, (size, size), 0) == lax.broadcasted_iota(jnp.int32, (size, size), 1)
    unit = jnp.where(same, 1.0, 0.0).astype(BF)
    copies = []
    for at, out in enumerate(outs):
        turned[at] = mm(unit, stacks[at], NT)
        copies.append(pltpu.make_async_copy(turned.at[at], out, sems.at[at]))
        copies[-1].start()
    arrive(copies)


def input_kernel(chunks, info, tokens, grads, grad_mid, own, other, *refs):
    shards, direct, passed = refs[:3], refs[3 : 3 + chunks], refs[3 + chunks : 3 + 2 * chunks]
    out, *weights, gain, sems = refs[3 + 2 * chunks :]
    y = info[0]
    loads = load_weights(info, shards, direct, passed, weights, sems)
    gain[:, half(y)] = own[6 * HEAD :].astype(F32)
    gain[:, half(1 - y)] = other[6 * HEAD :].astype(F32)
    heads, width = grads.shape[0], grads.shape[2]
    values = tokens[...].astype(F32)
    rate = lax.rsqrt(jnp.mean(values * values, axis=-1, keepdims=True) + EPS)
    turned_grad = None
    for at, ref in enumerate(weights):
        part = grads[:, at * HEAD : (at + 1) * HEAD, :].reshape(heads * HEAD, width)
        arrive(loads[at])
        product = mm(ref[...], part)
        turned_grad = product if turned_grad is None else turned_grad + product
    grad = turned_grad.T * gain[0:1]
    inner = jnp.mean(grad * values, axis=-1, keepdims=True)
    out[...] = (grad_mid[...] + rate * grad - values * (rate * rate * rate * inner)).astype(BF)


def after(values, *others):
    return lax.optimization_barrier((tuple(values), others))[0]


def weight_rows(shards, core):
    size = shards[0].shape[0] // 2
    return jnp.concatenate([lax.dynamic_slice_in_dim(shard, core * size, size, 0) for shard in shards], axis=0)


def ring_device(
    tokens, cotangent, deal, lengths, gain_attn, w_query, w_key, w_value, w_output, query_scale,
    gain_mlp, w_expand, w_contract
):
    rows, width = tokens.shape[1:]
    c, y = lax.axis_index("ctx"), lax.axis_index("wt")
    core, x, z = c % 2, (c // 2) % 2, c // 4
    table = lax.dynamic_index_in_dim(jnp.asarray(slot_table()), c, 0, keepdims=False)
    head = jnp.stack([y, core, c // 2, lengths[0, 0]]).astype(jnp.int32)
    info = jnp.concatenate([head, table, jnp.stack([x, z % 2, z // 2]).astype(jnp.int32)])
    dealt = deal[0]
    total = rows * 16
    softplus = jax.nn.softplus(query_scale)
    scale_col = (LOG2E / math.sqrt(HEAD) * softplus)[:, None]
    factor = (jax.nn.sigmoid(query_scale) / softplus)[None, :]
    inputs = tokens[0]
    cot = cotangent[0]
    cut = rows // 2
    mine, partner, gathered = [], [], []

    def project(other, *group):
        count = sum(part.shape[0] for part in group)
        start = sum(piece.shape[1] for piece in mine)
        args = [info, *group, own, other, scale_col]
        got = call(
            functools.partial(project_kernel, len(group), start),
            [((8 * rows, width), BF), ((3 * HEAD, count), BF), ((3 * HEAD, count), BF)],
            args + gathered[-1:],
            smem=1,
            anys=range(len(args), len(args) + 1),
            out_anys=(0,),
            aliases={len(args): 0} if gathered else None,
            scratch=[
                pltpu.VMEM((count, width), BF),
                pltpu.VMEM((6 * HEAD, width), BF),
                pltpu.VMEM((16, width), F32),
                pltpu.VMEM((6 * HEAD, count), BF),
                pltpu.SemaphoreType.DMA,
            ],
            cost=(2 * 480 * 1280 * count, 4 * 1280 * count, 0),
        )
        gathered.append(got[0])
        mine.append(got[1])
        partner.append(send(got[2], CORE_SWAP))
        return got[1]

    forth1, back1 = send(inputs, FORTH), send(inputs, BACK)
    size = width // 4
    first_rows = lax.dynamic_slice_in_dim(w_output, core * size, 128, 0)
    direct, passed = [send(first_rows, Y_SWAP)], []
    own = call(
        pick_kernel,
        [((6 * HEAD + 16, width // 2), BF)],
        [info, w_query, w_key, w_value, gain_attn[None], gain_mlp[None]],
        smem=1,
        cost=(2 * 480 * 640 * 1280, 3 * 640 * 1280 * 2, 0),
    )[0]
    other = send(own, Y_SWAP)
    forth1, back1, direct[0] = after((forth1, back1, direct[0]), own)

    forth2, back2 = send(forth1, FORTH), send(back1, BACK)
    rows_out = weight_rows(after((w_output, w_expand, w_contract), forth1), core)
    rows_back = weight_rows(after((w_query, w_key, w_value), forth1), core)
    chunks = [rows_out[128:448], rows_out[448:624], rows_out[624:]]
    chunks += [rows_back[:224], rows_back[224:384], rows_back[384:608], rows_back[608:]]
    passed.append(send(direct[0], CORE_SWAP))
    forth2, back2, other, passed[0], *chunks = after((forth2, back2, other, passed[0], *chunks))

    forth3, back3 = send(forth2, FORTH), send(back2, BACK)
    direct.append(send(after(chunks[:1], passed[0])[0], Y_SWAP))
    done = project(other, inputs)
    done = project(other, forth1, back1), done
    done = project(other, forth2, back2), done
    forth3, back3, direct[1] = after((forth3, back3, direct[1]), done)

    forth4, back4 = send(forth3[:cut], FORTH), send(back3[cut:], BACK)
    passed.append(send(direct[1], CORE_SWAP))
    direct.append(send(after(chunks[1:2], direct[1])[0], Y_SWAP))
    done = project(other, forth3, back3)
    forth4, back4, direct[2], passed[1] = after((forth4, back4, direct[2], passed[1]), done)
    passed.append(send(direct[2], CORE_SWAP))
    direct.append(send(after(chunks[2:3], direct[2])[0], Y_SWAP))
    project(other, forth4, back4)
    *spans, passed[2] = after((*mine, *partner, passed[2]))

    tall, flat_t = ((total, WIDE), BF), ((WIDE, total), BF)
    attended, q_t, k_n = call(
        forward_kernel,
        [((16, HEAD, rows), BF), flat_t, tall],
        [info, dealt, *spans],
        smem=2,
        scratch=[
            pltpu.VMEM((HEAD + 16, total), BF),
            pltpu.VMEM((1, total), F32),
            pltpu.SMEM((total // SPAN,), jnp.int32),
        ],
        cost=(2 * total * total * 256, 3 * total * 160, total * total // 2),
    )
    attended, direct[3] = after((attended, direct[3]))
    passed.append(send(direct[3], CORE_SWAP))
    direct_back = [send(after(chunks[3:4], direct[3])[0], Y_SWAP)]
    attn_in = gathered[-1]
    attn_in_partner, cot_partner = (send(value, CORE_SWAP) for value in after((attn_in, cot), attended))
    attn_t = lax.all_to_all(attended, "ctx", 0, 0).reshape(width, rows)
    k_t, q_n, v_n = call(
        turn_kernel,
        [((HEAD, total), BF), tall, tall],
        [info, dealt, *after(spans, attended)],
        smem=2,
        cost=(0, 6 * total * 256, 0),
    )
    attn_t, passed[3], attn_in_partner, cot_partner, direct_back[0] = after(
        (attn_t, passed[3], attn_in_partner, cot_partner, direct_back[0]), k_t
    )
    direct_back.append(send(after(chunks[4:5], attn_t)[0], Y_SWAP))
    whole_scratch = [pltpu.VMEM((width, width), BF)] * 3 + [pltpu.VMEM((16, width), F32)]
    wide, low = ((rows, width), F32), ((rows, width), BF)
    result, grad_mid, grad_attended_t, packed, rights = call(
        functools.partial(mlp_kernel, 4),
        [low, wide, ((width, rows), BF), ((3, rows, width), BF), low],
        [info, inputs, cot, attn_t, own, other, w_output, w_expand, w_contract, *direct, *passed],
        smem=1,
        anys=range(6, 17),
        scratch=whole_scratch + [pltpu.VMEM((2, rows, width), BF), pltpu.SemaphoreType.DMA((24,))],
        cost=(12 * rows * width * width, 6 * width * width, 0),
    )
    grad_attended_t, packed, direct_back[1] = after((grad_attended_t, packed, direct_back[1]))
    grad_out = lax.all_to_all(grad_attended_t.reshape(16, HEAD, rows), "ctx", 0, 0)
    packed_partner = send(packed, CORE_SWAP)
    direct_back.append(send(after(chunks[5:6], packed)[0], Y_SWAP))
    attn_t_partner = send(attn_t, CORE_SWAP)

    half_width = width // 2
    terms = call(
        outer_kernel,
        [((half_width, half_width), BF)] * 6,
        [info, packed, rights, packed_partner, attn_t, attn_t_partner, cot, cot_partner],
        smem=1,
        scratch=[
            pltpu.VMEM((width, 2 * rows), BF),
            pltpu.VMEM((2 * rows, half_width), BF),
            pltpu.VMEM((width, half_width), BF),
        ],
        cost=(6 * rows * width * width, 6 * width * width, 0),
    )
    moves = {"y": Y_SWAP, "x": X_SWAP, "near": NEAR_SWAP, "far": FAR_SWAP}

    def travel(values, done):
        return [send(value, moves[order[done]]) for value, order in zip(values, ORDERS)]

    def halving(kept, came, done):
        size = half_width >> done
        shapes = [((size, half_width), BF)] * 6 if done < 3 else [((3 * PART, half_width), BF)] * 2
        return call(
            functools.partial(round_kernel, done),
            shapes,
            [info, *kept, *came],
            smem=1,
            cost=(0, 12 * size * half_width, 0),
        )

    came = travel(terms[3:], 0)
    kept = terms[:3]
    grad_out, direct_back[2] = after((grad_out, direct_back[2]), kept[0])
    direct_back.append(send(after(chunks[6:], kept[0])[0], Y_SWAP))
    grads = call(
        backward_kernel,
        [((16, 3 * HEAD, rows), BF)],
        [info, dealt, q_t, k_n, k_t, q_n, v_n, attended, grad_out, scale_col],
        smem=2,
        scratch=[
            pltpu.VMEM((WIDE, total), BF),
            pltpu.VMEM((total, WIDE), BF),
            pltpu.VMEM((1, total), F32),
            pltpu.VMEM((HEAD, total), F32),
            pltpu.VMEM((BLOCK, WIDE), F32),
            pltpu.VMEM((BLOCK, WIDE), F32),
            pltpu.SMEM((total // SPAN,), jnp.int32),
        ],
        cost=(5 * total * total * 256, 6 * total * 160, total * total // 2),
    )[0]
    grads, *came = after((grads, *came))
    returned = lax.all_to_all(grads, "ctx", 0, 0)
    keep, away = call(
        weight_kernel,
        [((256, half_width), F32), ((256, half_width), BF)],
        [info, grads, own, other, attn_in, attn_in_partner],
        smem=1,
        anys=(4, 5),
        scratch=[
            pltpu.VMEM((3 * HEAD, total), BF),
            pltpu.VMEM((3 * HEAD, width), F32),
            pltpu.VMEM((3 * HEAD, width), F32),
            pltpu.VMEM((1, width), F32),
            pltpu.VMEM((total, width), BF),
            pltpu.SemaphoreType.DMA((8,)),
        ],
        cost=(2 * 240 * total * width, 2 * total * width, 0),
    )
    from_pair = send(away, Y_SWAP)
    terms = halving(kept, after(came, keep), 1)
    kept, came = terms[:3], travel(terms[3:], 1)
    keep = after((keep,), kept[0])[0]
    summed = (keep + from_pair.astype(F32)).astype(BF)
    passed_back = [send(value, CORE_SWAP) for value in after(direct_back, summed)]

    shard = ((half_width, width), F32)
    line = ((half_width,), F32)

    def stacked(values):
        stack = call(stack_kernel, [((len(values), *values[0].shape), BF)], values)[0]
        return stack, send(stack, CORE_SWAP)

    forth1, back1 = send(summed, FORTH), send(summed, BACK)
    forth2, back2 = send(forth1, FORTH), send(back1, BACK)
    terms = halving(kept, after(came, forth1), 2)
    kept, came = terms[:3], travel(terms[3:], 2)
    forth2, back2 = after((forth2, back2), kept[0], returned, *passed_back)
    forth3, back3 = send(forth2, FORTH), send(back2, BACK)
    near, near_partner = stacked([summed, forth1, back1, forth2, back2])
    terms = halving(kept, came, 3)
    far = send(terms[1], FAR_SWAP)
    forth3, back3 = after((forth3, back3), terms[0])
    last = [send(forth3[:128], FORTH), send(back3[128:], BACK)]
    beyond = [send(value, CORE_SWAP) for value in (forth3, back3)]
    piece = (terms[0].astype(F32) + far.astype(F32)).astype(BF)
    grad_inputs = call(
        functools.partial(input_kernel, 4),
        [low],
        [info, inputs, returned, grad_mid, own, other, w_query, w_key, w_value, *direct_back, *passed_back],
        smem=1,
        anys=range(6, 17),
        scratch=whole_scratch + [pltpu.SemaphoreType.DMA((24,))],
        cost=(6 * rows * width * width, 6 * width * width, 0),
    )[0]
    last = after(last, *beyond, grad_inputs, near_partner)
    piece = after((piece,), last[0])[0]
    query_pieces = [near, near_partner, forth3, back3, *last, *beyond, *(send(value, CORE_SWAP) for value in last)]

    forth1, back1 = send(piece, FORTH), send(piece, BACK)
    grad_query, grad_key, grad_value, grad_gain_attn, grad_scale = call(
        finish_kernel,
        [shard] * 3 + [line, ((1, HEAD), F32)],
        [info, *query_pieces, gain_attn[None], factor],
        smem=1,
        out_anys=range(3),
        scratch=[
            pltpu.VMEM((3, width, half_width), BF),
            pltpu.VMEM((2, 256, half_width), BF),
            pltpu.VMEM((3, half_width, width), F32),
            pltpu.SemaphoreType.DMA((3,)),
        ],
        cost=(6 * 640 * 640 * 1280, 3 * 640 * 1280 * 4, 0),
    )
    forth1, back1 = after((forth1, back1), grad_query)
    forth2, back2 = send(forth1, FORTH), send(back1, BACK)
    forth3, back3 = send(forth2, FORTH), send(back2, BACK)
    near = [piece, forth1, back1, forth2, back2]
    near_partner = [send(value, CORE_SWAP) for value in near]
    partial_out = call(
        spread_kernel,
        [((half_width, 128), F32), shard, shard, shard],
        [info, *near, *near_partner, w_expand],
        smem=1,
        out_anys=(1, 2, 3),
        scratch=[pltpu.VMEM((30, PART, half_width), F32), pltpu.SemaphoreType.DMA((30,))],
        cost=(0, 3 * 640 * 1280 * 4, 0),
    )
    forth3, back3 = after((forth3, back3), partial_out[0])
    last = [send(forth3[:112], FORTH), send(back3[112:], BACK)]
    beyond = [send(value, CORE_SWAP) for value in (forth3, back3)]
    last = after(last, *beyond)
    args = [info, forth3, back3, *last, *beyond, *(send(value, CORE_SWAP) for value in last)]
    args += [partial_out[0], gain_mlp[None], w_expand, *partial_out[1:]]
    grad_contract, grad_expand, grad_output, grad_gain_mlp = call(
        spread_last_kernel,
        [shard] * 3 + [line],
        args,
        smem=1,
        anys=range(len(args) - 3, len(args)),
        out_anys=range(3),
        aliases={len(args) - 3 + at: at for at in range(3)},
        scratch=[
            pltpu.VMEM((18, PART, half_width), F32),
            pltpu.VMEM((2, *piece.shape), BF),
            pltpu.VMEM((half_width, 128), F32),
            pltpu.SemaphoreType.DMA((18,)),
        ],
        cost=(0, 3 * 640 * 1280 * 4, 0),
    )
    return (
        result[None], grad_inputs[None], grad_gain_attn, grad_query, grad_key, grad_value, grad_output,
        grad_scale[0], grad_gain_mlp, grad_expand, grad_contract,
    )


def solution(mesh):
    in_specs = (
        P("wt", "ctx", None),
        P("wt", "ctx", None),
        P("wt", None),
        P("wt", None),
        P("wt"),
        P("wt", None),
        P("wt", None),
        P("wt", None),
        P("wt", None),
        P(),
        P("wt"),
        P("wt", None),
        P("wt", None),
    )
    out_specs = (
        P("wt", "ctx", None),
        P("wt", "ctx", None),
        P("wt"),
        P("wt", None),
        P("wt", None),
        P("wt", None),
        P("wt", None),
        P(),
        P("wt"),
        P("wt", None),
        P("wt", None),
    )
    body = ring_device if mesh.shape["ctx"] == HEADS and mesh.shape["wt"] == 2 else per_device
    return jax.shard_map(
        body, mesh=mesh, in_specs=in_specs, out_specs=out_specs, check_vma=False
    )
```
